128 devices in a mesh: rep: 2 (over z_lo), shard: 64 (over y, x, z_hi, core).
Axes of the slice: x: 4, y: 4, z: 4 (z_hi: 2, z_lo: 2; z = z_hi * 2 + z_lo), core: 2. Of those that a mesh axis runs over, the one named last changes fastest.
Arguments:
- tokens: bfloat16 [32768, 1024], P(('rep', 'shard')), may hold values from -6 to 6
- lengths: int32 [2], replicated, may hold values from 4096 to 16384, as said below
- norm1_gain: bfloat16 [1024], P('shard'), may hold values from 0.099609375 to 1.8984375
- in_proj: bfloat16 [1024, 3072], P('shard'), may hold values from -0.1875 to 0.1875
- conv_weight: bfloat16 [3, 1024], P(None, 'shard'), may hold values from -3.5 to 3.5
- out_proj: bfloat16 [1024, 1024], P('shard'), may hold values from -0.1875 to 0.1875
- norm2_gain: bfloat16 [1024], P('shard'), may hold values from 0.099609375 to 1.8984375
- w_gate: bfloat16 [1024, 4608], P('shard'), may hold values from -0.1875 to 0.1875
- w_up: bfloat16 [1024, 4608], P('shard'), may hold values from -0.1875 to 0.1875
- w_down: bfloat16 [4608, 1024], P('shard'), may hold values from -0.09375 to 0.09375
- cotangent: bfloat16 [32768, 1024], P(('rep', 'shard')), may hold values from -6 to 6
Outputs:
- mixed: bfloat16 [32768, 1024], P(('rep', 'shard'))
- d_tokens: float32 [32768, 1024], P(('rep', 'shard'))
- d_norm1_gain: float32 [1024], P('shard')
- d_in_proj: float32 [1024, 3072], P('shard')
- d_conv_weight: float32 [3, 1024], P(None, 'shard')
- d_out_proj: float32 [1024, 1024], P('shard')
- d_norm2_gain: float32 [1024], P('shard')
- d_w_gate: float32 [1024, 4608], P('shard')
- d_w_up: float32 [1024, 4608], P('shard')
- d_w_down: float32 [4608, 1024], P('shard')
The draws below stay inside these ranges and needn't reach their ends.
Inputs may be any that keep to these rules, and one draw needn't show every extreme that they name: `lengths`: each slot holds 4096 to 16384 valid tokens at its start; at least one slot is full.
All inputs are finite; a program needn't handle non-finite values.
Results may differ from the reference program's by a relative error of at most 0.019.
Values may be sent and summed in bfloat16 or wider, within the bound.
A program may use at most 192 MiB of HBM per device.

```python
import math
import jax
import jax.numpy as jnp
from jax import lax

D = 1024
FF = 4608
SLOT = 16384
TOKENS = 32768
SLOTS = 2


def draw_lengths(key, part):
    key = jax.random.fold_in(key, 11)
    first, second = jax.random.split(key, 2)
    base = jax.random.randint(first, (SLOTS,), SLOT // 4, SLOT + 1)
    chosen = jax.random.randint(second, (), 0, SLOTS)
    return jnp.where(jnp.arange(SLOTS) == chosen, SLOT, base).astype(jnp.int32)


def level_of(rng, shape, cuts, least, top_value):
    def one(position, blocks):
        heights = jax.random.uniform(jax.random.fold_in(jax.random.fold_in(rng, 6), position), (blocks,), jnp.float32, least / len(cuts), top_value / len(cuts))
        return jnp.repeat(jnp.exp(heights), shape[position] // blocks).reshape((-1,) + (1,) * (len(shape) - position - 1))

    loudness = one(*cuts[0])
    for cut in cuts[1:]:
        loudness = loudness * one(*cut)
    return loudness


def normal_values(rng, dims, scale, limit, pieces=(), kind=jnp.bfloat16):
    level = level_of(rng, dims, pieces, -0.22, 0.18) if pieces else 1.0
    result = jax.random.normal(rng, dims, jnp.float32) * scale * level
    return jnp.minimum(jnp.maximum(result, -limit), limit).astype(kind)


def setup_inputs(seed: int = 0) -> dict:
    splits = jax.random.split(jax.random.key(seed), 12)
    tokens = normal_values(splits[0], (TOKENS, D), 1.0, 6.0, ((0, 128),))
    lengths = draw_lengths(jax.random.fold_in(splits[11], 71), 0)
    norm1_gain = jnp.clip(1.0 + 0.18 * jax.random.normal(splits[2], (D,), jnp.float32), 0.099609375, 1.8984375).astype(jnp.bfloat16)
    in_proj = normal_values(splits[3], (D, 3 * D), D ** -0.5, 0.1875, ((0, 64),))
    conv_weight = normal_values(splits[4], (3, D), 3 ** -0.5, 3.5, ((1, 64),))
    out_proj = normal_values(splits[5], (D, D), D ** -0.5, 0.1875, ((0, 64),))
    norm2_gain = jnp.clip(1.0 + 0.18 * jax.random.normal(splits[6], (D,), jnp.float32), 0.099609375, 1.8984375).astype(jnp.bfloat16)
    w_gate = normal_values(splits[7], (D, FF), D ** -0.5, 0.1875, ((0, 64),))
    w_up = normal_values(splits[8], (D, FF), D ** -0.5, 0.1875, ((0, 64),))
    w_down = normal_values(splits[9], (FF, D), FF ** -0.5, 0.09375, ((0, 64),))
    cotangent = normal_values(splits[10], (TOKENS, D), 1.0, 6.0, ((0, 128),))
    return {"tokens": tokens, "lengths": lengths, "norm1_gain": norm1_gain, "in_proj": in_proj, "conv_weight": conv_weight, "out_proj": out_proj, "norm2_gain": norm2_gain, "w_gate": w_gate, "w_up": w_up, "w_down": w_down, "cotangent": cotangent}


@jax.custom_vjp
def low(v):
    return lax.optimization_barrier(v.astype(jnp.bfloat16)).astype(jnp.float32)

@jax.custom_vjp
def low_back(v):
    return v

def low_keep(v):
    return (low(v), None)

def low_pass(kept, grad):
    return (grad,)

def back_keep(v):
    return (v, None)

def back_low(kept, grad):
    return (low(grad),)
low.defvjp(low_keep, low_pass)
low_back.defvjp(back_keep, back_low)
EPS = 1e-05

def matmul(left, right):
    return jnp.dot(left, right, preferred_element_type=jnp.float32, precision=lax.Precision.HIGHEST)

def forward(params, rows, valid):
    gain_one, proj_in, taps, proj_out, gain_two, gate_w, up_w, down_w = params
    count = rows.shape[0]
    flat = rows.reshape(count * SLOT, D)
    scale_one = lax.rsqrt(lax.optimization_barrier(jnp.mean(flat * flat, axis=1, keepdims=True)) + EPS)
    normed = low(flat * scale_one * gain_one)
    bcx = low_back(matmul(normed, proj_in))
    b_part = bcx[:, :D]
    c_part = bcx[:, D:2 * D]
    x_part = bcx[:, 2 * D:]
    product = low(b_part * x_part).reshape(count, SLOT, D)
    padded = jnp.pad(product, ((0, 0), (2, 0), (0, 0)))
    conv = taps[0] * padded[:, :-2] + taps[1] * padded[:, 1:-1] + taps[2] * padded[:, 2:]
    gated = low(c_part * conv.reshape(count * SLOT, D))
    mix = low_back(matmul(gated, proj_out))
    resid = flat + mix
    scale_two = lax.rsqrt(lax.optimization_barrier(jnp.mean(resid * resid, axis=1, keepdims=True)) + EPS)
    normed_two = low(resid * scale_two * gain_two)
    gate = low_back(matmul(normed_two, gate_w))
    upper = low_back(matmul(normed_two, up_w))
    act = low(jax.nn.silu(gate) * upper)
    ffo = low_back(matmul(act, down_w))
    return valid * (resid + ffo).reshape(count, SLOT, D)

def reference(tokens, lengths, norm1_gain, in_proj, conv_weight, out_proj, norm2_gain, w_gate, w_up, w_down, cotangent):
    params = tuple((a.astype(jnp.float32) for a in (norm1_gain, in_proj, conv_weight, out_proj, norm2_gain, w_gate, w_up, w_down)))
    per = math.gcd(SLOTS, max(1, 4096 // SLOT))
    groups = SLOTS // per
    rows_all = tokens.astype(jnp.float32).reshape(groups, per, SLOT, D)
    cot_all = cotangent.astype(jnp.float32).reshape(groups, per, SLOT, D)
    len_all = lengths.astype(jnp.int32).reshape(groups, per)
    places = jnp.arange(SLOT, dtype=jnp.int32)

    def step(acc, item):
        rows, cot, lens = item
        valid = (places[None, :] < lens[:, None]).astype(jnp.float32)[:, :, None]
        out, pull = jax.vjp(lambda p, r: forward(p, r, valid), params, rows)
        grads, d_rows = pull(cot)
        acc = jax.tree.map(lambda a, b: a + b, acc, grads)
        return (acc, (out.astype(jnp.bfloat16), d_rows))
    zeros = tuple((jnp.zeros_like(p) for p in params))
    acc, (outs, d_rows) = lax.scan(step, zeros, (rows_all, cot_all, len_all))
    return (outs.reshape(TOKENS, D), d_rows.reshape(TOKENS, D), acc[0], acc[1], acc[2], acc[3], acc[4], acc[5], acc[6], acc[7])
```

```python
import functools
import jax, jax.numpy as jnp
from jax import lax
from jax.experimental import pallas as pl
from jax.experimental.pallas import tpu as pltpu
from jax.sharding import PartitionSpec as P
MESH = pl.DeviceIdType.MESH
C1 = 2176; HALF = 1152; CAT = 6784; UNIT = 32; DUNIT = 144
COPIES = 160

def spot():
    rep = lax.axis_index("rep"); s = lax.axis_index("shard")
    return (s // 4) % 4, s // 16, ((s // 2) % 2) * 2 + rep, s % 2

def device(x, y, z, c):
    return (z % 2, ((y * 4 + x) * 2 + z // 2) * 2 + c)

def moved(x, y, z, c, axis, step):
    if axis == "x": return device((x + step + 4) % 4, y, z, c)
    return device(x, (y + step + 4) % 4, z, c)

def greet(devices):
    bar = pltpu.get_barrier_semaphore()
    for d in devices:
        pl.semaphore_signal(bar, inc=1, device_id=d, device_id_type=MESH)
    pl.semaphore_wait(bar, len(devices))

class Wire:
    def __init__(self, ss, rs): self.ss, self.rs, self.sent = ss, rs, []
    def send(self, src, dst, dev):
        i = len(self.sent)
        cp = pltpu.make_async_remote_copy(src_ref=src, dst_ref=dst, send_sem=self.ss.at[i], recv_sem=self.rs.at[i], device_id=dev, device_id_type=MESH)
        cp.start(); self.sent.append(cp); return cp
    def drain(self):
        for cp in self.sent: cp.wait_send()

def gather_kernel(cat_in, down_in, wcat, wd, wor, wdr, dnf, dnb, ss, rs, ls):
    x, y, z, c = spot()
    hi = z // 2
    s = ((y * 4 + x) * 2 + hi) * 2 + c
    k = s // 2
    pair = device(x, y, z + 1 - 2 * (z % 2), c)
    cross = device(x, y, 3 - z, c)
    other = device(x, y, z, 1 - c)
    go = {(a, st): moved(x, y, z, c, a, st) for a in "xy" for st in (1, -1)}
    greet(list(go.values()) + [pair, cross, other])
    w = Wire(ss, rs)
    rows = pl.ds(pl.multiple_of(16 * s, 16), 16)
    lc = pltpu.make_async_copy(cat_in.at[c], wcat.at[rows, :], ls.at[0]); lc.start()
    r0 = w.send(cat_in.at[1 - c], wcat.at[rows, :], other)
    dr = pl.ds(pl.multiple_of(72 * c, 8), 72)
    ld = pltpu.make_async_copy(down_in.at[c], dnf.at[dr, :], ls.at[1]); ld.start()
    r1 = w.send(down_in.at[1 - c], dnf.at[dr, :], other)
    lc.wait(); r0.wait_recv()
    urow = pl.ds(pl.multiple_of(UNIT * k, UNIT), UNIT)
    drow = pl.ds(pl.multiple_of(DUNIT * k, 16), DUNIT)
    z1 = w.send(wcat.at[urow, pl.ds(0, C1)], wcat.at[urow, pl.ds(0, C1)], cross)
    z2 = w.send(wcat.at[urow, pl.ds(C1, CAT - C1)], wcat.at[urow, pl.ds(C1, CAT - C1)], cross)
    ld.wait(); r1.wait_recv()
    dnb[...] = dnf[...].astype(jnp.bfloat16)
    ldb = pltpu.make_async_copy(dnb, wd.at[drow, :], ls.at[2]); ldb.start()
    z3 = w.send(dnb, wd.at[drow, :], cross)
    flows = [
        dict(buf=wcat, unit=UNIT, col=0, width=C1, order="xy", need=[z1], fwd=None),
        dict(buf=wcat, unit=UNIT, col=C1 + HALF * (z % 2), width=HALF, order="yx", need=[z2], fwd=pair),
        dict(buf=wcat, unit=UNIT, col=C1 + 2 * HALF + HALF * hi, width=HALF, order="xy", need=[], fwd=cross),
        dict(buf=wd, unit=DUNIT, col=0, width=512, order="yx", need=[z3], fwd=None),
    ]
    def block(f, da, db, unit=None):
        a, b = f["order"]
        pos = {"x": x, "y": y}
        pos[a] = (pos[a] + da + 4) % 4
        pos[b] = (pos[b] + db + 4) % 4
        u = f["unit"]
        row = (pos["y"] * 4 + pos["x"]) * (2 * u)
        n = 2 * u
        if unit is not None: row, n = row + unit * u, u
        col = f["col"] if isinstance(f["col"], int) else pl.multiple_of(f["col"], 128)
        return f["buf"].at[pl.ds(pl.multiple_of(row, 16), n), pl.ds(col, f["width"])]
    def push(f, da, db, dev, unit=None):
        v = block(f, da, db, unit)
        return w.send(v, v, dev)
    def fwd(f, da, db):
        if f["fwd"] is not None: f.setdefault("z", []).append(push(f, da, db, f["fwd"]))
    def open2(f, j):
        b = f["order"][1]
        f[("p", j)] = push(f, j, 0, go[(b, 1)])
        f[("m", j)] = push(f, j, 0, go[(b, -1)])
    for n, f in enumerate(flows):
        for q in f["need"]: q.wait_recv()
        if n == 3: ldb.wait()
        a = f["order"][0]
        f["p"] = push(f, 0, 0, go[(a, 1)])
        f["m"] = push(f, 0, 0, go[(a, -1)])
        open2(f, 0)
    for f in flows:
        a = f["order"][0]
        f["p"].wait_recv(); f["p2"] = push(f, -1, 0, go[(a, 1)], 0)
        f["m"].wait_recv(); f["m2"] = push(f, 1, 0, go[(a, -1)], 1)
        open2(f, -1); open2(f, 1)
        fwd(f, -1, 0); fwd(f, 1, 0)
    for f in flows:
        f["p2"].wait_recv(); f["m2"].wait_recv()
        open2(f, 2); fwd(f, 2, 0)
    for j in (0, -1, 1, 2):
        for f in flows:
            b = f["order"][1]
            f[("p", j)].wait_recv(); f[("p2", j)] = push(f, j, -1, go[(b, 1)], 0)
            f[("m", j)].wait_recv(); f[("m2", j)] = push(f, j, 1, go[(b, -1)], 1)
            fwd(f, j, -1); fwd(f, j, 1)
    for j in (0, -1, 1, 2):
        for f in flows:
            f[("p2", j)].wait_recv(); f[("m2", j)].wait_recv()
            fwd(f, j, 2)
    for f in flows:
        for q in f.get("z", []): q.wait_recv()
    a = w.send(wcat.at[pl.ds(pl.multiple_of(512 * (1 - c), 512), 512), pl.ds(1536, 512)], wor, other)
    b = w.send(wd.at[pl.ds(pl.multiple_of(2304 * (1 - c), 2304), 2304), :], wdr, other)
    a.wait_recv(); b.wait_recv()
    w.drain()

def gather_all(cat, down):
    return pl.pallas_call(
        gather_kernel,
        out_shape=(jax.ShapeDtypeStruct((1024, CAT), jnp.bfloat16), jax.ShapeDtypeStruct((4608, 512), jnp.bfloat16),
            jax.ShapeDtypeStruct((512, 512), jnp.bfloat16), jax.ShapeDtypeStruct((2304, 512), jnp.bfloat16)),
        in_specs=[pl.BlockSpec(memory_space=pl.ANY)] * 2,
        out_specs=(pl.BlockSpec(memory_space=pl.ANY),) * 4,
        scratch_shapes=[pltpu.VMEM((144, 512), jnp.float32), pltpu.VMEM((144, 512), jnp.bfloat16),
            pltpu.SemaphoreType.DMA((COPIES,)), pltpu.SemaphoreType.DMA((COPIES,)), pltpu.SemaphoreType.DMA((3,))],
        compiler_params=pltpu.CompilerParams(collective_id=1, has_side_effects=True, vmem_limit_bytes=32 * 2**20),
        name="gather")(cat, down)

def prepare(norm1_gain, in_proj, conv_weight, out_proj, norm2_gain, w_gate, w_up, w_down):
    small = jnp.stack([norm1_gain, norm2_gain, conv_weight[0], conv_weight[1], conv_weight[2]], axis=1)
    small = jnp.pad(small, ((0, 0), (0, 123)))
    cat = jnp.stack([jnp.concatenate([in_proj[:, 512*p:512*p+512], in_proj[:, 1024+512*p:1536+512*p], in_proj[:, 2048+512*p:2560+512*p],
        out_proj[:, 512*p:512*p+512], small, w_gate[:, 2304*p:2304*p+2304], w_up[:, 2304*p:2304*p+2304]], axis=1) for p in (0, 1)])
    down = jnp.stack([w_down[:, :512], w_down[:, 512:]]).astype(jnp.float32)
    return cat, down

JS = (2, -1, 1, 0)

def add_into(dst, srcs, rows, step=16):
    def body(i, _):
        r = pl.ds(pl.multiple_of(i * step, step), step)
        t = dst[r, :].astype(jnp.float32)
        for q in srcs: t = t + q[r, :].astype(jnp.float32)
        dst[r, :] = t.astype(jnp.bfloat16)
        return 0
    lax.fori_loop(0, rows // step, body, 0)

def scatter_kernel(gin, gout, gsm, gg, gu, gd, ocat, odn,
                   G1, GG, GU, GD, L1, LG, LU, LD, M1, MG, MU, MD,
                   d1, dg, du, dd, fcat, fdn, ss, rs, ls):
    x, y, z, c = spot()
    hi = z // 2
    pair = device(x, y, z + 1 - 2 * (z % 2), c)
    cross = device(x, y, 3 - z, c)
    other = device(x, y, z, 1 - c)
    go = {(a, st): moved(x, y, z, c, a, st) for a in "xy" for st in (1, -1)}
    greet(list(go.values()) + [pair, cross, other])
    w = Wire(ss, rs)
    nl = [0]
    def local(src, dst):
        cp = pltpu.make_async_copy(src, dst, ls.at[nl[0]]); nl[0] += 1; cp.start(); return cp
    rd = w.send(gd.at[1 - c], GD.at[pl.ds(2 * c, 2)], other)
    ld = local(gd.at[c], GD.at[pl.ds(2 * c, 2)])
    lg = [local(gg.at[:, :, :, pl.ds(h * HALF, HALF)], GG.at[h]) for h in (0, 1)]
    lu = [local(gu.at[:, :, :, pl.ds(h * HALF, HALF)], GU.at[h]) for h in (0, 1)]
    ro = w.send(gout.at[1 - c], G1.at[pl.ds(2 * c, 2), :, :, pl.ds(1536, 512)], other)
    lo = local(gout.at[c], G1.at[pl.ds(2 * c, 2), :, :, pl.ds(1536, 512)])
    li = local(gin, G1.at[:, :, :, pl.ds(0, 1536)])
    lsm = local(gsm, G1.at[:, :, :, pl.ds(2048, 128)])
    zl = z % 2
    fd = dict(G=GD, L=LD, M=MD, unit=DUNIT, order="yx")
    fg = dict(G=GG.at[zl], L=LG.at[zl], M=MG, unit=UNIT, order="yx")
    fu = dict(G=GU.at[hi], L=LU.at[hi], M=MU, unit=UNIT, order="xy")
    f1 = dict(G=G1, L=L1, M=M1, unit=UNIT, order="xy")
    flows = [fd, fg, fu, f1]
    def at(f, da, db):
        a, b = f["order"]
        pos = {"x": x, "y": y}
        pos[a] = (pos[a] + da + 4) % 4
        pos[b] = (pos[b] + db + 4) % 4
        return pos["y"], pos["x"]
    def line(f, j):
        return (x + j + 4) % 4 if f["order"] == "xy" else (y + j + 4) % 4
    for q in lg: q.wait()
    for q in lu: q.wait()
    for j in JS:
        yj = line(fg, j); fg[("A", j)] = w.send(GG.at[1 - zl, yj], LG.at[zl, yj], pair)
        xj = line(fu, j); fu[("A", j)] = w.send(GU.at[1 - hi, :, xj], LU.at[hi, :, xj], cross)
    def absorb(f, j):
        if ("A", j) not in f: return
        f[("A", j)].wait_recv()
        l = line(f, j)
        for i in range(4):
            if f is fg: add_into(GG.at[zl, l, i], [LG.at[1 - zl, l, i]], 64)
            else: add_into(GU.at[hi, i, l], [LU.at[1 - hi, i, l]], 64)
    def part(ref, f, pos, u):
        return ref.at[pos[0], pos[1], pl.ds(u * f["unit"], f["unit"])]
    ready = {id(fd): [ld.wait, rd.wait_recv], id(f1): [lo.wait, li.wait, lsm.wait, ro.wait_recv]}
    for f in flows:
        for q in ready.get(id(f), []): q()
        ready[id(f)] = []
        b = f["order"][1]
        for j in JS:
            absorb(f, j)
            p = at(f, j, 2)
            f[("s", j)] = w.send(part(f["G"], f, p, 0), part(f["L"], f, p, 0), go[(b, 1)])
            f[("t", j)] = w.send(part(f["G"], f, p, 1), part(f["L"], f, p, 1), go[(b, -1)])
    for j in JS:
        for f in flows:
            b = f["order"][1]
            f[("s", j)].wait_recv(); p = at(f, j, 1)
            add_into(part(f["G"], f, p, 0), [part(f["L"], f, p, 0)], f["unit"])
            f[("s2", j)] = w.send(f["G"].at[p[0], p[1]], f["L"].at[p[0], p[1]], go[(b, 1)])
            f[("t", j)].wait_recv(); p = at(f, j, -1)
            add_into(part(f["G"], f, p, 1), [part(f["L"], f, p, 1)], f["unit"])
            o = at(f, j, 1)
            f[("t2", j)] = w.send(f["G"].at[p[0], p[1]], f["L"].at[o[0], o[1]], go[(b, -1)])
    for j in JS:
        for f in flows:
            a = f["order"][0]
            f[("s2", j)].wait_recv(); f[("t2", j)].wait_recv()
            p = at(f, j, 0); o = at(f, j, 2)
            add_into(f["G"].at[p[0], p[1]], [f["L"].at[p[0], p[1]], f["L"].at[o[0], o[1]]], 2 * f["unit"])
            u = f["unit"]; M = f["M"]
            if j == 2:
                f["c"] = w.send(part(f["G"], f, p, 0), M.at[pl.ds(0, u)], go[(a, 1)])
                f["d"] = w.send(part(f["G"], f, p, 1), M.at[pl.ds(u, u)], go[(a, -1)])
            elif j == 1:
                f["c"].wait_recv(); add_into(part(f["G"], f, p, 0), [M.at[pl.ds(0, u)]], u)
                f["c2"] = w.send(f["G"].at[p[0], p[1]], M.at[pl.ds(2 * u, 2 * u)], go[(a, 1)])
            elif j == -1:
                f["d"].wait_recv(); add_into(part(f["G"], f, p, 1), [M.at[pl.ds(u, u)]], u)
                f["d2"] = w.send(f["G"].at[p[0], p[1]], M.at[pl.ds(4 * u, 2 * u)], go[(a, -1)])
    for f in flows:
        f["c2"].wait_recv(); f["d2"].wait_recv()
        u = f["unit"]; M = f["M"]; mine = f["G"].at[y, x]
        add_into(mine, [M.at[pl.ds(2 * u, 2 * u)], M.at[pl.ds(4 * u, 2 * u)]], 2 * u)
        away = mine.at[pl.ds(u * (1 - hi), u)]
        if f is fd: f["e"] = w.send(away, dd.at[0], cross)
        if f is f1: f["e"] = w.send(away, d1.at[0], cross)
        if f is fu: f["e"] = w.send(away, du.at[0, hi], cross)
        if f is fg: f["e"] = w.send(mine, dg.at[0, zl], pair)
    own = lambda f: f["G"].at[y, x, pl.ds(f["unit"] * hi, f["unit"])]
    fd["e"].wait_recv(); add_into(own(fd), [dd.at[0]], DUNIT)
    fd["e2"] = w.send(own(fd), dd.at[1], pair)
    fg["e"].wait_recv()
    fg["e2"] = w.send(fg["G"].at[y, x, pl.ds(UNIT * (1 - hi), UNIT)], dg.at[1, zl, pl.ds(0, UNIT)], cross)
    fg["e3"] = w.send(dg.at[0, 1 - zl, pl.ds(UNIT * (1 - hi), UNIT)], dg.at[1, 1 - zl, pl.ds(0, UNIT)], cross)
    fu["e"].wait_recv()
    fu["e2"] = w.send(own(fu), du.at[1, hi], pair)
    fu["e3"] = w.send(du.at[0, 1 - hi], du.at[1, 1 - hi], pair)
    f1["e"].wait_recv(); add_into(own(f1), [d1.at[0]], UNIT)
    f1["e2"] = w.send(own(f1), d1.at[1], pair)
    f32 = lambda v: v.astype(jnp.float32)
    fd["e2"].wait_recv()
    fdn[...] = f32(own(fd)[...]) + f32(dd[1])
    o1 = w.send(fdn.at[pl.ds(pl.multiple_of(72 * (1 - c), 8), 72)], odn.at[c], other)
    q1 = local(fdn.at[pl.ds(pl.multiple_of(72 * c, 8), 72)], odn.at[c])
    for q in ("e2", "e3"): fg[q].wait_recv(); fu[q].wait_recv()
    cg = C1 + HALF * zl; cgo = C1 + HALF * (1 - zl)
    cu = C1 + 2 * HALF + HALF * hi; cuo = C1 + 2 * HALF + HALF * (1 - hi)
    m128 = lambda v: pl.ds(pl.multiple_of(v, 128), HALF)
    fcat[:, m128(cg)] = f32(own(fg)[...]) + f32(dg[1, zl, pl.ds(0, UNIT), :])
    fcat[:, m128(cgo)] = f32(dg[0, 1 - zl, pl.ds(UNIT * hi, UNIT), :]) + f32(dg[1, 1 - zl, pl.ds(0, UNIT), :])
    fcat[:, m128(cu)] = f32(own(fu)[...]) + f32(du[1, hi])
    fcat[:, m128(cuo)] = f32(du[0, 1 - hi]) + f32(du[1, 1 - hi])
    f1["e2"].wait_recv()
    fcat[:, pl.ds(0, C1)] = f32(own(f1)[...]) + f32(d1[1])
    o2 = w.send(fcat.at[pl.ds(pl.multiple_of(16 * (1 - c), 16), 16)], ocat.at[c], other)
    q2 = local(fcat.at[pl.ds(pl.multiple_of(16 * c, 16), 16)], ocat.at[c])
    q1.wait(); q2.wait(); o1.wait_recv(); o2.wait_recv()
    w.drain()

def scatter_all(gin, gout, gsm, gg, gu, gd):
    bf = jnp.bfloat16
    V = lambda *s: pltpu.VMEM(s, bf)
    grid = lambda v: v.reshape(4, 4, -1, v.shape[-1])
    half = lambda v: v.reshape(2, 2, 4, -1, 512)
    return pl.pallas_call(
        scatter_kernel,
        out_shape=(jax.ShapeDtypeStruct((2, 16, CAT), jnp.float32), jax.ShapeDtypeStruct((2, 72, 512), jnp.float32)),
        in_specs=[pl.BlockSpec(memory_space=pl.ANY)] * 6,
        out_specs=(pl.BlockSpec(memory_space=pl.ANY),) * 2,
        scratch_shapes=[V(4, 4, 64, C1), V(2, 4, 4, 64, HALF), V(2, 4, 4, 64, HALF), V(4, 4, 288, 512),
            V(4, 4, 64, C1), V(2, 4, 4, 64, HALF), V(2, 4, 4, 64, HALF), V(4, 4, 288, 512),
            V(192, C1), V(192, HALF), V(192, HALF), V(864, 512),
            V(2, UNIT, C1), V(2, 2, 64, HALF), V(2, 2, UNIT, HALF), V(2, DUNIT, 512),
            pltpu.VMEM((UNIT, CAT), jnp.float32), pltpu.VMEM((DUNIT, 512), jnp.float32),
            pltpu.SemaphoreType.DMA((COPIES,)), pltpu.SemaphoreType.DMA((COPIES,)), pltpu.SemaphoreType.DMA((12,))],
        compiler_params=pltpu.CompilerParams(collective_id=2, has_side_effects=True, vmem_limit_bytes=60 * 2**20),
        name="scatter")(grid(gin), half(gout), grid(gsm), grid(gg), grid(gu), half(gd))

def finish(ocat, odn):
    a, b = ocat[0], ocat[1]
    j = lambda o, n: [a[:, o:o + n], b[:, o:o + n]]
    d_in = jnp.concatenate(j(0, 512) + j(512, 512) + j(1024, 512), axis=1)
    d_out = jnp.concatenate(j(1536, 512), axis=1)
    sm = a[:, 2048:2053] + b[:, 2048:2053]
    d_gate = jnp.concatenate(j(C1, 2304), axis=1)
    d_up = jnp.concatenate(j(C1 + 2304, 2304), axis=1)
    d_down = jnp.concatenate([odn[0], odn[1]], axis=1)
    return sm[:, 0], d_in, sm[:, 2:5].T, d_out, sm[:, 1], d_gate, d_up, d_down

EPS = 1e-05

def swap(v):
    return lax.ppermute(v, "shard", [(s, s ^ 1) for s in range(64)])

def ordered(own, oth, c, axis=0):
    return jnp.where(c == 0, jnp.concatenate([own, oth], axis), jnp.concatenate([oth, own], axis))

def norm_rows(rows, gain):
    scale = lax.rsqrt(jnp.mean(rows * rows, axis=1, keepdims=True) + EPS)
    return scale, rows * scale * gain

def norm_back(rows, scale, gain, grad_norm):
    gain_grad = jnp.sum(grad_norm * rows * scale, axis=0)
    weighted = grad_norm * gain
    inner = jnp.mean(weighted * rows, axis=1, keepdims=True)
    return scale * weighted - rows * (scale * scale * scale) * inner, gain_grad

def dot(a, b): return jnp.dot(a, b, preferred_element_type=jnp.float32)
def tn(a, b): return lax.dot_general(a, b, (((0,), (0,)), ((), ())), preferred_element_type=jnp.float32)
def nt(a, b): return lax.dot_general(a, b, (((1,), (1,)), ((), ())), preferred_element_type=jnp.float32)

def share(part, c):
    n = part.shape[0] // 2
    own = lax.dynamic_slice_in_dim(part, n * c, n, 0)
    away = lax.dynamic_slice_in_dim(part, n * (1 - c), n, 0)
    return own + swap(away)

def middle(tokens, keep, cot, wcat, wd, wor, wdr):
    s_id = lax.axis_index("shard"); c = s_id % 2
    bf = jnp.bfloat16; f32 = jnp.float32
    inside = (s_id >= 2).astype(f32)
    small = wcat[:, 2048:2053].astype(f32).T
    g1, g2, taps = small[0], small[1], small[2:5]
    taps = lax.dynamic_slice_in_dim(taps, 512 * c, 512, 1)
    rows2 = lambda v, n: lax.dynamic_slice_in_dim(v, n * c, n, 0)
    w_in = wcat[:, :1536]
    w_out = ordered(rows2(wcat[:, 1536:2048], 512), wor, c, 1)
    w_dn = ordered(rows2(wd, 2304), wdr, c, 1)
    w_g, w_u = wcat[:, C1:C1 + 2304], wcat[:, C1 + 2304:]
    d_ffo_own = (keep * cot.astype(f32)).astype(bf)
    T = ordered(tokens, swap(tokens), c).astype(f32)
    d_ffo = ordered(d_ffo_own, swap(d_ffo_own), c)
    src = tokens.astype(f32)
    _, hf = norm_rows(T, g1); h = hf.astype(bf)
    s1, _ = norm_rows(src, g1)
    bcx = dot(h, w_in)
    B, C, X = bcx[:, :512], bcx[:, 512:1024], bcx[:, 1024:]
    bx = (B * X).astype(bf)
    edge = lax.ppermute(bx[510:], "shard", [(s, s + 2) for s in range(62)])
    ext = jnp.concatenate([edge.astype(f32) * inside, bx.astype(f32)], axis=0)
    conv = taps[0] * ext[:-2] + taps[1] * ext[1:-1] + taps[2] * ext[2:]
    y = (C * conv).astype(bf)
    resid = src + share(dot(y, w_out), c)
    s2, h2f = norm_rows(resid, g2)
    h2o = h2f.astype(bf)
    h2 = ordered(h2o, swap(h2o), c)
    gate = dot(h2, w_g); up = dot(h2, w_u)
    sg = jax.nn.sigmoid(gate); sw = gate * sg
    act = (sw * up).astype(bf)
    ffo = share(dot(act, w_dn), c)
    mixed = (keep * (resid + ffo)).astype(bf)
    d_down = tn(act, d_ffo).astype(bf)
    d_act = nt(d_ffo, w_dn)
    d_gate = (d_act * up * sg * (1.0 + gate * (1.0 - sg))).astype(bf)
    d_up = (d_act * sw).astype(bf)
    d_wg = tn(h2, d_gate).astype(bf); d_wu = tn(h2, d_up).astype(bf)
    d_h2 = share(nt(d_gate, w_g) + nt(d_up, w_u), c)
    d_rn, d_g2 = norm_back(resid, s2, g2, d_h2)
    d_resid = keep * cot.astype(f32) + d_rn
    dmo = d_resid.astype(bf)
    d_mix = ordered(dmo, swap(dmo), c)
    d_out = tn(y, d_mix).astype(bf)
    d_y = nt(d_mix, w_out)
    d_c = d_y * conv; d_conv = d_y * C
    d_taps = jnp.stack([jnp.sum(d_conv * ext[i:i + 512], axis=0) for i in range(3)])
    z2 = jnp.zeros((2, 512), f32)
    de = jnp.concatenate([taps[0] * d_conv, z2], 0) + jnp.concatenate([z2[:1], taps[1] * d_conv, z2[:1]], 0) + jnp.concatenate([z2, taps[2] * d_conv], 0)
    back = lax.ppermute(de[:2] * inside, "shard", [(s, s - 2) for s in range(2, 64)])
    d_bx = de[2:] + jnp.concatenate([jnp.zeros((510, 512), f32), back], 0)
    d_bcx = jnp.concatenate([d_bx * X, d_c, d_bx * B], axis=1).astype(bf)
    d_in = tn(h, d_bcx).astype(bf)
    d_h = share(nt(d_bcx, w_in), c)
    d_src, d_g1 = norm_back(src, s1, g1, d_h)
    d_tokens = d_resid + d_src
    dt = lax.dynamic_update_slice(jnp.zeros((3, 1024), f32), d_taps, (0, 512 * c))
    sm = jnp.concatenate([d_g1[None], d_g2[None], dt], 0).T.astype(bf)
    sm = jnp.pad(sm, ((0, 0), (0, 123)))
    cols = lambda v: jnp.stack([v[:, :512], v[:, 512:]])
    return mixed, d_tokens, d_in, cols(d_out), sm, d_wg, d_wu, cols(d_down)


def body(tokens, lengths, norm1_gain, in_proj, conv_weight, out_proj, norm2_gain, w_gate, w_up, w_down, cotangent):
    rows = tokens.shape[0]
    place = lax.axis_index("shard")
    slot = lax.axis_index("rep")
    slot_ids = jnp.arange(lengths.shape[0], dtype=jnp.int32)
    length = jnp.sum(jnp.where(slot_ids == slot, lengths, 0))
    valid = jnp.clip(length - place * rows, 0, rows)
    keep = (jnp.arange(rows, dtype=jnp.int32) < valid).astype(jnp.float32)[:, None]
    cat, down = prepare(norm1_gain, in_proj, conv_weight, out_proj, norm2_gain, w_gate, w_up, w_down)
    weights = gather_all(cat, down)
    mixed, d_tokens, *grads = middle(tokens, keep, cotangent, *weights)
    return (mixed, d_tokens) + finish(*scatter_all(*grads))

def solution(mesh):
    tok = P(("rep", "shard"), None)
    par = (P("shard"), P("shard", None), P(None, "shard"), P("shard", None), P("shard"), P("shard", None), P("shard", None), P("shard", None))
    return jax.shard_map(body, mesh=mesh, in_specs=(tok, P()) + par + (tok,), out_specs=(tok, tok) + par, check_vma=False)
```

```python
import functools
import jax, jax.numpy as jnp
from jax import lax
from jax.experimental import pallas as pl
from jax.experimental.pallas import tpu as pltpu
from jax.sharding import PartitionSpec as P
MESH = pl.DeviceIdType.MESH
C1 = 2176; HALF = 1152; CAT = 6784; UNIT = 32; DUNIT = 144
COPIES = 160

def spot():
    rep = lax.axis_index("rep"); s = lax.axis_index("shard")
    return (s // 4) % 4, s // 16, ((s // 2) % 2) * 2 + rep, s % 2

def device(x, y, z, c):
    return (z % 2, ((y * 4 + x) * 2 + z // 2) * 2 + c)

def moved(x, y, z, c, axis, step):
    if axis == "x": return device((x + step + 4) % 4, y, z, c)
    return device(x, (y + step + 4) % 4, z, c)

def greet(devices):
    bar = pltpu.get_barrier_semaphore()
    for d in devices:
        pl.semaphore_signal(bar, inc=1, device_id=d, device_id_type=MESH)
    pl.semaphore_wait(bar, len(devices))

class Wire:
    def __init__(self, ss, rs): self.ss, self.rs, self.sent = ss, rs, []
    def send(self, src, dst, dev):
        i = len(self.sent)
        cp = pltpu.make_async_remote_copy(src_ref=src, dst_ref=dst, send_sem=self.ss.at[i], recv_sem=self.rs.at[i], device_id=dev, device_id_type=MESH)
        cp.start(); self.sent.append(cp); return cp
    def drain(self):
        for cp in self.sent: cp.wait_send()

def gather_kernel(cat_in, down_in, wcat, wd, wor, wdr, dnf, dnb, ss, rs, ls):
    x, y, z, c = spot()
    hi = z // 2
    s = ((y * 4 + x) * 2 + hi) * 2 + c
    k = s // 2
    pair = device(x, y, z + 1 - 2 * (z % 2), c)
    cross = device(x, y, 3 - z, c)
    other = device(x, y, z, 1 - c)
    go = {(a, st): moved(x, y, z, c, a, st) for a in "xy" for st in (1, -1)}
    greet(list(go.values()) + [pair, cross, other])
    w = Wire(ss, rs)
    rows = pl.ds(pl.multiple_of(16 * s, 16), 16)
    lc = pltpu.make_async_copy(cat_in.at[c], wcat.at[rows, :], ls.at[0]); lc.start()
    r0 = w.send(cat_in.at[1 - c], wcat.at[rows, :], other)
    dr = pl.ds(pl.multiple_of(72 * c, 8), 72)
    ld = pltpu.make_async_copy(down_in.at[c], dnf.at[dr, :], ls.at[1]); ld.start()
    r1 = w.send(down_in.at[1 - c], dnf.at[dr, :], other)
    lc.wait(); r0.wait_recv()
    urow = pl.ds(pl.multiple_of(UNIT * k, UNIT), UNIT)
    drow = pl.ds(pl.multiple_of(DUNIT * k, 16), DUNIT)
    z1 = w.send(wcat.at[urow, pl.ds(0, C1)], wcat.at[urow, pl.ds(0, C1)], cross)
    z2 = w.send(wcat.at[urow, pl.ds(C1, CAT - C1)], wcat.at[urow, pl.ds(C1, CAT - C1)], cross)
    ld.wait(); r1.wait_recv()
    dnb[...] = dnf[...].astype(jnp.bfloat16)
    ldb = pltpu.make_async_copy(dnb, wd.at[drow, :], ls.at[2]); ldb.start()
    z3 = w.send(dnb, wd.at[drow, :], cross)
    flows = [
        dict(buf=wcat, unit=UNIT, col=0, width=C1, order="xy", need=[z1], fwd=None),
        dict(buf=wcat, unit=UNIT, col=C1 + HALF * (z % 2), width=HALF, order="yx", need=[z2], fwd=pair),
        dict(buf=wcat, unit=UNIT, col=C1 + 2 * HALF + HALF * hi, width=HALF, order="xy", need=[], fwd=cross),
        dict(buf=wd, unit=DUNIT, col=0, width=512, order="yx", need=[z3], fwd=None),
    ]
    def block(f, da, db, unit=None):
        a, b = f["order"]
        pos = {"x": x, "y": y}
        pos[a] = (pos[a] + da + 4) % 4
        pos[b] = (pos[b] + db + 4) % 4
        u = f["unit"]
        row = (pos["y"] * 4 + pos["x"]) * (2 * u)
        n = 2 * u
        if unit is not None: row, n = row + unit * u, u
        col = f["col"] if isinstance(f["col"], int) else pl.multiple_of(f["col"], 128)
        return f["buf"].at[pl.ds(pl.multiple_of(row, 16), n), pl.ds(col, f["width"])]
    def push(f, da, db, dev, unit=None):
        v = block(f, da, db, unit)
        return w.send(v, v, dev)
    def fwd(f, da, db):
        if f["fwd"] is not None: f.setdefault("z", []).append(push(f, da, db, f["fwd"]))
    def open2(f, j):
        b = f["order"][1]
        f[("p", j)] = push(f, j, 0, go[(b, 1)])
        f[("m", j)] = push(f, j, 0, go[(b, -1)])
    for n, f in enumerate(flows):
        for q in f["need"]: q.wait_recv()
        if n == 3: ldb.wait()
        a = f["order"][0]
        f["p"] = push(f, 0, 0, go[(a, 1)])
        f["m"] = push(f, 0, 0, go[(a, -1)])
        open2(f, 0)
    for f in flows:
        a = f["order"][0]
        f["p"].wait_recv(); f["p2"] = push(f, -1, 0, go[(a, 1)], 0)
        f["m"].wait_recv(); f["m2"] = push(f, 1, 0, go[(a, -1)], 1)
        open2(f, -1); open2(f, 1)
        fwd(f, -1, 0); fwd(f, 1, 0)
    for f in flows:
        f["p2"].wait_recv(); f["m2"].wait_recv()
        open2(f, 2); fwd(f, 2, 0)
    for j in (0, -1, 1, 2):
        for f in flows:
            b = f["order"][1]
            f[("p", j)].wait_recv(); f[("p2", j)] = push(f, j, -1, go[(b, 1)], 0)
            f[("m", j)].wait_recv(); f[("m2", j)] = push(f, j, 1, go[(b, -1)], 1)
            fwd(f, j, -1); fwd(f, j, 1)
    for j in (0, -1, 1, 2):
        for f in flows:
            f[("p2", j)].wait_recv(); f[("m2", j)].wait_recv()
            fwd(f, j, 2)
    for f in flows:
        for q in f.get("z", []): q.wait_recv()
    a = w.send(wcat.at[pl.ds(pl.multiple_of(512 * (1 - c), 512), 512), pl.ds(1536, 512)], wor, other)
    b = w.send(wd.at[pl.ds(pl.multiple_of(2304 * (1 - c), 2304), 2304), :], wdr, other)
    a.wait_recv(); b.wait_recv()
    w.drain()

def gather_all(cat, down):
    return pl.pallas_call(
        gather_kernel,
        out_shape=(jax.ShapeDtypeStruct((1024, CAT), jnp.bfloat16), jax.ShapeDtypeStruct((4608, 512), jnp.bfloat16),
            jax.ShapeDtypeStruct((512, 512), jnp.bfloat16), jax.ShapeDtypeStruct((2304, 512), jnp.bfloat16)),
        in_specs=[pl.BlockSpec(memory_space=pl.ANY)] * 2,
        out_specs=(pl.BlockSpec(memory_space=pl.ANY),) * 4,
        scratch_shapes=[pltpu.VMEM((144, 512), jnp.float32), pltpu.VMEM((144, 512), jnp.bfloat16),
            pltpu.SemaphoreType.DMA((COPIES,)), pltpu.SemaphoreType.DMA((COPIES,)), pltpu.SemaphoreType.DMA((3,))],
        compiler_params=pltpu.CompilerParams(collective_id=1, has_side_effects=True, vmem_limit_bytes=32 * 2**20),
        name="gather")(cat, down)

def prepare(norm1_gain, in_proj, conv_weight, out_proj, norm2_gain, w_gate, w_up, w_down):
    small = jnp.stack([norm1_gain, norm2_gain, conv_weight[0], conv_weight[1], conv_weight[2]], axis=1)
    small = jnp.pad(small, ((0, 0), (0, 123)))
    cat = jnp.stack([jnp.concatenate([in_proj[:, 512*p:512*p+512], in_proj[:, 1024+512*p:1536+512*p], in_proj[:, 2048+512*p:2560+512*p],
        out_proj[:, 512*p:512*p+512], small, w_gate[:, 2304*p:2304*p+2304], w_up[:, 2304*p:2304*p+2304]], axis=1) for p in (0, 1)])
    down = jnp.stack([w_down[:, :512], w_down[:, 512:]]).astype(jnp.float32)
    return cat, down

JS = (2, -1, 1, 0)

def add_into(dst, srcs, rows, step=16):
    def body(i, _):
        r = pl.ds(pl.multiple_of(i * step, step), step)
        t = dst[r, :].astype(jnp.float32)
        for q in srcs: t = t + q[r, :].astype(jnp.float32)
        dst[r, :] = t.astype(jnp.bfloat16)
        return 0
    lax.fori_loop(0, rows // step, body, 0)

def scatter_kernel(gin, gout, gsm, gg, gu, gd, ocat, odn,
                   G1, GG, GU, GD, L1, LG, LU, LD, M1, MG, MU, MD,
                   d1, dg, du, dd, fcat, fdn, ss, rs, ls):
    x, y, z, c = spot()
    hi = z // 2
    pair = device(x, y, z + 1 - 2 * (z % 2), c)
    cross = device(x, y, 3 - z, c)
    other = device(x, y, z, 1 - c)
    go = {(a, st): moved(x, y, z, c, a, st) for a in "xy" for st in (1, -1)}
    greet(list(go.values()) + [pair, cross, other])
    w = Wire(ss, rs)
    nl = [0]
    def local(src, dst):
        cp = pltpu.make_async_copy(src, dst, ls.at[nl[0]]); nl[0] += 1; cp.start(); return cp
    rd = w.send(gd.at[1 - c], GD.at[pl.ds(2 * c, 2)], other)
    ld = local(gd.at[c], GD.at[pl.ds(2 * c, 2)])
    lg = [local(gg.at[:, :, :, pl.ds(h * HALF, HALF)], GG.at[h]) for h in (0, 1)]
    lu = [local(gu.at[:, :, :, pl.ds(h * HALF, HALF)], GU.at[h]) for h in (0, 1)]
    ro = w.send(gout.at[1 - c], G1.at[pl.ds(2 * c, 2), :, :, pl.ds(1536, 512)], other)
    lo = local(gout.at[c], G1.at[pl.ds(2 * c, 2), :, :, pl.ds(1536, 512)])
    li = local(gin, G1.at[:, :, :, pl.ds(0, 1536)])
    lsm = local(gsm, G1.at[:, :, :, pl.ds(2048, 128)])
    zl = z % 2
    fd = dict(G=GD, L=LD, M=MD, unit=DUNIT, order="yx")
    fg = dict(G=GG.at[zl], L=LG.at[zl], M=MG, unit=UNIT, order="yx")
    fu = dict(G=GU.at[hi], L=LU.at[hi], M=MU, unit=UNIT, order="xy")
    f1 = dict(G=G1, L=L1, M=M1, unit=UNIT, order="xy")
    flows = [fd, fg, fu, f1]
    def at(f, da, db):
        a, b = f["order"]
        pos = {"x": x, "y": y}
        pos[a] = (pos[a] + da + 4) % 4
        pos[b] = (pos[b] + db + 4) % 4
        return pos["y"], pos["x"]
    def line(f, j):
        return (x + j + 4) % 4 if f["order"] == "xy" else (y + j + 4) % 4
    for q in lg: q.wait()
    for q in lu: q.wait()
    for j in JS:
        yj = line(fg, j); fg[("A", j)] = w.send(GG.at[1 - zl, yj], LG.at[zl, yj], pair)
        xj = line(fu, j); fu[("A", j)] = w.send(GU.at[1 - hi, :, xj], LU.at[hi, :, xj], cross)
    def absorb(f, j):
        if ("A", j) not in f: return
        f[("A", j)].wait_recv()
        l = line(f, j)
        for i in range(4):
            if f is fg: add_into(GG.at[zl, l, i], [LG.at[1 - zl, l, i]], 64)
            else: add_into(GU.at[hi, i, l], [LU.at[1 - hi, i, l]], 64)
    def part(ref, f, pos, u):
        return ref.at[pos[0], pos[1], pl.ds(u * f["unit"], f["unit"])]
    ready = {id(fd): [ld.wait, rd.wait_recv], id(f1): [lo.wait, li.wait, lsm.wait, ro.wait_recv]}
    def first(f, j):
        b = f["order"][1]
        absorb(f, j)
        p = at(f, j, 2)
        f[("s", j)] = w.send(part(f["G"], f, p, 0), part(f["L"], f, p, 0), go[(b, 1)])
        f[("t", j)] = w.send(part(f["G"], f, p, 1), part(f["L"], f, p, 1), go[(b, -1)])
    def second(f, j):
        b = f["order"][1]
        f[("s", j)].wait_recv(); p = at(f, j, 1)
        add_into(part(f["G"], f, p, 0), [part(f["L"], f, p, 0)], f["unit"])
        f[("s2", j)] = w.send(f["G"].at[p[0], p[1]], f["L"].at[p[0], p[1]], go[(b, 1)])
        f[("t", j)].wait_recv(); p = at(f, j, -1)
        add_into(part(f["G"], f, p, 1), [part(f["L"], f, p, 1)], f["unit"])
        o = at(f, j, 1)
        f[("t2", j)] = w.send(f["G"].at[p[0], p[1]], f["L"].at[o[0], o[1]], go[(b, -1)])

    def third(f, j):
        a = f["order"][0]
        f[("s2", j)].wait_recv(); f[("t2", j)].wait_recv()
        p = at(f, j, 0); o = at(f, j, 2)
        add_into(f["G"].at[p[0], p[1]], [f["L"].at[p[0], p[1]], f["L"].at[o[0], o[1]]], 2 * f["unit"])
        u = f["unit"]; M = f["M"]
        if j == 2:
            f["c"] = w.send(part(f["G"], f, p, 0), M.at[pl.ds(0, u)], go[(a, 1)])
            f["d"] = w.send(part(f["G"], f, p, 1), M.at[pl.ds(u, u)], go[(a, -1)])
        elif j == 1:
            f["c"].wait_recv(); add_into(part(f["G"], f, p, 0), [M.at[pl.ds(0, u)]], u)
            f["c2"] = w.send(f["G"].at[p[0], p[1]], M.at[pl.ds(2 * u, 2 * u)], go[(a, 1)])
        elif j == -1:
            f["d"].wait_recv(); add_into(part(f["G"], f, p, 1), [M.at[pl.ds(u, u)]], u)
            f["d2"] = w.send(f["G"].at[p[0], p[1]], M.at[pl.ds(4 * u, 2 * u)], go[(a, -1)])

    for f in (fd, f1):
        for q in ready[id(f)]: q()
    for f in (fd, f1):
        for j in JS: first(f, j)
    second(fd, 2); second(f1, 2); first(fg, 2); first(fu, 2)
    second(fd, -1); second(f1, -1); third(fd, 2); third(f1, 2); first(fg, -1); first(fu, -1); second(fg, 2); second(fu, 2)
    second(fd, 1); second(f1, 1); third(fd, -1); third(f1, -1); first(fg, 1); first(fu, 1); second(fg, -1); second(fu, -1); third(fg, 2); third(fu, 2)
    second(fd, 0); second(f1, 0); third(fd, 1); third(f1, 1); first(fg, 0); first(fu, 0); second(fg, 1); second(fu, 1); third(fg, -1); third(fu, -1)
    third(fd, 0); third(f1, 0); second(fg, 0); second(fu, 0); third(fg, 1); third(fu, 1)
    third(fg, 0); third(fu, 0)
    for f in flows:
        f["c2"].wait_recv(); f["d2"].wait_recv()
        u = f["unit"]; M = f["M"]; mine = f["G"].at[y, x]
        add_into(mine, [M.at[pl.ds(2 * u, 2 * u)], M.at[pl.ds(4 * u, 2 * u)]], 2 * u)
        away = mine.at[pl.ds(u * (1 - hi), u)]
        if f is fd: f["e"] = w.send(away, dd.at[0], cross)
        if f is f1: f["e"] = w.send(away, d1.at[0], cross)
        if f is fu: f["e"] = w.send(away, du.at[0, hi], cross)
        if f is fg: f["e"] = w.send(mine, dg.at[0, zl], pair)
    own = lambda f: f["G"].at[y, x, pl.ds(f["unit"] * hi, f["unit"])]
    fd["e"].wait_recv(); add_into(own(fd), [dd.at[0]], DUNIT)
    fd["e2"] = w.send(own(fd), dd.at[1], pair)
    fg["e"].wait_recv()
    fg["e2"] = w.send(fg["G"].at[y, x, pl.ds(UNIT * (1 - hi), UNIT)], dg.at[1, zl, pl.ds(0, UNIT)], cross)
    fg["e3"] = w.send(dg.at[0, 1 - zl, pl.ds(UNIT * (1 - hi), UNIT)], dg.at[1, 1 - zl, pl.ds(0, UNIT)], cross)
    fu["e"].wait_recv()
    fu["e2"] = w.send(own(fu), du.at[1, hi], pair)
    fu["e3"] = w.send(du.at[0, 1 - hi], du.at[1, 1 - hi], pair)
    f1["e"].wait_recv(); add_into(own(f1), [d1.at[0]], UNIT)
    f1["e2"] = w.send(own(f1), d1.at[1], pair)
    f32 = lambda v: v.astype(jnp.float32)
    fd["e2"].wait_recv()
    fdn[...] = f32(own(fd)[...]) + f32(dd[1])
    o1 = w.send(fdn.at[pl.ds(pl.multiple_of(72 * (1 - c), 8), 72)], odn.at[c], other)
    q1 = local(fdn.at[pl.ds(pl.multiple_of(72 * c, 8), 72)], odn.at[c])
    for q in ("e2", "e3"): fg[q].wait_recv(); fu[q].wait_recv()
    cg = C1 + HALF * zl; cgo = C1 + HALF * (1 - zl)
    cu = C1 + 2 * HALF + HALF * hi; cuo = C1 + 2 * HALF + HALF * (1 - hi)
    m128 = lambda v: pl.ds(pl.multiple_of(v, 128), HALF)
    fcat[:, m128(cg)] = f32(own(fg)[...]) + f32(dg[1, zl, pl.ds(0, UNIT), :])
    fcat[:, m128(cgo)] = f32(dg[0, 1 - zl, pl.ds(UNIT * hi, UNIT), :]) + f32(dg[1, 1 - zl, pl.ds(0, UNIT), :])
    fcat[:, m128(cu)] = f32(own(fu)[...]) + f32(du[1, hi])
    fcat[:, m128(cuo)] = f32(du[0, 1 - hi]) + f32(du[1, 1 - hi])
    f1["e2"].wait_recv()
    fcat[:, pl.ds(0, C1)] = f32(own(f1)[...]) + f32(d1[1])
    o2 = w.send(fcat.at[pl.ds(pl.multiple_of(16 * (1 - c), 16), 16)], ocat.at[c], other)
    q2 = local(fcat.at[pl.ds(pl.multiple_of(16 * c, 16), 16)], ocat.at[c])
    q1.wait(); q2.wait(); o1.wait_recv(); o2.wait_recv()
    w.drain()

def scatter_all(gin, gout, gsm, gg, gu, gd):
    bf = jnp.bfloat16
    V = lambda *s: pltpu.VMEM(s, bf)
    grid = lambda v: v.reshape(4, 4, -1, v.shape[-1])
    half = lambda v: v.reshape(2, 2, 4, -1, 512)
    return pl.pallas_call(
        scatter_kernel,
        out_shape=(jax.ShapeDtypeStruct((2, 16, CAT), jnp.float32), jax.ShapeDtypeStruct((2, 72, 512), jnp.float32)),
        in_specs=[pl.BlockSpec(memory_space=pl.ANY)] * 6,
        out_specs=(pl.BlockSpec(memory_space=pl.ANY),) * 2,
        scratch_shapes=[V(4, 4, 64, C1), V(2, 4, 4, 64, HALF), V(2, 4, 4, 64, HALF), V(4, 4, 288, 512),
            V(4, 4, 64, C1), V(2, 4, 4, 64, HALF), V(2, 4, 4, 64, HALF), V(4, 4, 288, 512),
            V(192, C1), V(192, HALF), V(192, HALF), V(864, 512),
            V(2, UNIT, C1), V(2, 2, 64, HALF), V(2, 2, UNIT, HALF), V(2, DUNIT, 512),
            pltpu.VMEM((UNIT, CAT), jnp.float32), pltpu.VMEM((DUNIT, 512), jnp.float32),
            pltpu.SemaphoreType.DMA((COPIES,)), pltpu.SemaphoreType.DMA((COPIES,)), pltpu.SemaphoreType.DMA((12,))],
        compiler_params=pltpu.CompilerParams(collective_id=2, has_side_effects=True, vmem_limit_bytes=60 * 2**20),
        name="scatter")(grid(gin), half(gout), grid(gsm), grid(gg), grid(gu), half(gd))

def finish(ocat, odn):
    a, b = ocat[0], ocat[1]
    j = lambda o, n: [a[:, o:o + n], b[:, o:o + n]]
    d_in = jnp.concatenate(j(0, 512) + j(512, 512) + j(1024, 512), axis=1)
    d_out = jnp.concatenate(j(1536, 512), axis=1)
    sm = a[:, 2048:2053] + b[:, 2048:2053]
    d_gate = jnp.concatenate(j(C1, 2304), axis=1)
    d_up = jnp.concatenate(j(C1 + 2304, 2304), axis=1)
    d_down = jnp.concatenate([odn[0], odn[1]], axis=1)
    return sm[:, 0], d_in, sm[:, 2:5].T, d_out, sm[:, 1], d_gate, d_up, d_down

EPS = 1e-05

def swap(v):
    return lax.ppermute(v, "shard", [(s, s ^ 1) for s in range(64)])

def ordered(own, oth, c, axis=0):
    return jnp.where(c == 0, jnp.concatenate([own, oth], axis), jnp.concatenate([oth, own], axis))

def norm_rows(rows, gain):
    scale = lax.rsqrt(jnp.mean(rows * rows, axis=1, keepdims=True) + EPS)
    return scale, rows * scale * gain

def norm_back(rows, scale, gain, grad_norm):
    gain_grad = jnp.sum(grad_norm * rows * scale, axis=0)
    weighted = grad_norm * gain
    inner = jnp.mean(weighted * rows, axis=1, keepdims=True)
    return scale * weighted - rows * (scale * scale * scale) * inner, gain_grad

def dot(a, b): return jnp.dot(a, b, preferred_element_type=jnp.float32)
def tn(a, b): return lax.dot_general(a, b, (((0,), (0,)), ((), ())), preferred_element_type=jnp.float32)
def nt(a, b): return lax.dot_general(a, b, (((1,), (1,)), ((), ())), preferred_element_type=jnp.float32)

def share(part, c):
    n = part.shape[0] // 2
    own = lax.dynamic_slice_in_dim(part, n * c, n, 0)
    away = lax.dynamic_slice_in_dim(part, n * (1 - c), n, 0)
    return own + swap(away)

def middle(tokens, keep, cot, wcat, wd, wor, wdr):
    s_id = lax.axis_index("shard"); c = s_id % 2
    bf = jnp.bfloat16; f32 = jnp.float32
    inside = (s_id >= 2).astype(f32)
    small = wcat[:, 2048:2053].astype(f32).T
    g1, g2, taps = small[0], small[1], small[2:5]
    taps = lax.dynamic_slice_in_dim(taps, 512 * c, 512, 1)
    rows2 = lambda v, n: lax.dynamic_slice_in_dim(v, n * c, n, 0)
    w_in = wcat[:, :1536]
    w_out = ordered(rows2(wcat[:, 1536:2048], 512), wor, c, 1)
    w_dn = ordered(rows2(wd, 2304), wdr, c, 1)
    w_g, w_u = wcat[:, C1:C1 + 2304], wcat[:, C1 + 2304:]
    d_ffo_own = (keep * cot.astype(f32)).astype(bf)
    T = ordered(tokens, swap(tokens), c).astype(f32)
    d_ffo = ordered(d_ffo_own, swap(d_ffo_own), c)
    src = tokens.astype(f32)
    _, hf = norm_rows(T, g1); h = hf.astype(bf)
    s1, _ = norm_rows(src, g1)
    bcx = dot(h, w_in)
    B, C, X = bcx[:, :512], bcx[:, 512:1024], bcx[:, 1024:]
    bx = (B * X).astype(bf)
    edge = lax.ppermute(bx[510:], "shard", [(s, s + 2) for s in range(62)])
    ext = jnp.concatenate([edge.astype(f32) * inside, bx.astype(f32)], axis=0)
    conv = taps[0] * ext[:-2] + taps[1] * ext[1:-1] + taps[2] * ext[2:]
    y = (C * conv).astype(bf)
    resid = src + share(dot(y, w_out), c)
    s2, h2f = norm_rows(resid, g2)
    h2o = h2f.astype(bf)
    h2 = ordered(h2o, swap(h2o), c)
    gate = dot(h2, w_g); up = dot(h2, w_u)
    sg = jax.nn.sigmoid(gate); sw = gate * sg
    act = (sw * up).astype(bf)
    ffo = share(dot(act, w_dn), c)
    mixed = (keep * (resid + ffo)).astype(bf)
    d_down = tn(act, d_ffo).astype(bf)
    d_act = nt(d_ffo, w_dn)
    d_gate = (d_act * up * sg * (1.0 + gate * (1.0 - sg))).astype(bf)
    d_up = (d_act * sw).astype(bf)
    d_wg = tn(h2, d_gate).astype(bf); d_wu = tn(h2, d_up).astype(bf)
    d_h2 = share(nt(d_gate, w_g) + nt(d_up, w_u), c)
    d_rn, d_g2 = norm_back(resid, s2, g2, d_h2)
    d_resid = keep * cot.astype(f32) + d_rn
    dmo = d_resid.astype(bf)
    d_mix = ordered(dmo, swap(dmo), c)
    d_out = tn(y, d_mix).astype(bf)
    d_y = nt(d_mix, w_out)
    d_c = d_y * conv; d_conv = d_y * C
    d_taps = jnp.stack([jnp.sum(d_conv * ext[i:i + 512], axis=0) for i in range(3)])
    z2 = jnp.zeros((2, 512), f32)
    de = jnp.concatenate([taps[0] * d_conv, z2], 0) + jnp.concatenate([z2[:1], taps[1] * d_conv, z2[:1]], 0) + jnp.concatenate([z2, taps[2] * d_conv], 0)
    back = lax.ppermute(de[:2] * inside, "shard", [(s, s - 2) for s in range(2, 64)])
    d_bx = de[2:] + jnp.concatenate([jnp.zeros((510, 512), f32), back], 0)
    d_bcx = jnp.concatenate([d_bx * X, d_c, d_bx * B], axis=1).astype(bf)
    d_in = tn(h, d_bcx).astype(bf)
    d_h = share(nt(d_bcx, w_in), c)
    d_src, d_g1 = norm_back(src, s1, g1, d_h)
    d_tokens = d_resid + d_src
    dt = lax.dynamic_update_slice(jnp.zeros((3, 1024), f32), d_taps, (0, 512 * c))
    sm = jnp.concatenate([d_g1[None], d_g2[None], dt], 0).T.astype(bf)
    sm = jnp.pad(sm, ((0, 0), (0, 123)))
    cols = lambda v: jnp.stack([v[:, :512], v[:, 512:]])
    return mixed, d_tokens, d_in, cols(d_out), sm, d_wg, d_wu, cols(d_down)


def body(tokens, lengths, norm1_gain, in_proj, conv_weight, out_proj, norm2_gain, w_gate, w_up, w_down, cotangent):
    rows = tokens.shape[0]
    place = lax.axis_index("shard")
    slot = lax.axis_index("rep")
    slot_ids = jnp.arange(lengths.shape[0], dtype=jnp.int32)
    length = jnp.sum(jnp.where(slot_ids == slot, lengths, 0))
    valid = jnp.clip(length - place * rows, 0, rows)
    keep = (jnp.arange(rows, dtype=jnp.int32) < valid).astype(jnp.float32)[:, None]
    cat, down = prepare(norm1_gain, in_proj, conv_weight, out_proj, norm2_gain, w_gate, w_up, w_down)
    weights = gather_all(cat, down)
    mixed, d_tokens, *grads = middle(tokens, keep, cotangent, *weights)
    return (mixed, d_tokens) + finish(*scatter_all(*grads))

def solution(mesh):
    tok = P(("rep", "shard"), None)
    par = (P("shard"), P("shard", None), P(None, "shard"), P("shard", None), P("shard"), P("shard", None), P("shard", None), P("shard", None))
    return jax.shard_map(body, mesh=mesh, in_specs=(tok, P()) + par + (tok,), out_specs=(tok, tok) + par, check_vma=False)
```

```python
import functools
import jax, jax.numpy as jnp
from jax import lax
from jax.experimental import pallas as pl
from jax.experimental.pallas import tpu as pltpu
from jax.sharding import PartitionSpec as P
MESH = pl.DeviceIdType.MESH
EPS = 1e-05
bf, f32 = jnp.bfloat16, jnp.float32
C1 = 2176; HALF = 1152; CAT = 6784; UNIT = 32; DUNIT = 144; FH = 2304
COPIES = 272
JS = (2, -1, 1, 0)
PAIR, CROSS, X, Y = 1, 2, 0, 1
ONE, TWO, THREE = 1, 2, 3
XY, YX = (X, Y), (Y, X)
class Box:
    def __init__(self, *a, **kw):
        for d in a: self.__dict__.update(d)
        self.__dict__.update(kw)

FLOWS = Box(
    f1a=Box(kind=1, base=0, step=512, gw=512, fw=512, to=PAIR, order=XY),
    f1b=Box(kind=1, base=1024, step=384, gw=768, fw=384, to=CROSS, order=YX),
    f2a=Box(kind=2, base=C1, step=768, gw=1536, fw=768, to=PAIR, order=YX),
    f2b=Box(kind=2, base=C1 + FH, step=640, gw=1664, fw=640, to=CROSS, order=XY),
    f3a=Box(kind=3, base=0, step=0, gw=256, fw=0, to=None, order=XY),
    f3b=Box(kind=3, base=256, step=0, gw=256, fw=0, to=None, order=YX))

def spot():
    rep = lax.axis_index("rep"); s = lax.axis_index("shard")
    return (s // 4) % 4, s // 16, ((s // 2) % 2) * 2 + rep, s % 2

def device(x, y, z, c):
    return (z % 2, ((y * 4 + x) * 2 + z // 2) * 2 + c)

def moved(x, y, z, c, axis, step):
    if axis == X: return device((x + step + 4) % 4, y, z, c)
    return device(x, (y + step + 4) % 4, z, c)

def along(x, y, z, c, step):
    k = ((y * 4 + x) * 2 + z // 2 + step + 32) % 32
    return device((k // 2) % 4, k // 8, (k % 2) * 2 + z % 2, c)

def greet(devices):
    bar = pltpu.get_barrier_semaphore()
    for d in devices:
        pl.semaphore_signal(bar, inc=1, device_id=d, device_id_type=MESH)
    pl.semaphore_wait(bar, len(devices))

class Copy:
    def __init__(self, cp): self.cp, self.here, self.gone = cp, False, False
    def wait_recv(self): self.cp.wait_recv(); self.here = True
    def wait_send(self): self.cp.wait_send(); self.gone = True

class Wire:
    def __init__(self, ss, rs, ls): self.ss, self.rs, self.ls, self.sent, self.n = ss, rs, ls, [], 0
    def send(self, src, dst, dev):
        i = len(self.sent)
        cp = pltpu.make_async_remote_copy(src_ref=src, dst_ref=dst, send_sem=self.ss.at[i], recv_sem=self.rs.at[i], device_id=dev, device_id_type=MESH)
        cp.start(); self.sent.append(Copy(cp)); return self.sent[-1]
    def local(self, src, dst):
        cp = pltpu.make_async_copy(src, dst, self.ls.at[self.n]); self.n += 1; cp.start(); return cp
    def drain(self):
        for cp in self.sent:
            if not cp.here: cp.wait_recv()
            if not cp.gone: cp.wait_send()

def at_rows(v, n, m=16): return pl.ds(pl.multiple_of(v, m), n)

class Pump:
    def __init__(self, steps): self.steps, self.seen = steps, set()
    def run(self, n):
        for _ in range(n):
            t = next(self.steps, None)
            if t is None: return False
            self.seen.add(t)
        return True
    def until(self, tag):
        while tag not in self.seen:
            if not self.run(1): raise ValueError(tag)
    def finish(self):
        while self.run(1): pass

def gather_steps(w, go, pair, cross, other, x, y, z, wcat, wd, wdr, dnb, k, unit_in, unit_down):
    hi = z // 2
    urow = at_rows(UNIT * k, UNIT, UNIT)
    drow = at_rows(DUNIT * k, DUNIT)
    cat = lambda a, n: wcat.at[urow, pl.ds(a, n)]
    unit_in()
    z1 = w.send(cat(0, C1), cat(0, C1), cross)
    z2 = w.send(cat(C1, CAT - C1), cat(C1, CAT - C1), cross)
    unit_down()
    z3 = w.send(dnb, wd.at[drow, :], cross)
    ldb = w.local(dnb, wd.at[drow, :])
    def F(t, need):
        sel = {PAIR: z % 2, CROSS: hi, None: 0}[t.to]
        d = t.kind == 3
        return Box(vars(t), buf=wd if d else wcat, unit=DUNIT if d else UNIT, mine=(t.base + t.step * sel, t.gw), alone=(t.base + t.gw * sel, t.fw),
            need=need, fwd={PAIR: pair, CROSS: cross, None: None}[t.to], z=[], p={}, m={}, p2={}, m2={})
    p1 = [F(FLOWS.f1a, [z1.wait_recv]), F(FLOWS.f1b, [])]
    p2 = [F(FLOWS.f2a, [z2.wait_recv]), F(FLOWS.f2b, [])]
    p3 = [F(FLOWS.f3a, [z3.wait_recv, ldb.wait]), F(FLOWS.f3b, [])]
    def block(f, da, db, unit=None, cols=None, buf=None):
        a, b = f.order
        pos = {X: x, Y: y}
        pos[a] = (pos[a] + da + 4) % 4
        pos[b] = (pos[b] + db + 4) % 4
        u = f.unit
        row = (pos[Y] * 4 + pos[X]) * (2 * u)
        n = 2 * u
        if unit is not None: row, n = row + unit * u, u
        col, width = cols or f.mine
        return (f.buf if buf is None else buf).at[at_rows(row, n), pl.ds(col if isinstance(col, int) else pl.multiple_of(col, 128), width)]
    def push(f, da, db, dev, unit=None):
        v = block(f, da, db, unit)
        return w.send(v, v, dev)
    def fwd(f, da, db):
        if f.fwd is not None:
            v = block(f, da, db, None, f.alone)
            f.z.append(w.send(v, v, f.fwd))
        if f.kind == 3:
            v = block(f, da, db)
            f.z.append(w.send(v, block(f, da, db, None, f.mine, wdr), other))
    def open2(f, j):
        b = f.order[1]
        f.p[j] = push(f, j, 0, go[(b, 1)])
        f.m[j] = push(f, j, 0, go[(b, -1)])
    def r1(f):
        for q in f.need: q()
        a = f.order[0]
        f.p[None] = push(f, 0, 0, go[(a, 1)])
        f.m[None] = push(f, 0, 0, go[(a, -1)])
        open2(f, 0)
        if f.kind == 3: fwd(f, 0, 0)
    def r2(f):
        a = f.order[0]
        f.p[None].wait_recv(); f.p2[None] = push(f, -1, 0, go[(a, 1)], 0)
        f.m[None].wait_recv(); f.m2[None] = push(f, 1, 0, go[(a, -1)], 1)
        open2(f, -1); open2(f, 1)
        fwd(f, -1, 0); fwd(f, 1, 0)
    def r3(f):
        f.p2[None].wait_recv(); f.m2[None].wait_recv()
        open2(f, 2); fwd(f, 2, 0)
    def r4(f, j):
        b = f.order[1]
        f.p[j].wait_recv(); f.p2[j] = push(f, j, -1, go[(b, 1)], 0)
        f.m[j].wait_recv(); f.m2[j] = push(f, j, 1, go[(b, -1)], 1)
        fwd(f, j, -1); fwd(f, j, 1)
    def r5(f, j):
        f.p2[j].wait_recv(); f.m2[j].wait_recv()
        fwd(f, j, 2)
    def both(g, p, *a):
        for f in p: g(f, *a)
    order = (0, -1, 1, 2)
    both(r1, p1); yield 0
    both(r2, p1); yield 0
    both(r3, p1); yield 0
    both(r1, p2); yield 0
    both(r4, p1, 0); yield 0
    both(r4, p1, -1); yield 0
    both(r4, p1, 1); yield 0
    both(r2, p2); yield 0
    both(r4, p1, 2); yield 0
    both(r3, p2); yield 0
    for j in order: both(r5, p1, j)
    for f in p1:
        for q in f.z: q.wait_recv()
    yield ONE
    both(r4, p2, 0); yield 0
    both(r1, p3); yield 0
    both(r4, p2, -1); yield 0
    both(r4, p2, 1); yield 0
    both(r2, p3); yield 0
    both(r4, p2, 2); yield 0
    both(r3, p3); yield 0
    both(r5, p2, 0); both(r5, p2, -1); yield 0
    both(r4, p3, 0); yield 0
    both(r5, p2, 1); both(r5, p2, 2); yield 0
    both(r4, p3, -1); yield 0
    for f in p2:
        for q in f.z: q.wait_recv()
    yield TWO
    both(r4, p3, 1); yield 0
    both(r4, p3, 2); yield 0
    for j in order: both(r5, p3, j)
    yield THREE

def dot(a, b): return jnp.dot(a, b, preferred_element_type=f32)
def tn(a, b): return lax.dot_general(a, b, (((0,), (0,)), ((), ())), preferred_element_type=f32)
def nt(a, b): return lax.dot_general(a, b, (((1,), (1,)), ((), ())), preferred_element_type=f32)

A_GOT = dict(wcat=((1024, CAT), bf), wd=((4608, 512), bf), wor=((512, 512), bf), wdr=((4608, 512), bf))
A_MADE = dict(h=((512, 1024), bf), bcx=((512, 1536), bf), ext=((528, 512), f32), conv=((512, 512), bf), y=((512, 512), bf),
    resid=((256, 1024), f32), h2=((512, 1024), bf), gate=((512, FH), bf), up=((512, FH), bf), act=((512, FH), bf),
    dffo=((512, 1024), bf), ddown=((2, FH, 512), bf), small=((8, 1024), f32))
A_SCR = dict(T=((512, 1024), bf), cotv=((256, 1024), bf), win=((1024, 1536), bf), wo=((512, 1024), bf), wsm=((1024, 128), bf),
    wg=((1024, FH), bf), wu=((1024, FH), bf), cpart=((512, 512), f32), mixs=((256, 1024), f32), mixr=((256, 1024), f32),
    dnf=((DUNIT, 512), f32), dns=((72, 512), f32), dnb=((DUNIT, 512), bf),
    inp=((16, 3072), bf), outp=((16, 1024), bf), sml=((16, 128), bf), wgs=((16, 4608), bf), wus=((16, 4608), bf), wds=((72, 1024), bf), keepv=((256, 1), f32))

def named(groups, refs):
    refs, out = list(refs), []
    for g in groups:
        out.append(Box(dict(zip(g, refs)))); refs = refs[len(g):]
    return out, refs

def forward_kernel(*refs):
    A_IN = dict(tokens=0, cot=0, keep=0, inp=0, outp=0, sml=0, wgs=0, wus=0, wds=0)
    (I, O, M, V, S), (ss, rs, ls) = named([A_IN, A_GOT, A_MADE, A_MADE, A_SCR], refs)
    wcat, wd, wor, wdr = O.wcat, O.wd, O.wor, O.wdr
    x, y, z, c = spot()
    hi = z // 2
    s = ((y * 4 + x) * 2 + hi) * 2 + c
    k = s // 2
    pair = device(x, y, z + 1 - 2 * (z % 2), c)
    cross = device(x, y, 3 - z, c)
    other = device(x, y, z, 1 - c)
    nxt, prv = along(x, y, z, c, 1), along(x, y, z, c, -1)
    go = {(a, st): moved(x, y, z, c, a, st) for a in XY for st in (1, -1)}
    w = Wire(ss, rs, ls)
    own, oth = at_rows(256 * c, 256, 256), at_rows(256 * (1 - c), 256, 256)
    col = lambda p, n: pl.ds(pl.multiple_of(p, 128), n)
    lds = w.local(I.wds, S.wds)
    lin = [w.local(a, b) for a, b in ((I.sml, S.sml), (I.inp, S.inp), (I.outp, S.outp), (I.wgs, S.wgs), (I.wus, S.wus))]
    lcot = [w.local(I.cot, S.cotv), w.local(I.keep, S.keepv)]
    ltok = w.local(I.tokens, S.T.at[own])
    greet(list(go.values()) + [pair, cross, other, nxt, prv])
    rows = at_rows(16 * s, 16)
    pieces = [(I.inp, S.inp, 1024 * i, 512, 512 * i) for i in range(3)] + [(I.outp, S.outp, 0, 512, 1536), (I.wgs, S.wgs, 0, FH, C1), (I.wus, S.wus, 0, FH, C1 + FH)]
    got = [w.send(I.sml, wcat.at[rows, pl.ds(2048, 128)], other)]
    for src, _, a, n, d in pieces: got.append(w.send(src.at[:, col(a + n * (1 - c), n)], wcat.at[rows, pl.ds(d, n)], other))
    for q in lin: q.wait()
    mine = [w.local(S.sml, wcat.at[rows, pl.ds(2048, 128)])]
    for _, src, a, n, d in pieces: mine.append(w.local(src.at[:, col(a + n * c, n)], wcat.at[rows, pl.ds(d, n)]))
    lds.wait()
    S.dns[...] = S.wds[:, col(512 * (1 - c), 512)].astype(f32)
    gdn = w.send(S.dns, S.dnf.at[at_rows(72 * c, 72, 8)], other)
    S.dnf[at_rows(72 * c, 72, 8), :] = S.wds[:, col(512 * c, 512)].astype(f32)
    gtok = w.send(I.tokens, S.T.at[own], other)
    def unit_in():
        for q in mine: q.wait()
        for q in got: q.wait_recv()
    def unit_down():
        gdn.wait_recv()
        S.dnb[...] = S.dnf[...].astype(bf)
    pump = Pump(gather_steps(w, go, pair, cross, other, x, y, z, wcat, wd, wdr, S.dnb, k, unit_in, unit_down))
    pump.run(1)
    for q in lcot: q.wait()
    V.dffo[own, :] = (S.keepv[...] * S.cotv[...].astype(f32)).astype(bf)
    gdf = w.send(V.dffo.at[own], V.dffo.at[own], other)
    ltok.wait(); gtok.wait_recv()
    outs = []
    def save(**kw):
        for n in kw: outs.append(w.local(vars(V)[n], vars(M)[n]))
    pump.until(ONE)
    l1 = w.local(wcat.at[:, pl.ds(2048, 128)], S.wsm)
    l2 = w.local(wcat.at[:, pl.ds(0, 1536)], S.win)
    go_ = w.send(wcat.at[at_rows(512 * (1 - c), 512, 512), pl.ds(1536, 512)], wor, other)
    l3 = w.local(wcat.at[at_rows(512 * c, 512, 512), pl.ds(1536, 512)], S.wo.at[:, col(512 * c, 512)])
    l1.wait()
    eye = (lax.broadcasted_iota(jnp.int32, (8, 128), 0) == lax.broadcasted_iota(jnp.int32, (8, 128), 1)).astype(f32).astype(bf)
    V.small[...] = nt(eye, S.wsm[...])
    g1, g2 = V.small[0:1, :], V.small[1:2, :]
    def norm1(i, _):
        q = at_rows(i * 64, 64, 64)
        t = S.T[q, :].astype(f32)
        sc = lax.rsqrt(jnp.mean(t * t, axis=1, keepdims=True) + EPS)
        V.h[q, :] = (t * sc * g1).astype(bf)
        return 0
    lax.fori_loop(0, 8, norm1, 0)
    l2.wait(); go_.wait_recv()
    l4 = w.local(wor, S.wo.at[:, col(512 * (1 - c), 512)])
    ext = V.ext
    for n in (0, 256):
        b_ = dot(V.h[...], S.win[:, n:n + 256])
        x_ = dot(V.h[...], S.win[:, 1024 + n:1280 + n])
        V.bcx[:, n:n + 256] = b_.astype(bf)
        V.bcx[:, 1024 + n:1280 + n] = x_.astype(bf)
        ext[16:528, n:n + 256] = (b_ * x_).astype(bf).astype(f32)
    ghalo = w.send(ext.at[pl.ds(520, 8)], ext.at[pl.ds(8, 8)], nxt)
    pump.run(1)
    for n in (0, 256):
        c_ = dot(V.h[...], S.win[:, 512 + n:768 + n])
        S.cpart[:, n:n + 256] = c_
        V.bcx[:, 512 + n:768 + n] = c_.astype(bf)
    l3.wait(); l4.wait()
    ghalo.wait_recv()
    inside = (k > 0).astype(f32)
    ext[8:16, :] = ext[8:16, :] * inside
    t0, t1, t2 = (V.small[2 + i:3 + i, col(512 * c, 512)] for i in range(3))
    for q in range(0, 512, 128):
        cv = t0 * ext[14 + q:142 + q, :] + t1 * ext[15 + q:143 + q, :] + t2 * ext[16 + q:144 + q, :]
        V.conv[q:q + 128, :] = cv.astype(bf)
        V.y[q:q + 128, :] = (S.cpart[q:q + 128, :] * cv).astype(bf)
    S.mixs[...] = dot(V.y[oth, :], S.wo[...])
    gmix = w.send(S.mixs, S.mixr, other)
    V.resid[...] = dot(V.y[own, :], S.wo[...])
    save(h=1, bcx=1, ext=1, conv=1, y=1, small=1)
    pump.run(1)
    gmix.wait_recv()
    def norm2(i, _):
        q = at_rows(i * 64, 64, 64)
        t = S.T[at_rows(256 * c + i * 64, 64, 64), :].astype(f32) + (V.resid[q, :] + S.mixr[q, :])
        V.resid[q, :] = t
        sc = lax.rsqrt(jnp.mean(t * t, axis=1, keepdims=True) + EPS)
        V.h2[at_rows(256 * c + i * 64, 64, 64), :] = (t * sc * g2).astype(bf)
        return 0
    lax.fori_loop(0, 4, norm2, 0)
    gh2 = w.send(V.h2.at[own], V.h2.at[own], other)
    save(resid=1)
    pump.until(TWO)
    lg = w.local(wcat.at[:, pl.ds(C1, FH)], S.wg)
    lu = w.local(wcat.at[:, pl.ds(C1 + FH, FH)], S.wu)
    gh2.wait_recv(); gdf.wait_recv()
    save(h2=1, dffo=1)
    lg.wait(); lu.wait()
    for n in range(0, FH, 768):
        g_ = dot(V.h2[...], S.wg[:, n:n + 768])
        u_ = dot(V.h2[...], S.wu[:, n:n + 768])
        V.gate[:, n:n + 768] = g_.astype(bf)
        V.up[:, n:n + 768] = u_.astype(bf)
        V.act[:, n:n + 768] = (g_ * jax.nn.sigmoid(g_) * u_).astype(bf)
        pump.run(1)
    save(gate=1, up=1, act=1)
    def down(i, _):
        q = at_rows(i * 256, 256, 256)
        t = tn(V.act[:, q], V.dffo[...]).astype(bf)
        V.ddown[0, q, :] = t[:, :512]
        V.ddown[1, q, :] = t[:, 512:]
        return 0
    lax.fori_loop(0, 9, down, 0)
    save(ddown=1)
    pump.finish()
    for q in outs: q.wait()
    w.drain()

def call(kernel, outs, scratch, ident, limit, extra, *args):
    hbm = pl.BlockSpec(memory_space=pl.ANY)
    return pl.pallas_call(
        kernel, out_shape=tuple(jax.ShapeDtypeStruct(*v) for v in outs), in_specs=[hbm] * len(args), out_specs=(hbm,) * len(outs),
        scratch_shapes=[pltpu.VMEM(*v) for v in scratch] + [pltpu.SemaphoreType.DMA((n,)) for n in (COPIES, COPIES, 96)] + extra,
        compiler_params=pltpu.CompilerParams(collective_id=ident, has_side_effects=True, vmem_limit_bytes=limit * 2**20))(*args)

def forward_all(*args):
    outs = call(forward_kernel, [*A_GOT.values(), *A_MADE.values()], [*A_MADE.values(), *A_SCR.values()], 1, 60, [], *args)
    return dict(zip([*A_GOT, *A_MADE], outs))

def smalls(norm1_gain, norm2_gain, conv_weight):
    small = jnp.concatenate([norm1_gain[:, None], norm2_gain[:, None], conv_weight.T], axis=1)
    return jnp.pad(small, ((0, 0), (0, 123)))


RFLOWS = dict(
    f1a=Box(kind=1, base=0, step=0, gw=256, fw=0, to=None, order=XY),
    f1b=Box(kind=1, base=256, step=0, gw=256, fw=0, to=None, order=YX),
    f1s=Box(kind=0, base=0, step=0, gw=128, fw=0, to=None, order=XY),
    f2a=Box(kind=2, base=0, step=768, gw=1536, fw=768, to=PAIR, order=YX),
    f2b=Box(kind=2, base=FH, step=640, gw=1664, fw=640, to=CROSS, order=XY),
    f3a=Box(kind=3, base=0, step=128, gw=128, fw=128, to=PAIR, order=YX),
    f3b=Box(kind=3, base=256, step=128, gw=128, fw=128, to=CROSS, order=XY))
UNITS, WIDTH = (32, 128, 32, 144), (128, 512, 2 * FH, 512)
B_OUT = dict(mixed=((256, 1024), bf), dtok=((256, 1024), f32), din=((16, 3072), f32), dout=((16, 1024), f32),
    dg=((16, 4608), f32), du=((16, 4608), f32), dd=((72, 1024), f32), ds=((2, 16, 128), f32))
GRADS = [((4, 4, 2, u, n), bf) for u, n in zip(UNITS, WIDTH)]
def flow_scratch(t):
    u, both = UNITS[t.kind], t.gw + t.fw
    n = 2 if t.to == PAIR else 1
    return [((6, u, t.gw), bf), ((n, u, t.gw), bf), ((n, u, both), bf), ((u, both), bf), ((u, both), f32)]
B_SCR = dict(W=((2, FH, 512), bf), gate=((512, FH), bf), up=((512, FH), bf), dffo=((512, 1024), bf), h2=((512, 1024), bf),
    bcx=((512, 1536), bf), ext=((528, 512), f32), resid=((256, 1024), f32), small=((8, 1024), f32),
    tok=((256, 1024), bf), dhs=((256, 1024), f32), dhr=((256, 1024), f32), dho=((256, 1024), f32), dcv=((520, 512), f32),
    gsum=((8, 1024), f32), keep=((256, 1), f32))

def add_into(dst, srcs, rows, step=16):
    def body(i, _):
        r = pl.ds(pl.multiple_of(i * step, step), step)
        t = dst[r, :].astype(f32)
        for q in srcs: t = t + q[r, :].astype(f32)
        dst[r, :] = t.astype(bf)
        return 0
    lax.fori_loop(0, rows // step, body, 0)

class Scatter:
    def __init__(self, w, go, pair, cross, x, y, z, c, other, grads, lands, bufs):
        self.w, self.go, self.x, self.y, self.z, self.c, self.other = w, go, x, y, z, c, other
        self.hi, self.zl = z // 2, z % 2
        self.f = Box()
        for i, (n, t) in enumerate(RFLOWS.items()):
            sel = {PAIR: self.zl, CROSS: self.hi, None: 0}[t.to]
            k = t.kind
            f = Box(vars(t), G=grads[k], L=lands[k], u=UNITS[k], sel=sel, col=t.base + t.step * sel, out=[],
                ecol=t.base + t.gw * sel, pcol=t.base + t.gw * (1 - sel), dev={PAIR: pair, CROSS: cross, None: None}[t.to],
                A={}, s={}, t={}, s2={}, t2={})
            f.M, f.E, f.S, f.R, f.F = bufs[5 * i:5 * i + 5]
            vars(self.f)[n] = f
        self.pair, self.cross = pair, cross
    def cols(self, c, n): return pl.ds(c if isinstance(c, int) else pl.multiple_of(c, 128), n)
    def at(self, f, da, db):
        a, b = f.order
        pos = {X: self.x, Y: self.y}
        pos[a] = (pos[a] + da + 4) % 4
        pos[b] = (pos[b] + db + 4) % 4
        return pos[Y], pos[X]
    def part(self, ref, f, p, u=None):
        if u is None: return ref.at[p[0], p[1], :, :, self.cols(f.col, f.gw)]
        return ref.at[p[0], p[1], u, :, self.cols(f.col, f.gw)]
    def zline(self, ref, f, j, col):
        l = self.at(f, j, 0)
        cs = self.cols(col, f.fw)
        return ref.at[l[0], :, :, :, cs] if f.order[0] == Y else ref.at[:, l[1], :, :, cs]
    def zsend(self, f, j):
        f.A[j] = self.w.send(self.zline(f.G, f, j, f.pcol), self.zline(f.L, f, j, f.ecol), f.dev)
    def first(self, f, j):
        b = f.order[1]
        if f.to:
            f.A[j].wait_recv()
            g, l = self.zline(f.G, f, j, f.ecol), self.zline(f.L, f, j, f.pcol)
            for i in range(4):
                for u in (0, 1): add_into(g.at[i, u], [l.at[i, u]], f.u)
        p = self.at(f, j, 2)
        f.s[j] = self.w.send(self.part(f.G, f, p, 0), self.part(f.L, f, p, 0), self.go[(b, 1)])
        f.t[j] = self.w.send(self.part(f.G, f, p, 1), self.part(f.L, f, p, 1), self.go[(b, -1)])
    def second(self, f, j):
        b, u = f.order[1], f.u
        f.s[j].wait_recv(); p = self.at(f, j, 1)
        add_into(self.part(f.G, f, p, 0), [self.part(f.L, f, p, 0)], u)
        f.s2[j] = self.w.send(self.part(f.G, f, p), self.part(f.L, f, p), self.go[(b, 1)])
        f.t[j].wait_recv(); p = self.at(f, j, -1)
        add_into(self.part(f.G, f, p, 1), [self.part(f.L, f, p, 1)], u)
        f.t2[j] = self.w.send(self.part(f.G, f, p), self.part(f.L, f, self.at(f, j, 1)), self.go[(b, -1)])
    def third(self, f, j):
        a, u, M = f.order[0], f.u, f.M
        f.s2[j].wait_recv(); f.t2[j].wait_recv()
        p = self.at(f, j, 0); o = self.at(f, j, 2)
        for v in (0, 1): add_into(self.part(f.G, f, p, v), [self.part(f.L, f, p, v), self.part(f.L, f, o, v)], u)
        if j == 2:
            f.c = self.w.send(self.part(f.G, f, p, 0), M.at[0], self.go[(a, 1)])
            f.d = self.w.send(self.part(f.G, f, p, 1), M.at[1], self.go[(a, -1)])
        elif j == 1:
            f.c.wait_recv(); add_into(self.part(f.G, f, p, 0), [M.at[0]], u)
            f.c2 = self.w.send(self.part(f.G, f, p), M.at[pl.ds(2, 2)], self.go[(a, 1)])
        elif j == -1:
            f.d.wait_recv(); add_into(self.part(f.G, f, p, 1), [M.at[1]], u)
            f.d2 = self.w.send(self.part(f.G, f, p), M.at[pl.ds(4, 2)], self.go[(a, -1)])
    def last1(self, f):
        u, M, me = f.u, f.M, (self.y, self.x)
        f.c2.wait_recv(); f.d2.wait_recv()
        for v in (0, 1): add_into(self.part(f.G, f, me, v), [M.at[2 + v], M.at[4 + v]], u)
        if f.to == PAIR: f.e = self.w.send(self.part(f.G, f, me), f.E, self.pair)
        else: f.e = self.w.send(self.part(f.G, f, me, 1 - self.hi), f.E.at[0], self.cross)
    def last2(self, f):
        E, S, R = f.E, f.S, f.R
        f.e.wait_recv()
        gw, fw, sel, base = f.gw, f.fw, f.sel, f.base
        ov = gw - fw
        def merge(i, v):
            G = f.G.at[self.y, self.x, v]
            m = self.cols(fw * 0 + (gw * sel if fw else 0), fw) if fw else None
            if fw:
                S[i, :, self.cols(gw * sel, fw)] = G[:, self.cols(base + gw * sel, fw)]
                S[i, :, self.cols(gw * (1 - sel), fw)] = E[i, :, self.cols(ov * (1 - sel), fw)]
            if ov:
                S[i, :, pl.ds(fw, ov)] = (G[:, pl.ds(base + fw, ov)].astype(f32) + E[i, :, self.cols(fw * sel, ov)].astype(f32)).astype(bf)
        if f.to == PAIR:
            merge(0, 0); merge(1, 1)
            f.e2 = self.w.send(S.at[1 - self.hi], R, self.cross)
        else:
            merge(0, self.hi)
            f.e2 = self.w.send(S.at[0], R, self.pair)
    def last3(self, f, targets):
        S, R, F = f.S, f.R, f.F
        f.e2.wait_recv()
        i = self.hi if f.to == PAIR else 0
        F[...] = S[i].astype(f32) + R[...].astype(f32)
        rows = f.u if f.kind == 3 else 32
        half = rows // 2
        m = 8
        for prow, pcol, pw, out, ocol in targets:
            src = lambda q: F.at[pl.ds(pl.multiple_of(prow + half * q, m), half), pl.ds(pcol, pw)]
            dst = out if ocol is None else out.at[:, self.cols(ocol, pw)]
            f.out.append(self.w.send(src(1 - self.c), dst, self.other))
            f.out.append(self.w.local(src(self.c), dst))
    def wait_out(self, f):
        for i, q in enumerate(f.out):
            if i % 2: q.wait()
            else: q.wait_recv()

def backward_kernel(*refs):
    (I, O, r), refs = named([dict(A_GOT, **A_MADE, tokens=0, keep=0), B_OUT, B_SCR], refs)
    grads, lands, bufs, (ss, rs, ls, free) = refs[:4], refs[4:8], refs[8:-4], refs[-4:]
    x, y, z, c = spot()
    hi = z // 2
    k = (y * 4 + x) * 2 + hi
    pair = device(x, y, z + 1 - 2 * (z % 2), c)
    cross = device(x, y, 3 - z, c)
    other = device(x, y, z, 1 - c)
    nxt, prv = along(x, y, z, c, 1), along(x, y, z, c, -1)
    go = {(a, st): moved(x, y, z, c, a, st) for a in XY for st in (1, -1)}
    greet(list(go.values()) + [pair, cross, other, nxt, prv])
    w = Wire(ss, rs, ls)
    sc = Scatter(w, go, pair, cross, x, y, z, c, other, grads, lands, bufs)
    F = sc.f
    own, oth = at_rows(256 * c, 256, 256), at_rows(256 * (1 - c), 256, 256)
    col = lambda p, n: pl.ds(pl.multiple_of(p, 128), n)
    W = r.W
    slot = lambda i: W.at[i // 2, pl.ds(1024 * (i % 2), 1024)]
    rdd = w.send(I.ddown.at[1 - c], grads[3].at[pl.ds(2 * c, 2)], other)
    ldd = w.local(I.ddown.at[c], grads[3].at[pl.ds(2 * c, 2)])
    lw = [w.local(I.wd.at[at_rows(FH * c, FH, FH), :], W.at[c]), w.local(I.wdr.at[at_rows(FH * c, FH, FH), :], W.at[1 - c])]
    ld = Box({n: w.local(vars(I)[n], vars(r)[n]) for n in dict(dffo=0, gate=0, up=0, h2=0, small=0, resid=0, ext=0, bcx=0, keep=0)})
    ld.tok = w.local(I.tokens, r.tok)
    ldd.wait(); rdd.wait_recv()
    for j in JS:
        sc.zsend(F.f3a, j); sc.zsend(F.f3b, j)
    for q in lw: q.wait()
    for q in (ld.dffo, ld.gate, ld.up): q.wait()
    def d_act(n):
        t = nt(r.dffo[:, :512], W[0, n:n + 768, :]) + nt(r.dffo[:, 512:], W[1, n:n + 768, :])
        g, u = r.gate[:, n:n + 768].astype(f32), r.up[:, n:n + 768].astype(f32)
        sg = jax.nn.sigmoid(g)
        r.gate[:, n:n + 768] = (t * u * sg * (1.0 + g * (1.0 - sg))).astype(bf)
        r.up[:, n:n + 768] = (t * (g * sg)).astype(bf)
    for n in range(0, FH, 768): d_act(n)
    P3, P2, P1, P0 = (F.f3a, F.f3b), (F.f2a, F.f2b), (F.f1a, F.f1b), (F.f1s,)
    def do(fn, ns, *a):
        for n in ns: fn(n, *a)
    panels = [[(r.gate, C1 + 512 * p, 512, 512 * p)] for p in range(4)] + [[(r.up, C1 + FH + 512 * p, 512, 512 * p)] for p in range(4)]
    panels += [[(r.gate, C1 + 2048, 256, 2048), (r.up, C1 + FH + 2048, 256, 2048)]]
    def fetch(i):
        out, o = [], 0
        for _, cc, n, _ in panels[i]:
            out.append(w.local(I.wcat.at[:, pl.ds(cc, n)], slot(i % 4).at[:, pl.ds(o, n)])); o += n
        return out
    got = {i: fetch(i) for i in range(4)}
    ld.h2.wait()
    def slab(src, yy, base):
        t = tn(r.h2[:, col(256 * yy, 256)], src[...]).astype(bf)
        for xx in range(4):
            for u in (0, 1): grads[2][yy, xx, u, :, base:base + FH] = t[64 * xx + 32 * u:64 * xx + 32 * u + 32]
    for j in JS:
        slab(r.gate, (y + j + 4) % 4, 0)
        sc.zsend(F.f2a, j)
    do(sc.first, P3, 2)
    def slabs(i, _):
        slab(r.up, i, FH)
        return 0
    lax.fori_loop(0, 4, slabs, 0)
    for j in JS: sc.zsend(F.f2b, j)
    do(sc.first, P3, -1); do(sc.second, P3, 2)
    for i in range(9):
        for q in got[i]: q.wait()
        o = 0
        for nm, _, n, off in panels[i]:
            for rr, acc in ((oth, r.dhs), (own, r.dho)):
                t = nt(nm[rr, off:off + n], slot(i % 4)[:, o:o + n])
                acc[...] = t if i == 0 else acc[...] + t
            o += n
        if i + 4 < 9: got[i + 4] = fetch(i + 4)
        if i == 4: do(sc.first, P3, 1)
    gdh = w.send(r.dhs, r.dhr, other)
    r.h, r.y, r.conv = (r.gate.at[:, pl.ds(o, m)] for o, m in ((0, 1024), (1024, 512), (1536, 512)))
    ld.h, ld.y, ld.conv = w.local(I.h, r.h), w.local(I.y, r.y), w.local(I.conv, r.conv)
    lin = [w.local(I.wcat.at[:, pl.ds(512 * i, 512)], slot(i + 1)) for i in range(3)]
    lo = [w.local(I.wcat.at[at_rows(512 * c, 512, 512), pl.ds(1536, 512)], slot(0).at[at_rows(512 * c, 512, 512)]),
          w.local(I.wor, slot(0).at[at_rows(512 * (1 - c), 512, 512)])]
    do(sc.second, P3, -1); do(sc.third, P3, 2)
    ld.small.wait(); ld.resid.wait()
    r.gsum[...] = jnp.zeros((8, 1024), f32)
    gain = lambda i: r.small[i:i + 1, :]
    gdh.wait_recv()
    def back2(i, _):
        q = at_rows(i * 64, 64, 64); qo = at_rows(256 * c + i * 64, 64, 64)
        rs_ = r.resid[q, :]
        s2 = lax.rsqrt(jnp.mean(rs_ * rs_, axis=1, keepdims=True) + EPS)
        d = r.dho[q, :] + r.dhr[q, :]
        r.gsum[1:2, :] += jnp.sum(d * rs_ * s2, axis=0, keepdims=True)
        wt = d * gain(1)
        inner = jnp.mean(wt * rs_, axis=1, keepdims=True)
        dr = r.dffo[qo, :].astype(f32) + (s2 * wt - rs_ * (s2 * s2 * s2) * inner)
        r.resid[q, :] = dr
        r.h2[qo, :] = dr.astype(bf)
        return 0
    lax.fori_loop(0, 4, back2, 0)
    gdm = w.send(r.h2.at[own], r.h2.at[own], other)
    do(sc.first, P3, 0); do(sc.second, P3, 1); do(sc.third, P3, -1)
    for q in (ld.y, ld.ext, ld.conv, ld.bcx, ld.h, ld.tok, ld.keep): q.wait()
    for q in lo: q.wait()
    gdm.wait_recv()
    d_y = nt(r.h2[:, :512], slot(0)[0:512, :]) + nt(r.h2[:, 512:], slot(0)[512:1024, :])
    cpart = r.bcx[:, 512:1024].astype(f32)
    r.dcv[0:512, :] = d_y * cpart
    r.bcx[:, 512:1024] = (d_y * r.conv[...].astype(f32)).astype(bf)
    ghalo = w.send(r.dcv.at[pl.ds(0, 8)], r.dcv.at[pl.ds(512, 8)], prv)
    def d_out(i, _):
        t = tn(r.y[:, at_rows(256 * i, 256, 256)], r.h2[...]).astype(bf)
        for xx in range(4):
            for u in (0, 1):
                v = t[64 * xx + 32 * u:64 * xx + 32 * u + 32]
                r.up[at_rows(256 * i + 64 * xx + 32 * u, 32, 32), 0:512] = jnp.where(c == 0, v[:, 512:], v[:, :512])
                grads[1][2 * c + i, xx, u, 96:128, :] = jnp.where(c == 0, v[:, :512], v[:, 512:])
        return 0
    lax.fori_loop(0, 2, d_out, 0)
    gdo = [w.send(r.up.at[pl.ds(256 * i + 64 * xx + 32 * u, 32), pl.ds(0, 512)], grads[1].at[2 * c + i, xx, u, pl.ds(96, 32), :], other)
           for i in (0, 1) for xx in range(4) for u in (0, 1)]
    tap = [r.small[2 + i:3 + i, col(512 * c, 512)] for i in range(3)]
    for q in range(0, 512, 128):
        dv = r.dcv[q:q + 128, :]
        for i in range(3):
            r.gsum[2 + i:3 + i, col(512 * c, 512)] += jnp.sum(dv * r.ext[14 + i + q:142 + i + q, :], axis=0, keepdims=True)
    ghalo.wait_recv()
    r.dcv[512:520, :] = r.dcv[512:520, :] * (k < 31).astype(f32)
    for q in range(0, 512, 128):
        dx = tap[2] * r.dcv[q:q + 128, :] + tap[1] * r.dcv[q + 1:q + 129, :] + tap[0] * r.dcv[q + 2:q + 130, :]
        bp, xp = r.bcx[q:q + 128, 0:512].astype(f32), r.bcx[q:q + 128, 1024:1536].astype(f32)
        r.bcx[q:q + 128, 0:512] = (dx * xp).astype(bf)
        r.bcx[q:q + 128, 1024:1536] = (dx * bp).astype(bf)
    def d_in(yy, _):
        t = tn(r.h[:, at_rows(256 * yy, 256, 256)], r.bcx[...]).astype(bf)
        for p in range(3):
            for xx in range(4):
                for u in (0, 1): grads[1][yy, xx, u, 32 * p:32 * p + 32, :] = t[64 * xx + 32 * u:64 * xx + 32 * u + 32, 512 * p:512 * p + 512]
        return 0
    lax.fori_loop(0, 4, d_in, 0)
    for q in gdo: q.wait_recv()
    for j in JS: do(sc.first, P1, j)
    do(sc.second, P3, 0); do(sc.third, P3, 1)
    gdh.wait_send()
    for q in lin: q.wait()
    for rr, acc in ((oth, r.dhs), (own, r.dho)):
        acc[...] = sum(nt(r.bcx[rr, 512 * i:512 * i + 512], slot(i + 1)[...]) for i in range(3))
    gdh = w.send(r.dhs, r.dhr, other)
    la = w.local(I.act, r.gate)
    lw = [w.local(I.wd.at[at_rows(FH * c, FH, FH), :], W.at[c]), w.local(I.wdr.at[at_rows(FH * c, FH, FH), :], W.at[1 - c])]
    do(sc.first, P2, 2); do(sc.third, P3, 0); do(sc.second, P1, 2)
    gdh.wait_recv()
    def back1(i, _):
        q = at_rows(i * 64, 64, 64)
        t = r.tok[q, :].astype(f32)
        s1 = lax.rsqrt(jnp.mean(t * t, axis=1, keepdims=True) + EPS)
        d = r.dho[q, :] + r.dhr[q, :]
        r.gsum[0:1, :] += jnp.sum(d * t * s1, axis=0, keepdims=True)
        wt = d * gain(0)
        inner = jnp.mean(wt * t, axis=1, keepdims=True)
        r.dho[q, :] = r.resid[q, :] + (s1 * wt - t * (s1 * s1 * s1) * inner)
        return 0
    lax.fori_loop(0, 4, back1, 0)
    pl.semaphore_signal(free, inc=1, device_id=other, device_id_type=MESH)
    ltk = w.local(r.dho, O.dtok)
    eye = (lax.broadcasted_iota(jnp.int32, (8, 128), 0) == lax.broadcasted_iota(jnp.int32, (8, 128), 1)).astype(f32).astype(bf)
    sm = tn(r.gsum[...].astype(bf), eye).astype(bf)
    for yy in range(4):
        for xx in range(4):
            for u in (0, 1):
                o = 256 * yy + 64 * xx + 32 * u
                grads[0][yy, xx, u] = sm[o:o + 32]
    for j in JS: do(sc.first, P0, j)
    PS = P1 + P0
    do(sc.second, P1, -1); do(sc.last1, P3)
    do(sc.first, P2, -1); do(sc.second, P2, 2); do(sc.second, P1, 1); do(sc.third, P1, 2)
    for j in JS: do(sc.second, P0, j)
    do(sc.second, P1, 0); do(sc.third, P1, -1); do(sc.last2, P3)
    gdh.wait_send()
    la.wait()
    for q in lw: q.wait()
    ltk.wait()
    for rr, acc in ((oth, r.dhs), (own, r.dho)):
        for h_ in (0, 1): acc[:, 512 * h_:512 * h_ + 512] = dot(r.gate[rr, :], W[h_])
    pl.semaphore_wait(free, 1)
    gdh = w.send(r.dhs, r.dhr, other)
    do(sc.first, P2, 1); do(sc.second, P2, -1); do(sc.third, P2, 2); do(sc.third, P1, 1)
    for j in JS: do(sc.third, P0, j)
    do(sc.third, P1, 0)
    t3 = lambda n: [(0, 0, 256, O.dd, 512 * c + (0 if n is F.f3a else 256))]
    for n in P3: sc.last3(n, t3(n))
    do(sc.first, P2, 0); do(sc.second, P2, 1); do(sc.third, P2, -1); do(sc.last1, PS)
    gdh.wait_recv()
    lres = w.local(I.resid, r.resid)
    lres.wait()
    r.tok[...] = (r.keep[...] * (r.resid[...] + (r.dho[...] + r.dhr[...]))).astype(bf)
    lmx = w.local(r.tok, O.mixed)
    do(sc.second, P2, 0); do(sc.third, P2, 1); do(sc.last2, PS)
    do(sc.third, P2, 0)
    do(sc.last1, P2)
    for n, o in ((F.f1a, 0), (F.f1b, 256)):
        sc.last3(n, [(32 * p, 0, 256, O.din, 1024 * p + 512 * c + o) for p in range(3)] + [(96, 0, 256, O.dout, 512 * c + o)])
    sc.last3(F.f1s, [(0, 0, 128, O.ds.at[c], None)])
    do(sc.last2, P2)
    sc.last3(F.f2a, [(0, 0, FH, O.dg, FH * c)])
    sc.last3(F.f2b, [(0, 0, FH, O.du, FH * c)])
    for f in vars(F).values(): sc.wait_out(f)
    lmx.wait()
    w.drain()

def backward_all(a, tokens, keep):
    a = Box(a)
    a.ddown = a.ddown.reshape(2, 2, 4, 2, 144, 512)
    scr = [*B_SCR.values()] + GRADS + GRADS + [v for t in RFLOWS.values() for v in flow_scratch(t)]
    outs = call(backward_kernel, [*B_OUT.values()], scr, 2, 63, [pltpu.SemaphoreType.REGULAR], *vars(a).values(), tokens, keep)
    return Box(dict(zip(B_OUT, outs)))


def body(tokens, lengths, norm1_gain, in_proj, conv_weight, out_proj, norm2_gain, w_gate, w_up, w_down, cotangent):
    rows = tokens.shape[0]
    place = lax.axis_index("shard")
    slot = lax.axis_index("rep")
    slot_ids = jnp.arange(lengths.shape[0], dtype=jnp.int32)
    length = jnp.sum(jnp.where(slot_ids == slot, lengths, 0))
    valid = jnp.clip(length - place * rows, 0, rows)
    keep = (jnp.arange(rows, dtype=jnp.int32) < valid).astype(jnp.float32)[:, None]
    a = forward_all(tokens, cotangent, keep, in_proj, out_proj, smalls(norm1_gain, norm2_gain, conv_weight), w_gate, w_up, w_down)
    b = backward_all(a, tokens, keep)
    sm = b.ds[0] + b.ds[1]
    return b.mixed, b.dtok, sm[:, 0], b.din, sm[:, 2:5].T, b.dout, sm[:, 1], b.dg, b.du, b.dd

def solution(mesh):
    tok = P(("rep", "shard"), None)
    par = (P("shard"), P("shard", None), P(None, "shard"), P("shard", None), P("shard"), P("shard", None), P("shard", None), P("shard", None))
    return jax.shard_map(body, mesh=mesh, in_specs=(tok, P()) + par + (tok,), out_specs=(tok, tok) + par, check_vma=False)
```

```python
ORDER_A = (
    (0, 0), (0, 1), (0, 2), (0, 3), (1, 0), (1, 1), (2, 0), (4, 0, 0), (2, 1), (4, 1, 0), (3, 0), (4, 0, -1), (4, 0, 1), (4, 1, -1), (5, 0, 0),
    (3, 1), (4, 1, 1), (4, 0, 2), (1, 2), (1, 3), (5, 1, 0), (5, 0, -1), (5, 0, 1), (5, 1, -1), (5, 0, 2), (4, 1, 2), (5, 1, 1), (2, 2), (4, 2, 0),
    (4, 3, 0), (2, 3), (3, 2), (5, 1, 2), (5, 3, 0), (4, 2, -1), (4, 3, -1), (4, 2, 1), (0,), (4, 3, 1), (5, 2, 0), (1,), (3, 3), (2,), (5, 3, -1),
    (3,), (5, 3, 1), (4, 2, 2), (5, 2, -1), (0, 4), (0, 5), (1, 4), (1, 5), (4,), (4, 3, 2), (5,), (5, 2, 1), (6,), (5, 2, 2), (7,), (4, 4, 0),
    (2, 5), (2, 4), (4, 5, 0), (5, 3, 2), (5, 4, 0), (3, 5), (4, 5, -1), (4, 4, -1), (4, 5, 1), (8,), (3, 4), (9,), (4, 4, 1), (5, 4, -1), (5, 5, 0),
    (10,), (4, 4, 2), (4, 5, 2), (5, 5, -1), (11,), (5, 4, 1), (5, 5, 1), (12,), (5, 4, 2), (5, 5, 2), (13,), (14,),)
ORDER_B = (
    (0, 5, 2), (0, 5, -1), (0, 5, 1), (0, 5, 0), (0, 6, 2), (0, 6, -1), (0, 6, 1), (0, 6, 0), (0,), (1,), (1, 5, 2), (1, 5, -1), (1, 6, 2),
    (1, 6, -1), (2,), (1, 5, 1), (1, 5, 0), (1, 6, 1), (1, 6, 0), (3,), (4,), (2, 5, 2), (2, 6, 2), (5,), (6,), (7,), (8,), (9,), (10,), (11,), (12,),
    (13,), (14,), (15,), (16,), (2, 5, 0), (2, 6, 0), (0, 3, 2), (17,), (2, 5, -1), (2, 5, 1), (0, 4, 2), (2, 6, -1), (2, 6, 1), (18,), (19,),
    (1, 3, 2), (0, 4, -1), (3, 5), (20,), (0, 3, -1), (3, 6), (1, 4, 2), (0, 4, 1), (21,), (1, 4, -1), (2, 3, 2), (22,), (23,), (1, 3, -1), (0, 4, 0),
    (4, 5), (0, 3, 1), (24,), (2, 4, 2), (4, 6), (25,), (26,), (1, 4, 1), (27,), (28,), (29,), (1, 3, 1), (0, 3, 0), (5, 5), (2, 4, -1), (30,),
    (2, 3, -1), (0, 2, 2), (0, 2, -1), (0, 2, 1), (0, 2, 0), (5, 6), (0, 1, 2), (1, 4, 0), (31,), (2, 3, 1), (1, 3, 0), (0, 0, 2), (0, 1, -1),
    (2, 4, 1), (32,), (1, 1, 2), (0, 1, 1), (0, 0, -1), (1, 2, 2), (1, 2, -1), (1, 2, 1), (1, 2, 0), (2, 3, 0), (1, 1, -1), (0, 1, 0), (0, 0, 1),
    (3, 3), (2, 4, 0), (1, 0, 2), (3, 4), (1, 0, -1), (2, 2, 2), (2, 1, 2), (2, 2, 0), (1, 1, 1), (1, 0, 1), (2, 2, -1), (0, 0, 0), (4, 3), (2, 2, 1),
    (2, 0, 2), (1, 1, 0), (2, 1, 1), (2, 1, -1), (4, 4), (3, 2), (2, 0, -1), (2, 0, 1), (1, 0, 0), (5, 3), (2, 1, 0), (4, 2), (3, 1), (2, 0, 0),
    (3, 0), (5, 4), (5, 2), (4, 1), (4, 0), (5, 1), (5, 0),)

import functools
import jax, jax.numpy as jnp
from jax import lax
from jax.experimental import pallas as pl
from jax.experimental.pallas import tpu as pltpu
from jax.sharding import PartitionSpec as P
MESH = pl.DeviceIdType.MESH
EPS = 1e-05
bf, f32 = jnp.bfloat16, jnp.float32
C1 = 2176; HALF = 1152; CAT = 6784; UNIT = 32; DUNIT = 144; FH = 2304
COPIES = 272
JS = (2, -1, 1, 0)
PAIR, CROSS, X, Y = 1, 2, 0, 1
ONE, TWO, THREE = 1, 2, 3
XY, YX = (X, Y), (Y, X)
class Box:
    def __init__(self, *a, **kw):
        for d in a: self.__dict__.update(d)
        self.__dict__.update(kw)

FLOWS = dict(
    f1a=Box(kind=1, base=0, step=512, gw=512, fw=512, to=PAIR, order=XY),
    f1b=Box(kind=1, base=1024, step=384, gw=768, fw=384, to=CROSS, order=YX),
    f2a=Box(kind=2, base=C1, step=768, gw=1536, fw=768, to=PAIR, order=YX),
    f2b=Box(kind=2, base=C1 + FH, step=640, gw=1664, fw=640, to=CROSS, order=XY),
    f3a=Box(kind=3, base=0, step=0, gw=256, fw=0, to=None, order=XY),
    f3b=Box(kind=3, base=256, step=0, gw=256, fw=0, to=None, order=YX))

def spot():
    rep = lax.axis_index("rep"); s = lax.axis_index("shard")
    return (s // 4) % 4, s // 16, ((s // 2) % 2) * 2 + rep, s % 2

def device(x, y, z, c):
    return (z % 2, ((y * 4 + x) * 2 + z // 2) * 2 + c)

def moved(x, y, z, c, axis, step):
    if axis == X: return device((x + step + 4) % 4, y, z, c)
    return device(x, (y + step + 4) % 4, z, c)

def along(x, y, z, c, step):
    k = ((y * 4 + x) * 2 + z // 2 + step + 32) % 32
    return device((k // 2) % 4, k // 8, (k % 2) * 2 + z % 2, c)

def greet(devices):
    bar = pltpu.get_barrier_semaphore()
    for d in devices:
        pl.semaphore_signal(bar, inc=1, device_id=d, device_id_type=MESH)
    pl.semaphore_wait(bar, len(devices))

class Copy:
    def __init__(self, cp): self.cp, self.here, self.gone = cp, False, False
    def wait_recv(self): self.cp.wait_recv(); self.here = True
    def wait_send(self): self.cp.wait_send(); self.gone = True

class Near:
    def __init__(self, cp): self.cp, self.here = cp, False
    def wait(self): self.cp.wait(); self.here = True

class Wire:
    def __init__(self, ss, rs, ls): self.ss, self.rs, self.ls, self.sent, self.near = ss, rs, ls, [], []
    def send(self, src, dst, dev):
        i = len(self.sent)
        cp = pltpu.make_async_remote_copy(src_ref=src, dst_ref=dst, send_sem=self.ss.at[i], recv_sem=self.rs.at[i], device_id=dev, device_id_type=MESH)
        cp.start(); self.sent.append(Copy(cp)); return self.sent[-1]
    def local(self, src, dst):
        cp = pltpu.make_async_copy(src, dst, self.ls.at[len(self.near)])
        cp.start(); self.near.append(Near(cp)); return self.near[-1]
    def drain(self):
        for cp in self.near:
            if not cp.here: cp.wait()
        for cp in self.sent:
            if not cp.here: cp.wait_recv()
            if not cp.gone: cp.wait_send()

def at_rows(v, n, m=16): return pl.ds(pl.multiple_of(v, m), n)

class All:
    def __init__(self, *q): self.q = q
    def wait_recv(self):
        for q in self.q: q.wait_recv()

class Gather:
    def __init__(self, w, go, pair, cross, other, x, y, z, wcat, wd, wdr):
        self.w, self.go, self.x, self.y, self.other, self.wdr, self.hi = w, go, x, y, other, wdr, z // 2
        self.f = Box()
        for n, t in FLOWS.items():
            sel = {PAIR: z % 2, CROSS: z // 2, None: 0}[t.to]
            d = t.kind == 3
            vars(self.f)[n] = Box(vars(t), buf=wd if d else wcat, unit=DUNIT if d else UNIT, mine=(t.base + t.step * sel, t.gw),
                alone=(t.base + t.gw * sel, t.fw), dev={PAIR: pair, CROSS: cross, None: None}[t.to], z=[], p={}, m={}, p2={}, m2={})
    def block(self, f, da, db, unit=None, cols=None, buf=None):
        a, b = f.order
        pos = {X: self.x, Y: self.y}
        pos[a] = (pos[a] + da + 4) % 4
        pos[b] = (pos[b] + db + 4) % 4
        u = f.unit
        row = (pos[Y] * 4 + pos[X]) * (2 * u)
        n = 2 * u
        if unit is not None: row, n = row + unit * u, u
        col, width = cols or f.mine
        return (f.buf if buf is None else buf).at[at_rows(row, n), pl.ds(col if isinstance(col, int) else pl.multiple_of(col, 128), width)]
    def push(self, f, da, db, dev, unit=None):
        v = self.block(f, da, db, unit)
        return self.w.send(v, v, dev)
    def fwd(self, f, da, db):
        if f.dev is not None and (da or db):
            v = self.block(f, da, db, None, f.alone)
            f.z.append(self.w.send(v, v, f.dev))
        if f.kind == 3: f.z.append(self.w.send(self.block(f, da, db), self.block(f, da, db, None, None, self.wdr), self.other))
    def open2(self, f, j):
        b = f.order[1]
        f.p[j] = self.push(f, j, 0, self.go[(b, 1)])
        f.m[j] = self.push(f, j, 0, self.go[(b, -1)])
    def r1(self, f, own):
        a, b = f.order
        u = self.hi if own else 1 - self.hi
        new = [self.push(f, 0, 0, self.go[(d, st)], u) for d in (a, b) for st in (1, -1)]
        if own: f.half = new
        else:
            f.p[None], f.m[None], f.p[0], f.m[0] = (All(*q) for q in zip(f.half, new))
            self.fwd(f, 0, 0)
    def r2(self, f):
        a = f.order[0]
        f.p[None].wait_recv(); f.p2[None] = self.push(f, -1, 0, self.go[(a, 1)], 0)
        f.m[None].wait_recv(); f.m2[None] = self.push(f, 1, 0, self.go[(a, -1)], 1)
        self.open2(f, -1); self.open2(f, 1)
        self.fwd(f, -1, 0); self.fwd(f, 1, 0)
    def r3(self, f):
        f.p2[None].wait_recv(); f.m2[None].wait_recv()
        self.open2(f, 2); self.fwd(f, 2, 0)
    def r4(self, f, j):
        b = f.order[1]
        f.p[j].wait_recv(); f.p2[j] = self.push(f, j, -1, self.go[(b, 1)], 0)
        f.m[j].wait_recv(); f.m2[j] = self.push(f, j, 1, self.go[(b, -1)], 1)
        self.fwd(f, j, -1); self.fwd(f, j, 1)
    def r5(self, f, j):
        f.p2[j].wait_recv(); f.m2[j].wait_recv()
        self.fwd(f, j, 2)
    def all_here(self, f):
        for q in f.z: q.wait_recv()

def dot(a, b): return jnp.dot(a, b, preferred_element_type=f32)
def tn(a, b): return lax.dot_general(a, b, (((0,), (0,)), ((), ())), preferred_element_type=f32)
def nt(a, b): return lax.dot_general(a, b, (((1,), (1,)), ((), ())), preferred_element_type=f32)

A_GOT = dict(wcat=((1024, CAT), bf), wd=((4608, 512), bf), wor=((512, 512), bf), wdr=((4608, 512), bf), ddown=((4608, 512), bf))
A_MADE = dict(h=((512, 1024), bf), bcx=((512, 1536), bf), ext=((528, 512), f32), conv=((512, 512), bf), y=((512, 512), bf),
    resid=((256, 1024), f32), h2=((512, 1024), bf), gate=((512, FH), bf), up=((512, FH), bf), act=((512, FH), bf),
    dffo=((512, 1024), bf), small=((8, 1024), f32))
A_SCR = dict(T=((512, 1024), bf), cotv=((256, 1024), bf), win=((1024, 1536), bf), wo=((512, 1024), bf), wsm=((1024, 128), bf),
    wg=((1024, FH), bf), wu=((1024, FH), bf), cpart=((512, 512), f32), mixs=((256, 1024), f32), mixr=((256, 1024), f32),
    dnf=((DUNIT, 512), f32), dns=((72, 512), f32), dnb=((DUNIT, 512), bf), ddn=((2, FH, 512), bf),
    inp=((16, 3072), bf), outp=((16, 1024), bf), sml=((16, 128), bf), wgs=((16, 4608), bf), wus=((16, 4608), bf), wds=((72, 1024), bf), keepv=((256, 1), f32))

def named(groups, refs):
    refs, out = list(refs), []
    for g in groups:
        out.append(Box(dict(zip(g, refs)))); refs = refs[len(g):]
    return out, refs

def forward_kernel(*refs):
    A_IN = dict(tokens=0, cot=0, keep=0, inp=0, outp=0, sml=0, wgs=0, wus=0, wds=0)
    (I, O, M, V, S), (ss, rs, ls) = named([A_IN, A_GOT, A_MADE, A_MADE, A_SCR], refs)
    wcat, wd, wor, wdr = O.wcat, O.wd, O.wor, O.wdr
    x, y, z, c = spot()
    hi = z // 2
    s = ((y * 4 + x) * 2 + hi) * 2 + c
    k = s // 2
    pair = device(x, y, z + 1 - 2 * (z % 2), c)
    cross = device(x, y, 3 - z, c)
    other = device(x, y, z, 1 - c)
    nxt, prv = along(x, y, z, c, 1), along(x, y, z, c, -1)
    go = {(a, st): moved(x, y, z, c, a, st) for a in XY for st in (1, -1)}
    w = Wire(ss, rs, ls)
    own, oth = at_rows(256 * c, 256, 256), at_rows(256 * (1 - c), 256, 256)
    col = lambda p, n: pl.ds(pl.multiple_of(p, 128), n)
    lds = w.local(I.wds, S.wds)
    lin = [w.local(a, b) for a, b in ((I.sml, S.sml), (I.inp, S.inp), (I.outp, S.outp), (I.wgs, S.wgs), (I.wus, S.wus))]
    lcot = [w.local(I.cot, S.cotv), w.local(I.keep, S.keepv)]
    ltok = w.local(I.tokens, S.T.at[own])
    greet(list(go.values()) + [pair, cross, other, nxt, prv])
    rows = at_rows(16 * s, 16)
    pieces = [(I.inp, S.inp, 1024 * i, 512, 512 * i) for i in range(3)] + [(I.outp, S.outp, 0, 512, 1536), (I.wgs, S.wgs, 0, FH, C1), (I.wus, S.wus, 0, FH, C1 + FH)]
    got = [w.send(I.sml, wcat.at[rows, pl.ds(2048, 128)], other)]
    for src, _, a, n, d in pieces: got.append(w.send(src.at[:, col(a + n * (1 - c), n)], wcat.at[rows, pl.ds(d, n)], other))
    for q in lin: q.wait()
    mine = [w.local(S.sml, wcat.at[rows, pl.ds(2048, 128)])]
    for _, src, a, n, d in pieces: mine.append(w.local(src.at[:, col(a + n * c, n)], wcat.at[rows, pl.ds(d, n)]))
    lds.wait()
    S.dns[...] = S.wds[:, col(512 * (1 - c), 512)].astype(f32)
    gdn = w.send(S.dns, S.dnf.at[at_rows(72 * c, 72, 8)], other)
    S.dnf[at_rows(72 * c, 72, 8), :] = S.wds[:, col(512 * c, 512)].astype(f32)
    gtok = w.send(I.tokens, S.T.at[own], other)
    g = Gather(w, go, pair, cross, other, x, y, z, wcat, wd, wdr)
    F = g.f
    for q in mine: q.wait()
    for q in got: q.wait_recv()
    urow, drow = at_rows(UNIT * k, UNIT, UNIT), at_rows(DUNIT * k, DUNIT)
    z1 = w.send(wcat.at[urow, pl.ds(0, C1)], wcat.at[urow, pl.ds(0, C1)], cross)
    z2 = w.send(wcat.at[urow, pl.ds(C1, CAT - C1)], wcat.at[urow, pl.ds(C1, CAT - C1)], cross)
    gdn.wait_recv()
    S.dnb[...] = S.dnf[...].astype(bf)
    z3 = w.send(S.dnb, wd.at[drow, :], cross)
    lwd = w.local(S.dnb, wd.at[drow, :])
    for q in lcot: q.wait()
    V.dffo[own, :] = (S.keepv[...] * S.cotv[...].astype(f32)).astype(bf)
    gdf = w.send(V.dffo.at[own], V.dffo.at[own], other)
    ltok.wait(); gtok.wait_recv(); lwd.wait()
    t = Box()
    def save(**kw):
        for n in kw: w.local(vars(V)[n], vars(M)[n])
    def one():
        for f in (F.f1a, F.f1b): g.all_here(f)
        l1 = w.local(wcat.at[:, pl.ds(2048, 128)], S.wsm)
        t.win = w.local(wcat.at[:, pl.ds(0, 1536)], S.win)
        t.wor = w.send(wcat.at[at_rows(512 * (1 - c), 512, 512), pl.ds(1536, 512)], wor, other)
        t.wo = w.local(wcat.at[at_rows(512 * c, 512, 512), pl.ds(1536, 512)], S.wo.at[:, col(512 * c, 512)])
        l1.wait()
        eye = (lax.broadcasted_iota(jnp.int32, (8, 128), 0) == lax.broadcasted_iota(jnp.int32, (8, 128), 1)).astype(f32).astype(bf)
        V.small[...] = nt(eye, S.wsm[...])
    def norm1():
        def rows(i, _):
            q = at_rows(i * 64, 64, 64)
            v = S.T[q, :].astype(f32)
            sc = lax.rsqrt(jnp.mean(v * v, axis=1, keepdims=True) + EPS)
            V.h[q, :] = (v * sc * V.small[0:1, :]).astype(bf)
            return 0
        lax.fori_loop(0, 8, rows, 0)
        t.win.wait()
    ext = V.ext
    def b_x():
        for n in (0, 256):
            b_ = dot(V.h[...], S.win[:, n:n + 256])
            x_ = dot(V.h[...], S.win[:, 1024 + n:1280 + n])
            V.bcx[:, n:n + 256] = b_.astype(bf)
            V.bcx[:, 1024 + n:1280 + n] = x_.astype(bf)
            ext[16:528, n:n + 256] = (b_ * x_).astype(bf).astype(f32)
        t.halo = w.send(ext.at[pl.ds(520, 8)], ext.at[pl.ds(8, 8)], nxt)
        t.wor.wait_recv()
        t.wo2 = w.local(wor, S.wo.at[:, col(512 * (1 - c), 512)])
    def c_():
        for n in (0, 256):
            v = dot(V.h[...], S.win[:, 512 + n:768 + n])
            S.cpart[:, n:n + 256] = v
            V.bcx[:, 512 + n:768 + n] = v.astype(bf)
        save(h=1, bcx=1, small=1)
    def conv():
        t.halo.wait_recv()
        ext[8:16, :] = ext[8:16, :] * (k > 0).astype(f32)
        t0, t1, t2 = (V.small[2 + i:3 + i, col(512 * c, 512)] for i in range(3))
        for q in range(0, 512, 128):
            cv = t0 * ext[14 + q:142 + q, :] + t1 * ext[15 + q:143 + q, :] + t2 * ext[16 + q:144 + q, :]
            V.conv[q:q + 128, :] = cv.astype(bf)
            V.y[q:q + 128, :] = (S.cpart[q:q + 128, :] * cv).astype(bf)
        t.wo.wait(); t.wo2.wait()
    def mix():
        S.mixs[...] = dot(V.y[oth, :], S.wo[...])
        t.mix = w.send(S.mixs, S.mixr, other)
    def mix2():
        V.resid[...] = dot(V.y[own, :], S.wo[...])
        save(ext=1, conv=1, y=1)
    def norm2():
        t.mix.wait_recv()
        def rows(i, _):
            q, qo = at_rows(i * 64, 64, 64), at_rows(256 * c + i * 64, 64, 64)
            v = S.T[qo, :].astype(f32) + (V.resid[q, :] + S.mixr[q, :])
            V.resid[q, :] = v
            sc = lax.rsqrt(jnp.mean(v * v, axis=1, keepdims=True) + EPS)
            V.h2[qo, :] = (v * sc * V.small[1:2, :]).astype(bf)
            return 0
        lax.fori_loop(0, 4, rows, 0)
        t.h2 = w.send(V.h2.at[own], V.h2.at[own], other)
        save(resid=1)
    def two():
        for f in (F.f2a, F.f2b): g.all_here(f)
        t.wg = [(w.local(wcat.at[:, pl.ds(C1 + n, 768)], S.wg.at[:, pl.ds(n, 768)]), w.local(wcat.at[:, pl.ds(C1 + FH + n, 768)], S.wu.at[:, pl.ds(n, 768)]))
            for n in (0, 768, 1536)]
        t.h2.wait_recv(); gdf.wait_recv()
        save(h2=1, dffo=1)
    def gate_up(i):
        for q in t.wg[i]: q.wait()
        n = 768 * i
        g_ = dot(V.h2[...], S.wg[:, n:n + 768])
        u_ = dot(V.h2[...], S.wu[:, n:n + 768])
        V.gate[:, n:n + 768] = g_.astype(bf)
        V.up[:, n:n + 768] = u_.astype(bf)
        V.act[:, n:n + 768] = (g_ * jax.nn.sigmoid(g_) * u_).astype(bf)
        if i == 2: save(gate=1, up=1, act=1)
    def down(i):
        def rows(m, _):
            q = at_rows(768 * i + m * 256, 256, 256)
            v = tn(V.act[:, q], V.dffo[...]).astype(bf)
            S.ddn[0, q, :] = v[:, :512]
            S.ddn[1, q, :] = v[:, 512:]
            return 0
        lax.fori_loop(0, 3, rows, 0)
        to = at_rows(FH * c + 768 * i, 768, 256)
        w.send(S.ddn.at[1 - c, pl.ds(768 * i, 768)], O.ddown.at[to, :], other)
        w.local(S.ddn.at[c, pl.ds(768 * i, 768)], O.ddown.at[to, :])
    each = functools.partial
    chunks = [one, norm1, b_x, c_, conv, mix, mix2, norm2, two] + [each(gate_up, i) for i in range(3)] + [each(down, i) for i in range(3)]
    flows = list(vars(F).values())
    moves = (g.r1, g.r1, g.r2, g.r3, g.r4, g.r5)
    need = {0: z1, 2: z2, 4: z3}
    for what, *where in ORDER_A:
        if not where: chunks[what](); continue
        f = flows[where[0]]
        if what == 1:
            q = need.pop(where[0] // 2 * 2, None)
            if q is not None: q.wait_recv()
        if what < 2: g.r1(f, what == 0)
        else: moves[what](f, *where[1:])
    w.drain()

def call(kernel, outs, scratch, ident, limit, extra, *args):
    hbm = pl.BlockSpec(memory_space=pl.ANY)
    return pl.pallas_call(
        kernel, out_shape=tuple(jax.ShapeDtypeStruct(*v) for v in outs), in_specs=[hbm] * len(args), out_specs=(hbm,) * len(outs),
        scratch_shapes=[pltpu.VMEM(*v) for v in scratch] + [pltpu.SemaphoreType.DMA((n,)) for n in (COPIES, COPIES, 96)] + extra,
        compiler_params=pltpu.CompilerParams(collective_id=ident, has_side_effects=True, vmem_limit_bytes=limit * 2**20))(*args)

def forward_all(*args):
    outs = call(forward_kernel, [*A_GOT.values(), *A_MADE.values()], [*A_MADE.values(), *A_SCR.values()], 1, 60, [], *args)
    return dict(zip([*A_GOT, *A_MADE], outs))

def smalls(norm1_gain, norm2_gain, conv_weight):
    small = jnp.concatenate([norm1_gain[:, None], norm2_gain[:, None], conv_weight.T], axis=1)
    return jnp.pad(small, ((0, 0), (0, 123)))


RFLOWS = dict(
    f1a=Box(kind=1, base=0, step=128, gw=128, fw=128, to=PAIR, order=XY),
    f1b=Box(kind=1, base=256, step=128, gw=128, fw=128, to=CROSS, order=YX),
    f1s=Box(kind=0, base=0, step=0, gw=128, fw=0, to=None, order=XY),
    f2a=Box(kind=2, base=0, step=768, gw=1536, fw=768, to=PAIR, order=YX),
    f2b=Box(kind=2, base=FH, step=384, gw=1920, fw=384, to=CROSS, order=XY),
    f3a=Box(kind=3, base=0, step=0, gw=256, fw=0, to=None, order=YX),
    f3b=Box(kind=3, base=256, step=0, gw=256, fw=0, to=None, order=XY))
UNITS, WIDTH = (32, 128, 32, 144), (128, 512, 2 * FH, 512)
B_OUT = dict(mixed=((256, 1024), bf), dtok=((256, 1024), f32), din=((16, 3072), f32), dout=((16, 1024), f32),
    dg=((16, 4608), f32), du=((16, 4608), f32), dd=((72, 1024), f32), ds=((2, 16, 128), f32))
GRADS = [((4, 4, 2, u, n), bf) for u, n in zip(UNITS, WIDTH)]
def flow_scratch(t):
    u, both = UNITS[t.kind], t.gw + t.fw
    n = t.gw if t.to == PAIR else both
    return [((6, u, t.gw), bf), ((u, t.gw), bf), ((u, n), bf), ((u, n), bf), ((u, both), f32)]
B_SCR = dict(W=((2, FH, 512), bf), gate=((512, FH), bf), up=((512, FH), bf), dffo=((512, 1024), bf), h2=((512, 1024), bf),
    bcx=((512, 1536), bf), ext=((528, 512), f32), resid=((256, 1024), f32), small=((8, 1024), f32),
    tok=((256, 1024), bf), dhs=((256, 1024), f32), dhr=((256, 1024), f32), dho=((256, 1024), f32), dcv=((520, 512), f32),
    gsum=((8, 1024), f32), keep=((256, 1), f32))

def add_into(dst, srcs, rows, step=16):
    def body(i, _):
        r = pl.ds(pl.multiple_of(i * step, step), step)
        t = dst[r, :].astype(f32)
        for q in srcs: t = t + q[r, :].astype(f32)
        dst[r, :] = t.astype(bf)
        return 0
    lax.fori_loop(0, rows // step, body, 0)

class Scatter:
    def __init__(self, w, go, pair, cross, x, y, z, c, other, grads, lands, bufs):
        self.w, self.go, self.x, self.y, self.z, self.c, self.other = w, go, x, y, z, c, other
        self.hi, self.zl = z // 2, z % 2
        self.f = Box()
        for i, (n, t) in enumerate(RFLOWS.items()):
            sel = {PAIR: (self.zl + self.hi) % 2, CROSS: self.hi, None: 0}[t.to]
            k = t.kind
            f = Box(vars(t), G=grads[k], L=lands[k], u=UNITS[k], sel=sel, col=t.base + t.step * sel, out=[],
                ecol=t.base + t.gw * sel, pcol=t.base + t.gw * (1 - sel), dev={PAIR: pair, CROSS: cross, None: None}[t.to],
                A={}, s={}, t={}, s2={}, t2={})
            f.M, f.E, f.S, f.R, f.F = bufs[5 * i:5 * i + 5]
            vars(self.f)[n] = f
        self.pair, self.cross = pair, cross
    def cols(self, c, n): return pl.ds(c if isinstance(c, int) else pl.multiple_of(c, 128), n)
    def at(self, f, da, db):
        a, b = f.order
        pos = {X: self.x, Y: self.y}
        pos[a] = (pos[a] + da + 4) % 4
        pos[b] = (pos[b] + db + 4) % 4
        return pos[Y], pos[X]
    def part(self, ref, f, p, u=None):
        if u is None: return ref.at[p[0], p[1], :, :, self.cols(f.col, f.gw)]
        return ref.at[p[0], p[1], u, :, self.cols(f.col, f.gw)]
    def zline(self, ref, f, j, col):
        l = self.at(f, j, 0)
        cs = self.cols(col, f.fw)
        return ref.at[l[0], :, :, :, cs] if f.order[0] == Y else ref.at[:, l[1], :, :, cs]
    def zsend(self, f, j):
        f.A[j] = self.w.send(self.zline(f.G, f, j, f.pcol), self.zline(f.L, f, j, f.ecol), f.dev)
    def first(self, f, j):
        b = f.order[1]
        if f.to:
            f.A[j].wait_recv()
            g, l = self.zline(f.G, f, j, f.ecol), self.zline(f.L, f, j, f.pcol)
            for i in range(4):
                for u in (0, 1): add_into(g.at[i, u], [l.at[i, u]], f.u)
        p = self.at(f, j, 2)
        f.s[j] = self.w.send(self.part(f.G, f, p, 0), self.part(f.L, f, p, 0), self.go[(b, 1)])
        f.t[j] = self.w.send(self.part(f.G, f, p, 1), self.part(f.L, f, p, 1), self.go[(b, -1)])
    def second(self, f, j):
        b, u = f.order[1], f.u
        f.s[j].wait_recv(); p = self.at(f, j, 1)
        add_into(self.part(f.G, f, p, 0), [self.part(f.L, f, p, 0)], u)
        f.s2[j] = self.w.send(self.part(f.G, f, p), self.part(f.L, f, p), self.go[(b, 1)])
        f.t[j].wait_recv(); p = self.at(f, j, -1)
        add_into(self.part(f.G, f, p, 1), [self.part(f.L, f, p, 1)], u)
        f.t2[j] = self.w.send(self.part(f.G, f, p), self.part(f.L, f, self.at(f, j, 1)), self.go[(b, -1)])
    def third(self, f, j):
        a, u, M = f.order[0], f.u, f.M
        f.s2[j].wait_recv(); f.t2[j].wait_recv()
        p = self.at(f, j, 0); o = self.at(f, j, 2)
        for v in (0, 1): add_into(self.part(f.G, f, p, v), [self.part(f.L, f, p, v), self.part(f.L, f, o, v)], u)
        if j == 2:
            f.c = self.w.send(self.part(f.G, f, p, 0), M.at[0], self.go[(a, 1)])
            f.d = self.w.send(self.part(f.G, f, p, 1), M.at[1], self.go[(a, -1)])
        elif j == 1:
            f.c.wait_recv(); add_into(self.part(f.G, f, p, 0), [M.at[0]], u)
            f.c2 = self.w.send(self.part(f.G, f, p), M.at[pl.ds(2, 2)], self.go[(a, 1)])
        elif j == -1:
            f.d.wait_recv(); add_into(self.part(f.G, f, p, 1), [M.at[1]], u)
            f.d2 = self.w.send(self.part(f.G, f, p), M.at[pl.ds(4, 2)], self.go[(a, -1)])
    def last1(self, f):
        u, M, me = f.u, f.M, (self.y, self.x)
        f.c2.wait_recv(); f.d2.wait_recv()
        for v in (0, 1): add_into(self.part(f.G, f, me, v), [M.at[2 + v], M.at[4 + v]], u)
        f.e = self.w.send(self.part(f.G, f, me, 1 - self.hi), f.E, self.cross)
    def last2(self, f):
        f.e.wait_recv()
        E, S, gw, fw, sel = f.E, f.S, f.gw, f.fw, f.sel
        ov = gw - fw
        G = f.G.at[self.y, self.x, self.hi]
        if f.to == PAIR:
            S[...] = (G[:, self.cols(f.col, gw)].astype(f32) + E[...].astype(f32)).astype(bf)
        else:
            if fw:
                S[:, self.cols(gw * sel, fw)] = G[:, self.cols(f.base + gw * sel, fw)]
                S[:, self.cols(gw * (1 - sel), fw)] = E[:, self.cols(ov * (1 - sel), fw)]
            if ov:
                S[:, pl.ds(fw, ov)] = (G[:, pl.ds(f.base + fw, ov)].astype(f32) + E[:, self.cols(fw * sel, ov)].astype(f32)).astype(bf)
        f.e2 = self.w.send(S, f.R, self.pair)
    def last3(self, f, targets):
        S, R, F, gw, fw, sel = f.S, f.R, f.F, f.gw, f.fw, f.sel
        ov = gw - fw
        f.e2.wait_recv()
        if f.to == PAIR:
            F[:, self.cols(gw * sel, fw)] = S[:, self.cols(ov * sel, fw)].astype(f32)
            F[:, self.cols(gw * (1 - sel), fw)] = R[:, self.cols(ov * (1 - sel), fw)].astype(f32)
            if ov: F[:, pl.ds(fw, ov)] = S[:, self.cols(fw * (1 - sel), ov)].astype(f32) + R[:, self.cols(fw * sel, ov)].astype(f32)
        else: F[...] = S[...].astype(f32) + R[...].astype(f32)
        rows = f.u if f.kind == 3 else 32
        half = rows // 2
        m = 8
        for prow, pcol, pw, out, ocol in targets:
            src = lambda q: F.at[pl.ds(pl.multiple_of(prow + half * q, m), half), pl.ds(pcol, pw)]
            dst = out if ocol is None else out.at[:, self.cols(ocol, pw)]
            f.out.append(self.w.send(src(1 - self.c), dst, self.other))
            f.out.append(self.w.local(src(self.c), dst))
    def wait_out(self, f):
        for i, q in enumerate(f.out):
            if i % 2: q.wait()
            else: q.wait_recv()

def backward_kernel(*refs):
    (I, O, r), refs = named([dict(A_GOT, **A_MADE, tokens=0, keep=0), B_OUT, B_SCR], refs)
    grads, lands, bufs, (ss, rs, ls, free) = refs[:4], refs[4:8], refs[8:-4], refs[-4:]
    x, y, z, c = spot()
    hi = z // 2
    k = (y * 4 + x) * 2 + hi
    pair = device(x, y, z + 1 - 2 * (z % 2), c)
    cross = device(x, y, 3 - z, c)
    other = device(x, y, z, 1 - c)
    nxt, prv = along(x, y, z, c, 1), along(x, y, z, c, -1)
    go = {(a, st): moved(x, y, z, c, a, st) for a in XY for st in (1, -1)}
    w = Wire(ss, rs, ls)
    own, oth = at_rows(256 * c, 256, 256), at_rows(256 * (1 - c), 256, 256)
    col = lambda p, n: pl.ds(pl.multiple_of(p, 128), n)
    W = r.W
    slot = lambda i: W.at[i // 2, pl.ds(1024 * (i % 2), 1024)]
    def w_down():
        return [w.local(I.wd.at[at_rows(FH * c, FH, FH), :], W.at[c]), w.local(I.wdr.at[at_rows(FH * c, FH, FH), :], W.at[1 - c])]
    lgd = w.local(I.ddown, grads[3])
    lwd = w_down()
    ld = Box({n: w.local(vars(I)[n], vars(r)[n]) for n in dict(dffo=0, gate=0, up=0, h2=0, small=0, resid=0, ext=0, bcx=0, keep=0)})
    ld.tok = w.local(I.tokens, r.tok)
    greet(list(go.values()) + [pair, cross, other, nxt, prv])
    sc = Scatter(w, go, pair, cross, x, y, z, c, other, grads, lands, bufs)
    F = sc.f
    lgd.wait()
    r.gsum[...] = jnp.zeros((8, 1024), f32)
    gain = lambda i: r.small[i:i + 1, :]
    t = Box(got={})
    def d_act(n):
        if n == 0:
            for q in lwd + [ld.dffo, ld.gate, ld.up]: q.wait()
        d = nt(r.dffo[:, :512], W[0, n:n + 768, :]) + nt(r.dffo[:, 512:], W[1, n:n + 768, :])
        g, u = r.gate[:, n:n + 768].astype(f32), r.up[:, n:n + 768].astype(f32)
        sg = jax.nn.sigmoid(g)
        r.gate[:, n:n + 768] = (d * u * sg * (1.0 + g * (1.0 - sg))).astype(bf)
        r.up[:, n:n + 768] = (d * (g * sg)).astype(bf)
    panels = [[(r.gate, C1 + 512 * p, 512, 512 * p)] for p in range(4)] + [[(r.up, C1 + FH + 512 * p, 512, 512 * p)] for p in range(4)]
    panels += [[(r.gate, C1 + 2048, 256, 2048), (r.up, C1 + FH + 2048, 256, 2048)]]
    def fetch(i):
        out, o = [], 0
        for _, cc, n, _ in panels[i]:
            out.append(w.local(I.wcat.at[:, pl.ds(cc, n)], slot(i % 4).at[:, pl.ds(o, n)])); o += n
        return out
    def slab(src, yy, base):
        d = tn(r.h2[:, col(256 * yy, 256)], src[...]).astype(bf)
        for xx in range(4):
            for u in (0, 1): grads[2][yy, xx, u, :, base:base + FH] = d[64 * xx + 32 * u:64 * xx + 32 * u + 32]
    def d_gate(i):
        if i == 0:
            t.got.update({p: fetch(p) for p in range(4)})
            ld.h2.wait()
        slab(r.gate, (y + JS[i] + 4) % 4, 0)
        sc.zsend(F.f2a, JS[i])
    def d_up(i):
        slab(r.up, (y + JS[i] + 4) % 4, FH)
        if i == 3:
            for j in JS: sc.zsend(F.f2b, j)
    def panel(i):
        for q in t.got[i]: q.wait()
        o = 0
        for nm, _, n, off in panels[i]:
            for rr, acc in ((oth, r.dhs), (own, r.dho)):
                d = nt(nm[rr, off:off + n], slot(i % 4)[:, o:o + n])
                acc[...] = d if i == 0 else acc[...] + d
            o += n
        if i + 4 < 9: t.got[i + 4] = fetch(i + 4)
        if i == 8:
            t.dh = w.send(r.dhs, r.dhr, other)
            r.h, r.y, r.conv = (r.gate.at[:, pl.ds(a, m)] for a, m in ((0, 1024), (1024, 512), (1536, 512)))
            ld.h, ld.y, ld.conv = w.local(I.h, r.h), w.local(I.y, r.y), w.local(I.conv, r.conv)
            t.win = [w.local(I.wcat.at[:, pl.ds(512 * p, 512)], slot(p + 1)) for p in range(3)]
            t.wo = [w.local(I.wcat.at[at_rows(512 * c, 512, 512), pl.ds(1536, 512)], slot(0).at[at_rows(512 * c, 512, 512)]),
                w.local(I.wor, slot(0).at[at_rows(512 * (1 - c), 512, 512)])]
            ld.small.wait(); ld.resid.wait()
    def back2():
        t.dh.wait_recv()
        def rows(i, _):
            q = at_rows(i * 64, 64, 64); qo = at_rows(256 * c + i * 64, 64, 64)
            v = r.resid[q, :]
            s2 = lax.rsqrt(jnp.mean(v * v, axis=1, keepdims=True) + EPS)
            d = r.dho[q, :] + r.dhr[q, :]
            r.gsum[1:2, :] += jnp.sum(d * v * s2, axis=0, keepdims=True)
            wt = d * gain(1)
            inner = jnp.mean(wt * v, axis=1, keepdims=True)
            dr = r.dffo[qo, :].astype(f32) + (s2 * wt - v * (s2 * s2 * s2) * inner)
            r.resid[q, :] = dr
            r.h2[qo, :] = dr.astype(bf)
            return 0
        lax.fori_loop(0, 4, rows, 0)
        t.dm = w.send(r.h2.at[own], r.h2.at[own], other)
        for q in (ld.y, ld.ext, ld.conv, ld.bcx, ld.h, ld.tok, ld.keep): q.wait()
        for q in t.wo: q.wait()
    def d_y():
        t.dm.wait_recv()
        d = nt(r.h2[:, :512], slot(0)[0:512, :]) + nt(r.h2[:, 512:], slot(0)[512:1024, :])
        r.dcv[0:512, :] = d * r.bcx[:, 512:1024].astype(f32)
        r.bcx[:, 512:1024] = (d * r.conv[...].astype(f32)).astype(bf)
        t.halo = w.send(r.dcv.at[pl.ds(0, 8)], r.dcv.at[pl.ds(512, 8)], prv)
    def d_out():
        def rows(i, _):
            d = tn(r.y[:, at_rows(256 * i, 256, 256)], r.h2[...]).astype(bf)
            for xx in range(4):
                for u in (0, 1):
                    v = d[64 * xx + 32 * u:64 * xx + 32 * u + 32]
                    r.up[at_rows(256 * i + 64 * xx + 32 * u, 32, 32), 0:512] = jnp.where(c == 0, v[:, 512:], v[:, :512])
                    grads[1][2 * c + i, xx, u, 96:128, :] = jnp.where(c == 0, v[:, :512], v[:, 512:])
            return 0
        lax.fori_loop(0, 2, rows, 0)
        t.do = [w.send(r.up.at[pl.ds(256 * i + 64 * xx + 32 * u, 32), pl.ds(0, 512)], grads[1].at[2 * c + i, xx, u, pl.ds(96, 32), :], other)
            for i in (0, 1) for xx in range(4) for u in (0, 1)]
    def d_taps():
        for q in range(0, 512, 128):
            dv = r.dcv[q:q + 128, :]
            for i in range(3):
                r.gsum[2 + i:3 + i, col(512 * c, 512)] += jnp.sum(dv * r.ext[14 + i + q:142 + i + q, :], axis=0, keepdims=True)
    def d_bx():
        t.halo.wait_recv()
        tap = [r.small[2 + i:3 + i, col(512 * c, 512)] for i in range(3)]
        r.dcv[512:520, :] = r.dcv[512:520, :] * (k < 31).astype(f32)
        for q in range(0, 512, 128):
            dx = tap[2] * r.dcv[q:q + 128, :] + tap[1] * r.dcv[q + 1:q + 129, :] + tap[0] * r.dcv[q + 2:q + 130, :]
            bp, xp = r.bcx[q:q + 128, 0:512].astype(f32), r.bcx[q:q + 128, 1024:1536].astype(f32)
            r.bcx[q:q + 128, 0:512] = (dx * xp).astype(bf)
            r.bcx[q:q + 128, 1024:1536] = (dx * bp).astype(bf)
    def d_in(i):
        if i == 0:
            for q in t.do: q.wait_recv()
        yy = (y + JS[i] + 4) % 4
        d = tn(r.h[:, col(256 * yy, 256)], r.bcx[...]).astype(bf)
        for p in range(3):
            for xx in range(4):
                for u in (0, 1): grads[1][yy, xx, u, 32 * p:32 * p + 32, :] = d[64 * xx + 32 * u:64 * xx + 32 * u + 32, 512 * p:512 * p + 512]
        sc.zsend(F.f1b, JS[i])
        if i == 3:
            for j in JS: sc.zsend(F.f1a, j)
    def d_h():
        t.dh.wait_send()
        for q in t.win: q.wait()
        for rr, acc in ((oth, r.dhs), (own, r.dho)):
            acc[...] = sum(nt(r.bcx[rr, 512 * i:512 * i + 512], slot(i + 1)[...]) for i in range(3))
        t.dh = w.send(r.dhs, r.dhr, other)
        t.act = w_down() + [w.local(I.act, r.gate)]
    def back1():
        t.dh.wait_recv()
        def rows(i, _):
            q = at_rows(i * 64, 64, 64)
            v = r.tok[q, :].astype(f32)
            s1 = lax.rsqrt(jnp.mean(v * v, axis=1, keepdims=True) + EPS)
            d = r.dho[q, :] + r.dhr[q, :]
            r.gsum[0:1, :] += jnp.sum(d * v * s1, axis=0, keepdims=True)
            wt = d * gain(0)
            inner = jnp.mean(wt * v, axis=1, keepdims=True)
            r.dho[q, :] = r.resid[q, :] + (s1 * wt - v * (s1 * s1 * s1) * inner)
            return 0
        lax.fori_loop(0, 4, rows, 0)
        pl.semaphore_signal(free, inc=1, device_id=other, device_id_type=MESH)
        t.tok = w.local(r.dho, O.dtok)
        eye = (lax.broadcasted_iota(jnp.int32, (8, 128), 0) == lax.broadcasted_iota(jnp.int32, (8, 128), 1)).astype(f32).astype(bf)
        sm = tn(r.gsum[...].astype(bf), eye).astype(bf)
        for yy in range(4):
            for xx in range(4):
                for u in (0, 1):
                    o = 256 * yy + 64 * xx + 32 * u
                    grads[0][yy, xx, u] = sm[o:o + 32]
        t.dh.wait_send()
    def ffo():
        for q in t.act: q.wait()
        t.tok.wait()
        t.resid = w.local(I.resid, r.resid)
        for rr, acc in ((oth, r.dhs), (own, r.dho)):
            for i in (0, 1): acc[:, 512 * i:512 * i + 512] = dot(r.gate[rr, :], W[i])
        pl.semaphore_wait(free, 1)
        t.dh = w.send(r.dhs, r.dhr, other)
    def mixed():
        t.dh.wait_recv(); t.resid.wait()
        r.tok[...] = (r.keep[...] * (r.resid[...] + (r.dho[...] + r.dhr[...]))).astype(bf)
        w.local(r.tok, O.mixed)
    each = functools.partial
    chunks = [each(d_act, n) for n in (0, 768, 1536)] + [each(d_gate, i) for i in range(4)] + [each(d_up, i) for i in range(4)]
    chunks += [each(panel, i) for i in range(9)] + [back2, d_y, d_out, d_taps, d_bx] + [each(d_in, i) for i in range(4)] + [d_h, back1, ffo, mixed]
    half = 512 * c
    at_in = lambda o: [(32 * p, 0, 256, O.din, 1024 * p + half + o) for p in range(3)] + [(96, 0, 256, O.dout, half + o)]
    ends = [at_in(0), at_in(256), [(0, 0, 128, O.ds.at[c], None)], [(0, 0, FH, O.dg, FH * c)], [(0, 0, FH, O.du, FH * c)],
        [(0, 0, 256, O.dd, half)], [(0, 0, 256, O.dd, half + 256)]]
    flows = list(vars(F).values())
    moves = (sc.first, sc.second, sc.third, sc.last1, sc.last2)
    for what, *where in ORDER_B:
        if not where: chunks[what]()
        elif what < 3: moves[what](flows[where[0]], where[1])
        elif what < 5: moves[what](flows[where[0]])
        else: sc.last3(flows[where[0]], ends[where[0]])
    w.drain()

def backward_all(a, tokens, keep):
    a = Box(a)
    a.ddown = a.ddown.reshape(4, 4, 2, 144, 512)
    scr = [*B_SCR.values()] + GRADS + GRADS + [v for t in RFLOWS.values() for v in flow_scratch(t)]
    outs = call(backward_kernel, [*B_OUT.values()], scr, 2, 63, [pltpu.SemaphoreType.REGULAR], *vars(a).values(), tokens, keep)
    return Box(dict(zip(B_OUT, outs)))


def body(tokens, lengths, norm1_gain, in_proj, conv_weight, out_proj, norm2_gain, w_gate, w_up, w_down, cotangent):
    rows = tokens.shape[0]
    place = lax.axis_index("shard")
    slot = lax.axis_index("rep")
    slot_ids = jnp.arange(lengths.shape[0], dtype=jnp.int32)
    length = jnp.sum(jnp.where(slot_ids == slot, lengths, 0))
    valid = jnp.clip(length - place * rows, 0, rows)
    keep = (jnp.arange(rows, dtype=jnp.int32) < valid).astype(jnp.float32)[:, None]
    a = forward_all(tokens, cotangent, keep, in_proj, out_proj, smalls(norm1_gain, norm2_gain, conv_weight), w_gate, w_up, w_down)
    b = backward_all(a, tokens, keep)
    sm = b.ds[0] + b.ds[1]
    return b.mixed, b.dtok, sm[:, 0], b.din, sm[:, 2:5].T, b.dout, sm[:, 1], b.dg, b.du, b.dd

def solution(mesh):
    tok = P(("rep", "shard"), None)
    par = (P("shard"), P("shard", None), P(None, "shard"), P("shard", None), P("shard"), P("shard", None), P("shard", None), P("shard", None))
    return jax.shard_map(body, mesh=mesh, in_specs=(tok, P()) + par + (tok,), out_specs=(tok, tok) + par, check_vma=False)
```

```python
ORDER_A = (
    (0, 1), (0, 0), (0, 3), (0, 2), (1, 0), (1, 1), (2, 0), (4, 0, 0), (2, 1), (4, 1, 0), (3, 0), (4, 0, -1), (4, 1, -1), (4, 0, 1), (5, 0, 0),
    (4, 1, 1), (3, 1), (5, 1, 0), (4, 0, 2), (5, 1, -1), (1, 3), (1, 2), (5, 0, -1), (5, 1, 1), (5, 0, 1), (5, 0, 2), (4, 1, 2), (4, 3, 0), (2, 3),
    (2, 2), (4, 2, 0), (5, 1, 2), (5, 3, 0), (3, 3), (4, 3, -1), (4, 2, -1), (4, 3, 1), (4, 2, 1), (3, 2), (5, 2, 0), (0,), (4, 3, 2), (5, 2, -1),
    (1,), (2,), (5, 3, -1), (0, 4), (1, 4), (5, 3, 1), (5, 2, 1), (0, 5), (1, 5), (3,), (5, 3, 2), (4, 2, 2), (4,), (4, 4, 0), (2, 4), (5,), (6,),
    (2, 5), (4, 5, 0), (7,), (5, 4, 0), (5, 2, 2), (3, 4), (4, 4, -1), (8,), (4, 5, -1), (9,), (4, 4, 1), (10,), (3, 5), (11,), (4, 5, 1), (5, 5, 0),
    (4, 4, 2), (12,), (13,), (5, 4, -1), (5, 5, -1), (14,), (5, 4, 1), (4, 5, 2), (15,), (5, 4, 2), (5, 5, 1), (16,), (17,), (5, 5, 2), (18,),)
ORDER_B = (
    (0, 5, -1), (0, 5, 2), (0, 6, -1), (0, 6, 2), (0, 5, 0), (0, 5, 1), (0, 6, 0), (0, 6, 1), (0,), (1,), (1, 6, -1), (1, 5, -1), (2,), (1, 6, 2),
    (1, 6, 0), (1, 5, 2), (1, 5, 0), (3,), (1, 6, 1), (1, 5, 1), (4,), (5,), (6,), (7,), (8,), (9,), (10,), (11,), (2, 6, 2), (2, 5, 2), (12,), (13,),
    (14,), (15,), (16,), (17,), (18,), (19,), (2, 6, 0), (2, 5, 0), (0, 3, 2), (20,), (21,), (22,), (23,), (24,), (25,), (0, 4, 2), (26,), (27,),
    (28,), (2, 6, -1), (2, 6, 1), (2, 5, -1), (2, 5, 1), (29,), (0, 4, -1), (0, 3, -1), (1, 4, 2), (1, 3, 2), (30,), (31,), (3, 6), (3, 5), (0, 4, 1),
    (32,), (1, 3, -1), (1, 4, -1), (0, 3, 1), (33,), (0, 4, 0), (34,), (35,), (2, 3, 2), (36,), (2, 4, 2), (37,), (38,), (1, 4, 1), (4, 6), (0, 3, 0),
    (4, 5), (1, 3, 1), (39,), (2, 4, -1), (0, 1, 2), (0, 2, -1), (0, 2, 2), (0, 2, 0), (0, 2, 1), (40,), (0, 0, 2), (1, 4, 0), (2, 3, -1), (1, 3, 0),
    (0, 1, -1), (41,), (2, 3, 1), (0, 0, -1), (2, 4, 1), (1, 0, 2), (0, 1, 1), (1, 1, 2), (1, 2, -1), (1, 2, 2), (1, 2, 0), (1, 2, 1), (0, 0, 1),
    (2, 4, 0), (0, 1, 0), (2, 3, 0), (1, 1, -1), (3, 4), (0, 0, 0), (1, 1, 1), (3, 3), (2, 1, 2), (1, 0, -1), (2, 2, 2), (2, 2, 0), (2, 0, 2),
    (1, 1, 0), (1, 0, 1), (1, 0, 0), (2, 1, -1), (2, 1, 1), (2, 0, -1), (2, 2, -1), (2, 2, 1), (2, 0, 1), (2, 1, 0), (4, 4), (2, 0, 0), (3, 1),
    (3, 2), (3, 0), (4, 3), (4, 1), (4, 2), (4, 0),)

import functools
import jax, jax.numpy as jnp
from jax import lax
from jax.experimental import pallas as pl
from jax.experimental.pallas import tpu as pltpu
from jax.sharding import PartitionSpec as P
MESH = pl.DeviceIdType.MESH
EPS = 1e-05
bf, f32 = jnp.bfloat16, jnp.float32
C1 = 2176; HALF = 1152; CAT = 6784; UNIT = 32; DUNIT = 144; FH = 2304
COPIES = 272
JS = (2, -1, 1, 0)
PAIR, CROSS, X, Y = 1, 2, 0, 1
ONE, TWO, THREE = 1, 2, 3
XY, YX = (X, Y), (Y, X)
class Box:
    def __init__(self, *a, **kw):
        for d in a: self.__dict__.update(d)
        self.__dict__.update(kw)

FLOWS = dict(
    f1a=Box(kind=1, base=0, step=384, gw=640, fw=384, to=PAIR, order=XY),
    f1b=Box(kind=1, base=1024, step=384, gw=768, fw=384, to=CROSS, order=YX),
    f2a=Box(kind=2, base=0, step=768, gw=1536, fw=768, to=PAIR, order=YX),
    f2b=Box(kind=2, base=2304, step=896, gw=1408, fw=896, to=CROSS, order=XY),
    f3a=Box(kind=3, base=0, step=0, gw=256, fw=0, to=None, order=XY),
    f3b=Box(kind=3, base=256, step=0, gw=256, fw=0, to=None, order=YX))

def spot():
    rep = lax.axis_index("rep"); s = lax.axis_index("shard")
    return (s // 4) % 4, s // 16, ((s // 2) % 2) * 2 + rep, s % 2

def device(x, y, z, c):
    return (z % 2, ((y * 4 + x) * 2 + z // 2) * 2 + c)

def moved(x, y, z, c, axis, step):
    if axis == X: return device((x + step + 4) % 4, y, z, c)
    return device(x, (y + step + 4) % 4, z, c)

def along(x, y, z, c, step):
    k = ((y * 4 + x) * 2 + z // 2 + step + 32) % 32
    return device((k // 2) % 4, k // 8, (k % 2) * 2 + z % 2, c)

def greet(devices):
    bar = pltpu.get_barrier_semaphore()
    for d in devices:
        pl.semaphore_signal(bar, inc=1, device_id=d, device_id_type=MESH)
    pl.semaphore_wait(bar, len(devices))

class Copy:
    def __init__(self, cp): self.cp, self.here, self.gone = cp, False, False
    def wait_recv(self): self.cp.wait_recv(); self.here = True
    def wait_send(self): self.cp.wait_send(); self.gone = True

class Near:
    def __init__(self, cp): self.cp, self.here = cp, False
    def wait(self): self.cp.wait(); self.here = True

class Wire:
    def __init__(self, ss, rs, ls): self.ss, self.rs, self.ls, self.sent, self.near = ss, rs, ls, [], []
    def send(self, src, dst, dev):
        i = len(self.sent)
        cp = pltpu.make_async_remote_copy(src_ref=src, dst_ref=dst, send_sem=self.ss.at[i], recv_sem=self.rs.at[i], device_id=dev, device_id_type=MESH)
        cp.start(); self.sent.append(Copy(cp)); return self.sent[-1]
    def local(self, src, dst):
        cp = pltpu.make_async_copy(src, dst, self.ls.at[len(self.near)])
        cp.start(); self.near.append(Near(cp)); return self.near[-1]
    def drain(self):
        for cp in self.near:
            if not cp.here: cp.wait()
        for cp in self.sent:
            if not cp.here: cp.wait_recv()
            if not cp.gone: cp.wait_send()

def at_rows(v, n, m=16): return pl.ds(pl.multiple_of(v, m), n)

class All:
    def __init__(self, *q): self.q = q
    def wait_recv(self):
        for q in self.q: q.wait_recv()

class Gather:
    def __init__(self, w, go, pair, cross, other, x, y, z, w1, w2, wd, wdr):
        self.w, self.go, self.x, self.y, self.other, self.wdr, self.hi = w, go, x, y, other, wdr, z // 2
        self.f = Box()
        for n, t in FLOWS.items():
            sel = {PAIR: z % 2, CROSS: z // 2, None: 0}[t.to]
            d = t.kind == 3
            vars(self.f)[n] = Box(vars(t), buf=(w1, w2, wd)[t.kind - 1], unit=DUNIT if d else UNIT, mine=(t.base + t.step * sel, t.gw),
                alone=(t.base + t.gw * sel, t.fw), dev={PAIR: pair, CROSS: cross, None: None}[t.to], z=[], p={}, m={}, p2={}, m2={})
    def block(self, f, da, db, unit=None, cols=None, buf=None):
        a, b = f.order
        pos = {X: self.x, Y: self.y}
        pos[a] = (pos[a] + da + 4) % 4
        pos[b] = (pos[b] + db + 4) % 4
        u = f.unit
        row = (pos[Y] * 4 + pos[X]) * (2 * u)
        n = 2 * u
        if unit is not None: row, n = row + unit * u, u
        col, width = cols or f.mine
        return (f.buf if buf is None else buf).at[at_rows(row, n), pl.ds(col if isinstance(col, int) else pl.multiple_of(col, 128), width)]
    def push(self, f, da, db, dev, unit=None):
        v = self.block(f, da, db, unit)
        return self.w.send(v, v, dev)
    def fwd(self, f, da, db):
        if f.dev is not None and (da or db):
            v = self.block(f, da, db, None, f.alone)
            f.z.append(self.w.send(v, v, f.dev))
        if f.kind == 3: f.z.append(self.w.send(self.block(f, da, db), self.block(f, da, db, None, None, self.wdr), self.other))
    def open2(self, f, j):
        b = f.order[1]
        f.p[j] = self.push(f, j, 0, self.go[(b, 1)])
        f.m[j] = self.push(f, j, 0, self.go[(b, -1)])
    def r1(self, f, own):
        a, b = f.order
        u = self.hi if own else 1 - self.hi
        new = [self.push(f, 0, 0, self.go[(d, st)], u) for d in (a, b) for st in (1, -1)]
        if own: f.half = new
        else:
            f.p[None], f.m[None], f.p[0], f.m[0] = (All(*q) for q in zip(f.half, new))
            self.fwd(f, 0, 0)
    def r2(self, f):
        a = f.order[0]
        f.p[None].wait_recv(); f.p2[None] = self.push(f, -1, 0, self.go[(a, 1)], 0)
        f.m[None].wait_recv(); f.m2[None] = self.push(f, 1, 0, self.go[(a, -1)], 1)
        self.open2(f, -1); self.open2(f, 1)
        self.fwd(f, -1, 0); self.fwd(f, 1, 0)
    def r3(self, f):
        f.p2[None].wait_recv(); f.m2[None].wait_recv()
        self.open2(f, 2); self.fwd(f, 2, 0)
    def r4(self, f, j):
        b = f.order[1]
        f.p[j].wait_recv(); f.p2[j] = self.push(f, j, -1, self.go[(b, 1)], 0)
        f.m[j].wait_recv(); f.m2[j] = self.push(f, j, 1, self.go[(b, -1)], 1)
        self.fwd(f, j, -1); self.fwd(f, j, 1)
    def r5(self, f, j):
        f.p2[j].wait_recv(); f.m2[j].wait_recv()
        self.fwd(f, j, 2)
    def all_here(self, f):
        for q in f.z: q.wait_recv()

def dot(a, b): return jnp.dot(a, b, preferred_element_type=f32)
def tn(a, b): return lax.dot_general(a, b, (((0,), (0,)), ((), ())), preferred_element_type=f32)
def nt(a, b): return lax.dot_general(a, b, (((1,), (1,)), ((), ())), preferred_element_type=f32)

A_GOT = dict(w1=((1024, C1), bf), w2=((1024, 2 * FH), bf), wd=((4608, 512), bf), wor=((512, 512), bf), wdr=((4608, 512), bf), ddown=((4608, 512), bf))
A_MADE = dict(h=((512, 1024), bf), bcx=((512, 1536), bf), ext=((528, 512), f32), conv=((512, 512), bf), y=((512, 512), bf),
    resid=((256, 1024), f32), h2=((512, 1024), bf), gate=((512, FH), bf), up=((512, FH), bf), act=((512, FH), bf),
    dffo=((512, 1024), bf), small=((8, 1024), f32))
A_SCR = dict(T=((512, 1024), bf), cotv=((256, 1024), bf), win=((1024, 1536), bf), wo=((512, 1024), bf), wsm=((1024, 128), bf),
    w2=((1024, 2 * FH), bf), gf=((512, FH), f32), cpart=((512, 512), f32), mixs=((256, 1024), f32), mixr=((256, 1024), f32),
    dnf=((DUNIT, 512), f32), dns=((72, 512), f32), dnb=((DUNIT, 512), bf), ddn=((2, FH, 512), bf),
    inp=((16, 3072), bf), outp=((16, 1024), bf), sml=((16, 128), bf), srow=((16, 128), bf), wgs=((16, 4608), bf), wus=((16, 4608), bf), wds=((72, 1024), bf), keepv=((256, 1), f32))

def named(groups, refs):
    refs, out = list(refs), []
    for g in groups:
        out.append(Box(dict(zip(g, refs)))); refs = refs[len(g):]
    return out, refs

def forward_kernel(*refs):
    A_IN = dict(tokens=0, cot=0, keep=0, inp=0, outp=0, sml=0, wgs=0, wus=0, wds=0)
    (I, O, M, V, S), (ss, rs, ls) = named([A_IN, A_GOT, A_MADE, A_MADE, A_SCR], refs)
    w1, w2, wd, wor, wdr = O.w1, S.w2, O.wd, O.wor, O.wdr
    x, y, z, c = spot()
    hi = z // 2
    s = ((y * 4 + x) * 2 + hi) * 2 + c
    k = s // 2
    pair = device(x, y, z + 1 - 2 * (z % 2), c)
    cross = device(x, y, 3 - z, c)
    other = device(x, y, z, 1 - c)
    nxt, prv = along(x, y, z, c, 1), along(x, y, z, c, -1)
    go = {(a, st): moved(x, y, z, c, a, st) for a in XY for st in (1, -1)}
    w = Wire(ss, rs, ls)
    own, oth = at_rows(256 * c, 256, 256), at_rows(256 * (1 - c), 256, 256)
    col = lambda p, n: pl.ds(pl.multiple_of(p, 128), n)
    lds = w.local(I.wds, S.wds)
    lrow = w.local(I.sml, S.srow)
    lin = [w.local(a, b) for a, b in ((I.inp, S.inp), (I.outp, S.outp), (I.wgs, S.wgs), (I.wus, S.wus))]
    lcot = [w.local(I.cot, S.cotv), w.local(I.keep, S.keepv)]
    ltok = w.local(I.tokens, S.T.at[own])
    lrow.wait()
    eye = (lax.broadcasted_iota(jnp.int32, (16, 128), 0) == lax.broadcasted_iota(jnp.int32, (16, 128), 1)).astype(f32).astype(bf)
    S.sml[...] = tn(S.srow[...], eye)[0:16].astype(bf)
    greet(list(go.values()) + [pair, cross, other, nxt, prv])
    rows = at_rows(16 * s, 16)
    pieces = [(I.inp, S.inp, 1024 * i, 512, w1, 512 * i) for i in range(3)] + [(I.outp, S.outp, 0, 512, w1, 1536), (I.wgs, S.wgs, 0, FH, w2, 0), (I.wus, S.wus, 0, FH, w2, FH)]
    got = [w.send(S.sml, w1.at[rows, pl.ds(2048, 128)], other)]
    for src, _, a, n, to, d in pieces: got.append(w.send(src.at[:, col(a + n * (1 - c), n)], to.at[rows, pl.ds(d, n)], other))
    for q in lin: q.wait()
    mine = [w.local(S.sml, w1.at[rows, pl.ds(2048, 128)])]
    for _, src, a, n, to, d in pieces: mine.append(w.local(src.at[:, col(a + n * c, n)], to.at[rows, pl.ds(d, n)]))
    lds.wait()
    S.dns[...] = S.wds[:, col(512 * (1 - c), 512)].astype(f32)
    gdn = w.send(S.dns, S.dnf.at[at_rows(72 * c, 72, 8)], other)
    S.dnf[at_rows(72 * c, 72, 8), :] = S.wds[:, col(512 * c, 512)].astype(f32)
    gtok = w.send(I.tokens, S.T.at[own], other)
    g = Gather(w, go, pair, cross, other, x, y, z, w1, w2, wd, wdr)
    F = g.f
    for q in mine: q.wait()
    for q in got: q.wait_recv()
    urow, drow = at_rows(UNIT * k, UNIT, UNIT), at_rows(DUNIT * k, DUNIT)
    z1 = w.send(w1.at[urow], w1.at[urow], cross)
    z2 = w.send(w2.at[urow], w2.at[urow], cross)
    gdn.wait_recv()
    S.dnb[...] = S.dnf[...].astype(bf)
    z3 = w.send(S.dnb, wd.at[drow, :], cross)
    lwd = w.local(S.dnb, wd.at[drow, :])
    for q in lcot: q.wait()
    V.dffo[own, :] = (S.keepv[...] * S.cotv[...].astype(f32)).astype(bf)
    gdf = w.send(V.dffo.at[own], V.dffo.at[own], other)
    ltok.wait(); gtok.wait_recv(); lwd.wait()
    t = Box()
    def save(**kw):
        for n in kw: w.local(vars(V)[n], vars(M)[n])
    def one():
        for f in (F.f1a, F.f1b): g.all_here(f)
        l1 = w.local(w1.at[:, pl.ds(2048, 128)], S.wsm)
        t.win = w.local(w1.at[:, pl.ds(0, 1536)], S.win)
        t.wor = w.send(w1.at[at_rows(512 * (1 - c), 512, 512), pl.ds(1536, 512)], wor, other)
        t.wo = w.local(w1.at[at_rows(512 * c, 512, 512), pl.ds(1536, 512)], S.wo.at[:, col(512 * c, 512)])
        l1.wait()
        V.small[...] = nt(eye, S.wsm[...])[0:8]
    def norm1():
        def rows(i, _):
            q = at_rows(i * 64, 64, 64)
            v = S.T[q, :].astype(f32)
            sc = lax.rsqrt(jnp.mean(v * v, axis=1, keepdims=True) + EPS)
            V.h[q, :] = (v * sc * V.small[0:1, :]).astype(bf)
            return 0
        lax.fori_loop(0, 8, rows, 0)
        t.win.wait()
    ext = V.ext
    def b_x():
        for n in (0, 256):
            b_ = dot(V.h[...], S.win[:, n:n + 256])
            x_ = dot(V.h[...], S.win[:, 1024 + n:1280 + n])
            V.bcx[:, n:n + 256] = b_.astype(bf)
            V.bcx[:, 1024 + n:1280 + n] = x_.astype(bf)
            ext[16:528, n:n + 256] = (b_ * x_).astype(bf).astype(f32)
        t.halo = w.send(ext.at[pl.ds(520, 8)], ext.at[pl.ds(8, 8)], nxt)
        t.wor.wait_recv()
        t.wo2 = w.local(wor, S.wo.at[:, col(512 * (1 - c), 512)])
    def c_():
        for n in (0, 256):
            v = dot(V.h[...], S.win[:, 512 + n:768 + n])
            S.cpart[:, n:n + 256] = v
            V.bcx[:, 512 + n:768 + n] = v.astype(bf)
        save(h=1, bcx=1, small=1)
    def conv():
        t.halo.wait_recv()
        ext[8:16, :] = ext[8:16, :] * (k > 0).astype(f32)
        t0, t1, t2 = (V.small[2 + i:3 + i, col(512 * c, 512)] for i in range(3))
        for q in range(0, 512, 128):
            cv = t0 * ext[14 + q:142 + q, :] + t1 * ext[15 + q:143 + q, :] + t2 * ext[16 + q:144 + q, :]
            V.conv[q:q + 128, :] = cv.astype(bf)
            V.y[q:q + 128, :] = (S.cpart[q:q + 128, :] * cv).astype(bf)
        t.wo.wait(); t.wo2.wait()
    def mix():
        S.mixs[...] = dot(V.y[oth, :], S.wo[...])
        t.mix = w.send(S.mixs, S.mixr, other)
    def mix2():
        V.resid[...] = dot(V.y[own, :], S.wo[...])
        save(ext=1, conv=1, y=1)
    def norm2():
        t.mix.wait_recv()
        def rows(i, _):
            q, qo = at_rows(i * 64, 64, 64), at_rows(256 * c + i * 64, 64, 64)
            v = S.T[qo, :].astype(f32) + (V.resid[q, :] + S.mixr[q, :])
            V.resid[q, :] = v
            sc = lax.rsqrt(jnp.mean(v * v, axis=1, keepdims=True) + EPS)
            V.h2[qo, :] = (v * sc * V.small[1:2, :]).astype(bf)
            return 0
        lax.fori_loop(0, 4, rows, 0)
        t.h2 = w.send(V.h2.at[own], V.h2.at[own], other)
        save(resid=1)
    def two():
        g.all_here(F.f2a)
        w.local(w2.at[:, pl.ds(0, FH)], O.w2.at[:, pl.ds(0, FH)])
        t.h2.wait_recv(); gdf.wait_recv()
        save(h2=1, dffo=1)
    def gate(i):
        n = 768 * i
        v = dot(V.h2[...], w2[:, n:n + 768])
        S.gf[:, n:n + 768] = v
        V.gate[:, n:n + 768] = v.astype(bf)
    def up_here():
        g.all_here(F.f2b)
        w.local(w2.at[:, pl.ds(FH, FH)], O.w2.at[:, pl.ds(FH, FH)])
        save(gate=1)
    def up(i):
        n = 768 * i
        g_, u_ = S.gf[:, n:n + 768], dot(V.h2[...], w2[:, FH + n:FH + n + 768])
        V.up[:, n:n + 768] = u_.astype(bf)
        V.act[:, n:n + 768] = (g_ * jax.nn.sigmoid(g_) * u_).astype(bf)
        if i == 2: save(up=1, act=1)
    def down(i):
        def rows(m, _):
            q = at_rows(768 * i + m * 256, 256, 256)
            v = tn(V.act[:, q], V.dffo[...]).astype(bf)
            S.ddn[0, q, :] = v[:, :512]
            S.ddn[1, q, :] = v[:, 512:]
            return 0
        lax.fori_loop(0, 3, rows, 0)
        to = at_rows(FH * c + 768 * i, 768, 256)
        w.send(S.ddn.at[1 - c, pl.ds(768 * i, 768)], O.ddown.at[to, :], other)
        w.local(S.ddn.at[c, pl.ds(768 * i, 768)], O.ddown.at[to, :])
    each = functools.partial
    chunks = [one, norm1, b_x, c_, conv, mix, mix2, norm2, two] + [each(gate, i) for i in range(3)] + [up_here] + [each(up, i) for i in range(3)] + [each(down, i) for i in range(3)]
    flows = list(vars(F).values())
    moves = (g.r1, g.r1, g.r2, g.r3, g.r4, g.r5)
    need = {0: z1, 2: z2, 4: z3}
    for what, *where in ORDER_A:
        if not where: chunks[what](); continue
        f = flows[where[0]]
        if what == 1:
            q = need.pop(where[0] // 2 * 2, None)
            if q is not None: q.wait_recv()
        if what < 2: g.r1(f, what == 0)
        else: moves[what](f, *where[1:])
    w.drain()

def call(kernel, outs, scratch, ident, limit, extra, *args):
    hbm = pl.BlockSpec(memory_space=pl.ANY)
    return pl.pallas_call(
        kernel, out_shape=tuple(jax.ShapeDtypeStruct(*v) for v in outs), in_specs=[hbm] * len(args), out_specs=(hbm,) * len(outs),
        scratch_shapes=[pltpu.VMEM(*v) for v in scratch] + [pltpu.SemaphoreType.DMA((n,)) for n in (COPIES, COPIES, 96)] + extra,
        compiler_params=pltpu.CompilerParams(collective_id=ident, has_side_effects=True, vmem_limit_bytes=limit * 2**20))(*args)

def forward_all(*args):
    outs = call(forward_kernel, [*A_GOT.values(), *A_MADE.values()], [*A_MADE.values(), *A_SCR.values()], 1, 60, [], *args)
    return dict(zip([*A_GOT, *A_MADE], outs))

def smalls(norm1_gain, norm2_gain, conv_weight):
    return jnp.pad(jnp.concatenate([norm1_gain[None], norm2_gain[None], conv_weight]), ((0, 11), (0, 112)))


RFLOWS = dict(
    f1a=Box(kind=1, base=0, step=128, gw=128, fw=128, to=PAIR, order=XY),
    f1b=Box(kind=1, base=256, step=128, gw=128, fw=128, to=CROSS, order=YX),
    f1s=Box(kind=0, base=0, step=0, gw=128, fw=0, to=None, order=YX),
    f2a=Box(kind=2, base=0, step=640, gw=1664, fw=640, to=PAIR, order=YX),
    f2b=Box(kind=2, base=2304, step=384, gw=1920, fw=384, to=CROSS, order=XY),
    f3a=Box(kind=3, base=0, step=0, gw=256, fw=0, to=None, order=XY),
    f3b=Box(kind=3, base=256, step=0, gw=256, fw=0, to=None, order=YX))
UNITS, WIDTH = (32, 128, 32, 144), (128, 512, 2 * FH, 512)
B_OUT = dict(mixed=((256, 1024), bf), dtok=((256, 1024), f32), din=((16, 3072), f32), dout=((16, 1024), f32),
    dg=((16, 4608), f32), du=((16, 4608), f32), dd=((72, 1024), f32), ds=((2, 16, 128), f32))
GRADS = [((4, 4, 2, u, n), bf) for u, n in zip(UNITS, WIDTH)]
def flow_scratch(t):
    u = UNITS[t.kind]
    return [((6, u, t.gw), bf), ((3, u, t.gw), bf), ((u, t.gw + t.fw), f32)]
B_SCR = dict(W=((2, FH, 512), bf), gate=((512, FH), bf), up=((512, FH), bf), dffo=((512, 1024), bf), h2=((512, 1024), bf),
    bcx=((512, 1536), bf), ext=((528, 512), f32), resid=((256, 1024), f32), small=((8, 1024), f32),
    tok=((256, 1024), bf), dhs=((256, 1024), f32), dhr=((256, 1024), f32), dho=((256, 1024), f32), dcv=((520, 512), f32),
    gsum=((8, 1024), f32), keep=((256, 1), f32))

def add_into(dst, srcs, rows, step=16):
    def body(i, _):
        r = pl.ds(pl.multiple_of(i * step, step), step)
        if len(srcs) == 1: dst[r, :] = dst[r, :] + srcs[0][r, :]
        else:
            v = dst[r, :].astype(f32)
            for q in srcs: v = v + q[r, :].astype(f32)
            dst[r, :] = v.astype(bf)
        return 0
    lax.fori_loop(0, rows // step, body, 0)

class Scatter:
    def __init__(self, w, go, pair, cross, far, x, y, z, c, other, grads, lands, bufs):
        self.w, self.go, self.x, self.y, self.z, self.c, self.other = w, go, x, y, z, c, other
        self.hi, self.zl = z // 2, z % 2
        self.f = Box()
        for i, (n, t) in enumerate(RFLOWS.items()):
            sel = {PAIR: (self.zl + self.hi) % 2, CROSS: self.hi, None: 0}[t.to]
            k = t.kind
            f = Box(vars(t), G=grads[k], L=lands[k], u=UNITS[k], sel=sel, col=t.base + t.step * sel, out=[],
                ecol=t.base + t.gw * sel, pcol=t.base + t.gw * (1 - sel), dev={PAIR: pair, CROSS: cross, None: None}[t.to],
                A={}, s={}, t={}, s2={}, t2={})
            f.M, f.E, f.F = bufs[3 * i:3 * i + 3]
            vars(self.f)[n] = f
        self.pair, self.cross, self.far = pair, cross, far
    def cols(self, c, n): return pl.ds(c if isinstance(c, int) else pl.multiple_of(c, 128), n)
    def at(self, f, da, db):
        a, b = f.order
        pos = {X: self.x, Y: self.y}
        pos[a] = (pos[a] + da + 4) % 4
        pos[b] = (pos[b] + db + 4) % 4
        return pos[Y], pos[X]
    def part(self, ref, f, p, u=None):
        if u is None: return ref.at[p[0], p[1], :, :, self.cols(f.col, f.gw)]
        return ref.at[p[0], p[1], u, :, self.cols(f.col, f.gw)]
    def zline(self, ref, f, j, col):
        l = self.at(f, j, 0)
        cs = self.cols(col, f.fw)
        return ref.at[l[0], :, :, :, cs] if f.order[0] == Y else ref.at[:, l[1], :, :, cs]
    def zsend(self, f, j):
        f.A[j] = self.w.send(self.zline(f.G, f, j, f.pcol), self.zline(f.L, f, j, f.ecol), f.dev)
    def first(self, f, j):
        b = f.order[1]
        if f.to:
            f.A[j].wait_recv()
            g, l = self.zline(f.G, f, j, f.ecol), self.zline(f.L, f, j, f.pcol)
            for i in range(4):
                for u in (0, 1): add_into(g.at[i, u], [l.at[i, u]], f.u)
        p = self.at(f, j, 2)
        f.s[j] = self.w.send(self.part(f.G, f, p, 0), self.part(f.L, f, p, 0), self.go[(b, 1)])
        f.t[j] = self.w.send(self.part(f.G, f, p, 1), self.part(f.L, f, p, 1), self.go[(b, -1)])
    def second(self, f, j):
        b, u = f.order[1], f.u
        f.s[j].wait_recv(); p = self.at(f, j, 1)
        add_into(self.part(f.G, f, p, 0), [self.part(f.L, f, p, 0)], u)
        f.s2[j] = self.w.send(self.part(f.G, f, p), self.part(f.L, f, p), self.go[(b, 1)])
        f.t[j].wait_recv(); p = self.at(f, j, -1)
        add_into(self.part(f.G, f, p, 1), [self.part(f.L, f, p, 1)], u)
        f.t2[j] = self.w.send(self.part(f.G, f, p), self.part(f.L, f, self.at(f, j, 1)), self.go[(b, -1)])
    def third(self, f, j):
        a, u, M = f.order[0], f.u, f.M
        f.s2[j].wait_recv(); f.t2[j].wait_recv()
        p = self.at(f, j, 0); o = self.at(f, j, 2)
        for v in (0, 1): add_into(self.part(f.G, f, p, v), [self.part(f.L, f, p, v), self.part(f.L, f, o, v)], u)
        if j == 2:
            f.c = self.w.send(self.part(f.G, f, p, 0), M.at[0], self.go[(a, 1)])
            f.d = self.w.send(self.part(f.G, f, p, 1), M.at[1], self.go[(a, -1)])
        elif j == 1:
            f.c.wait_recv(); add_into(self.part(f.G, f, p, 0), [M.at[0]], u)
            f.c2 = self.w.send(self.part(f.G, f, p), M.at[pl.ds(2, 2)], self.go[(a, 1)])
        elif j == -1:
            f.d.wait_recv(); add_into(self.part(f.G, f, p, 1), [M.at[1]], u)
            f.d2 = self.w.send(self.part(f.G, f, p), M.at[pl.ds(4, 2)], self.go[(a, -1)])
    def last1(self, f):
        u, M, me = f.u, f.M, (self.y, self.x)
        f.c2.wait_recv(); f.d2.wait_recv()
        for v in (0, 1): add_into(self.part(f.G, f, me, v), [M.at[2 + v], M.at[4 + v]], u)
        away = self.part(f.G, f, me, 1 - self.hi)
        f.e = [self.w.send(self.part(f.G, f, me, self.hi), f.E.at[0], self.pair), self.w.send(away, f.E.at[1], self.cross), self.w.send(away, f.E.at[2], self.far)]
    def last2(self, f, targets):
        E, F, gw, fw, sel = f.E, f.F, f.gw, f.fw, f.sel
        for q in f.e: q.wait_recv()
        G = f.G.at[self.y, self.x, self.hi]
        same, two = (1, (0, 2)) if f.to == PAIR else (0, (1, 2))
        def mine(o, n): return G[:, self.cols(o + f.col, n)].astype(f32) + E[same, :, self.cols(o, n)].astype(f32)
        def theirs(o, n): return E[two[0], :, self.cols(o, n)].astype(f32) + E[two[1], :, self.cols(o, n)].astype(f32)
        ov = gw - fw
        if fw:
            F[:, self.cols(gw * sel, fw)] = mine(ov * sel, fw)
            F[:, self.cols(gw * (1 - sel), fw)] = theirs(ov * (1 - sel), fw)
        if ov: F[:, pl.ds(fw, ov)] = mine(fw * (1 - sel), ov) + theirs(fw * sel, ov)
        rows = f.u if f.kind == 3 else 32
        half = rows // 2
        m = 8
        for prow, pcol, pw, out, ocol in targets:
            src = lambda q: F.at[pl.ds(pl.multiple_of(prow + half * q, m), half), pl.ds(pcol, pw)]
            dst = out if ocol is None else out.at[:, self.cols(ocol, pw)]
            f.out.append(self.w.send(src(1 - self.c), dst, self.other))
            f.out.append(self.w.local(src(self.c), dst))
    def wait_out(self, f):
        for i, q in enumerate(f.out):
            if i % 2: q.wait()
            else: q.wait_recv()

def backward_kernel(*refs):
    (I, O, r), refs = named([dict(A_GOT, **A_MADE, tokens=0, keep=0), B_OUT, B_SCR], refs)
    grads, lands, bufs, (ss, rs, ls, free) = refs[:4], refs[4:8], refs[8:-4], refs[-4:]
    x, y, z, c = spot()
    hi = z // 2
    k = (y * 4 + x) * 2 + hi
    pair = device(x, y, z + 1 - 2 * (z % 2), c)
    cross = device(x, y, 3 - z, c)
    far = device(x, y, (z + 2) % 4, c)
    other = device(x, y, z, 1 - c)
    nxt, prv = along(x, y, z, c, 1), along(x, y, z, c, -1)
    go = {(a, st): moved(x, y, z, c, a, st) for a in XY for st in (1, -1)}
    w = Wire(ss, rs, ls)
    own, oth = at_rows(256 * c, 256, 256), at_rows(256 * (1 - c), 256, 256)
    col = lambda p, n: pl.ds(pl.multiple_of(p, 128), n)
    W = r.W
    slot = lambda i: W.at[i // 2, pl.ds(1024 * (i % 2), 1024)]
    def w_down():
        return [w.local(I.wd.at[at_rows(FH * c, FH, FH), :], W.at[c]), w.local(I.wdr.at[at_rows(FH * c, FH, FH), :], W.at[1 - c])]
    lgd = w.local(I.ddown, grads[3])
    lwd = w_down()
    ld = Box({n: w.local(vars(I)[n], vars(r)[n]) for n in dict(dffo=0, gate=0, up=0, h2=0, small=0, resid=0, ext=0, bcx=0, keep=0)})
    ld.tok = w.local(I.tokens, r.tok)
    greet(list(go.values()) + [pair, cross, far, other, nxt, prv])
    sc = Scatter(w, go, pair, cross, far, x, y, z, c, other, grads, lands, bufs)
    F = sc.f
    lgd.wait()
    r.gsum[...] = jnp.zeros((8, 1024), f32)
    gain = lambda i: r.small[i:i + 1, :]
    t = Box(got={})
    def d_act(n):
        if n == 0:
            for q in lwd + [ld.dffo, ld.gate, ld.up]: q.wait()
        d = nt(r.dffo[:, :512], W[0, n:n + 768, :]) + nt(r.dffo[:, 512:], W[1, n:n + 768, :])
        g, u = r.gate[:, n:n + 768].astype(f32), r.up[:, n:n + 768].astype(f32)
        sg = jax.nn.sigmoid(g)
        r.gate[:, n:n + 768] = (d * u * sg * (1.0 + g * (1.0 - sg))).astype(bf)
        r.up[:, n:n + 768] = (d * (g * sg)).astype(bf)
    panels = [[(r.gate, 512 * p, 512, 512 * p)] for p in range(4)] + [[(r.up, FH + 512 * p, 512, 512 * p)] for p in range(4)]
    panels += [[(r.gate, 2048, 256, 2048), (r.up, FH + 2048, 256, 2048)]]
    def fetch(i):
        out, o = [], 0
        for _, cc, n, _ in panels[i % 9]:
            out.append(w.local(I.w2.at[:, pl.ds(cc, n)], slot(i % 4).at[:, pl.ds(o, n)])); o += n
        return out
    def slab(src, yy, base):
        d = tn(r.h2[:, col(256 * yy, 256)], src[...]).astype(bf)
        for xx in range(4):
            for u in (0, 1): grads[2][yy, xx, u, :, base:base + FH] = d[64 * xx + 32 * u:64 * xx + 32 * u + 32]
    def d_gate(i):
        if i == 0:
            t.got.update({p: fetch(p) for p in range(4)})
            ld.h2.wait()
        slab(r.gate, (y + JS[i] + 4) % 4, 0)
        sc.zsend(F.f2a, JS[i])
    def d_up(i):
        slab(r.up, (y + JS[i] + 4) % 4, FH)
        if i == 3:
            for j in JS: sc.zsend(F.f2b, j)
    def panel(i):
        for q in t.got[i]: q.wait()
        rr, acc = ((oth, r.dhs), (own, r.dho))[i // 9]
        o, d = 0, 0
        for nm, _, n, off in panels[i % 9]:
            d = d + nt(nm[rr, off:off + n], slot(i % 4)[:, o:o + n])
            o += n
        acc[...] = d if i % 9 == 0 else acc[...] + d
        if i + 4 < 18: t.got[i + 4] = fetch(i + 4)
        if i == 8: t.dh = w.send(r.dhs, r.dhr, other)
        if i == 17:
            r.h, r.y, r.conv = (r.gate.at[:, pl.ds(a, m)] for a, m in ((0, 1024), (1024, 512), (1536, 512)))
            ld.h, ld.y, ld.conv = w.local(I.h, r.h), w.local(I.y, r.y), w.local(I.conv, r.conv)
            t.win = [w.local(I.w1.at[:, pl.ds(512 * p, 512)], slot(p + 1)) for p in range(3)]
            t.wo = [w.local(I.w1.at[at_rows(512 * c, 512, 512), pl.ds(1536, 512)], slot(0).at[at_rows(512 * c, 512, 512)]),
                w.local(I.wor, slot(0).at[at_rows(512 * (1 - c), 512, 512)])]
            ld.small.wait(); ld.resid.wait()
    def back2():
        t.dh.wait_recv()
        def rows(i, _):
            q = at_rows(i * 64, 64, 64); qo = at_rows(256 * c + i * 64, 64, 64)
            v = r.resid[q, :]
            s2 = lax.rsqrt(jnp.mean(v * v, axis=1, keepdims=True) + EPS)
            d = r.dho[q, :] + r.dhr[q, :]
            r.gsum[1:2, :] += jnp.sum(d * v * s2, axis=0, keepdims=True)
            wt = d * gain(1)
            inner = jnp.mean(wt * v, axis=1, keepdims=True)
            dr = r.dffo[qo, :].astype(f32) + (s2 * wt - v * (s2 * s2 * s2) * inner)
            r.resid[q, :] = dr
            r.h2[qo, :] = dr.astype(bf)
            return 0
        lax.fori_loop(0, 4, rows, 0)
        t.dm = w.send(r.h2.at[own], r.h2.at[own], other)
        for q in (ld.y, ld.ext, ld.conv, ld.bcx, ld.h, ld.tok, ld.keep): q.wait()
        for q in t.wo: q.wait()
    def d_y():
        t.dm.wait_recv()
        d = nt(r.h2[:, :512], slot(0)[0:512, :]) + nt(r.h2[:, 512:], slot(0)[512:1024, :])
        r.dcv[0:512, :] = d * r.bcx[:, 512:1024].astype(f32)
        r.bcx[:, 512:1024] = (d * r.conv[...].astype(f32)).astype(bf)
        t.halo = w.send(r.dcv.at[pl.ds(0, 8)], r.dcv.at[pl.ds(512, 8)], prv)
    def d_out():
        def rows(i, _):
            d = tn(r.y[:, at_rows(256 * i, 256, 256)], r.h2[...]).astype(bf)
            for xx in range(4):
                for u in (0, 1):
                    v = d[64 * xx + 32 * u:64 * xx + 32 * u + 32]
                    r.up[at_rows(256 * i + 64 * xx + 32 * u, 32, 32), 0:512] = jnp.where(c == 0, v[:, 512:], v[:, :512])
                    grads[1][2 * c + i, xx, u, 96:128, :] = jnp.where(c == 0, v[:, :512], v[:, 512:])
            return 0
        lax.fori_loop(0, 2, rows, 0)
        t.do = [w.send(r.up.at[pl.ds(256 * i + 64 * xx + 32 * u, 32), pl.ds(0, 512)], grads[1].at[2 * c + i, xx, u, pl.ds(96, 32), :], other)
            for i in (0, 1) for xx in range(4) for u in (0, 1)]
    def d_taps():
        for q in range(0, 512, 128):
            dv = r.dcv[q:q + 128, :]
            for i in range(3):
                r.gsum[2 + i:3 + i, col(512 * c, 512)] += jnp.sum(dv * r.ext[14 + i + q:142 + i + q, :], axis=0, keepdims=True)
    def d_bx():
        t.halo.wait_recv()
        tap = [r.small[2 + i:3 + i, col(512 * c, 512)] for i in range(3)]
        r.dcv[512:520, :] = r.dcv[512:520, :] * (k < 31).astype(f32)
        for q in range(0, 512, 128):
            dx = tap[2] * r.dcv[q:q + 128, :] + tap[1] * r.dcv[q + 1:q + 129, :] + tap[0] * r.dcv[q + 2:q + 130, :]
            bp, xp = r.bcx[q:q + 128, 0:512].astype(f32), r.bcx[q:q + 128, 1024:1536].astype(f32)
            r.bcx[q:q + 128, 0:512] = (dx * xp).astype(bf)
            r.bcx[q:q + 128, 1024:1536] = (dx * bp).astype(bf)
    def d_in(i):
        if i == 0:
            for q in t.do: q.wait_recv()
        yy = (y + JS[i] + 4) % 4
        d = tn(r.h[:, col(256 * yy, 256)], r.bcx[...]).astype(bf)
        for p in range(3):
            for xx in range(4):
                for u in (0, 1): grads[1][yy, xx, u, 32 * p:32 * p + 32, :] = d[64 * xx + 32 * u:64 * xx + 32 * u + 32, 512 * p:512 * p + 512]
        sc.zsend(F.f1b, JS[i])
        if i == 3:
            for j in JS: sc.zsend(F.f1a, j)
    def d_h():
        t.dh.wait_send()
        for q in t.win: q.wait()
        for rr, acc in ((oth, r.dhs), (own, r.dho)):
            acc[...] = sum(nt(r.bcx[rr, 512 * i:512 * i + 512], slot(i + 1)[...]) for i in range(3))
        t.dh = w.send(r.dhs, r.dhr, other)
        t.act = w_down() + [w.local(I.act, r.gate)]
    def back1():
        t.dh.wait_recv()
        def rows(i, _):
            q = at_rows(i * 64, 64, 64)
            v = r.tok[q, :].astype(f32)
            s1 = lax.rsqrt(jnp.mean(v * v, axis=1, keepdims=True) + EPS)
            d = r.dho[q, :] + r.dhr[q, :]
            r.gsum[0:1, :] += jnp.sum(d * v * s1, axis=0, keepdims=True)
            wt = d * gain(0)
            inner = jnp.mean(wt * v, axis=1, keepdims=True)
            r.dho[q, :] = r.resid[q, :] + (s1 * wt - v * (s1 * s1 * s1) * inner)
            return 0
        lax.fori_loop(0, 4, rows, 0)
        pl.semaphore_signal(free, inc=1, device_id=other, device_id_type=MESH)
        t.tok = w.local(r.dho, O.dtok)
        eye = (lax.broadcasted_iota(jnp.int32, (8, 128), 0) == lax.broadcasted_iota(jnp.int32, (8, 128), 1)).astype(f32).astype(bf)
        sm = tn(r.gsum[...].astype(bf), eye).astype(bf)
        for yy in range(4):
            for xx in range(4):
                for u in (0, 1):
                    o = 256 * yy + 64 * xx + 32 * u
                    grads[0][yy, xx, u] = sm[o:o + 32]
        t.dh.wait_send()
    def ffo():
        for q in t.act: q.wait()
        t.tok.wait()
        t.resid = w.local(I.resid, r.resid)
        for rr, acc in ((oth, r.dhs), (own, r.dho)):
            for i in (0, 1): acc[:, 512 * i:512 * i + 512] = dot(r.gate[rr, :], W[i])
        pl.semaphore_wait(free, 1)
        t.dh = w.send(r.dhs, r.dhr, other)
    def mixed():
        t.dh.wait_recv(); t.resid.wait()
        r.tok[...] = (r.keep[...] * (r.resid[...] + (r.dho[...] + r.dhr[...]))).astype(bf)
        w.local(r.tok, O.mixed)
    each = functools.partial
    chunks = [each(d_act, n) for n in (0, 768, 1536)] + [each(d_gate, i) for i in range(4)] + [each(d_up, i) for i in range(4)]
    chunks += [each(panel, i) for i in range(18)] + [back2, d_y, d_out, d_taps, d_bx] + [each(d_in, i) for i in range(4)] + [d_h, back1, ffo, mixed]
    half = 512 * c
    at_in = lambda o: [(32 * p, 0, 256, O.din, 1024 * p + half + o) for p in range(3)] + [(96, 0, 256, O.dout, half + o)]
    ends = [at_in(0), at_in(256), [(0, 0, 128, O.ds.at[c], None)], [(0, 0, FH, O.dg, FH * c)], [(0, 0, FH, O.du, FH * c)],
        [(0, 0, 256, O.dd, half)], [(0, 0, 256, O.dd, half + 256)]]
    flows = list(vars(F).values())
    moves = (sc.first, sc.second, sc.third, sc.last1)
    for what, *where in ORDER_B:
        if not where: chunks[what]()
        elif what < 3: moves[what](flows[where[0]], where[1])
        elif what < 4: moves[what](flows[where[0]])
        else: sc.last2(flows[where[0]], ends[where[0]])
    w.drain()

def backward_all(a, tokens, keep):
    a = Box(a)
    a.ddown = a.ddown.reshape(4, 4, 2, 144, 512)
    scr = [*B_SCR.values()] + GRADS + GRADS + [v for t in RFLOWS.values() for v in flow_scratch(t)]
    outs = call(backward_kernel, [*B_OUT.values()], scr, 2, 63, [pltpu.SemaphoreType.REGULAR], *vars(a).values(), tokens, keep)
    return Box(dict(zip(B_OUT, outs)))

def finish_kernel(*refs):
    n = len(refs) // 4
    src, dst, held, sems = refs[:n], refs[n:2 * n], refs[2 * n:3 * n], refs[3 * n:]
    ins = [pltpu.make_async_copy(a, v, s) for a, v, s in zip(src, held, sems)]
    for cp in ins: cp.start()
    outs = [pltpu.make_async_copy(v, d, s) for v, d, s in zip(held, dst, sems)]
    for a, d in zip(ins, outs): a.wait(); d.start()
    for d in outs: d.wait()

def finish_all(*args):
    hbm = pl.BlockSpec(memory_space=pl.ANY)
    n = len(args)
    return pl.pallas_call(
        finish_kernel, out_shape=tuple(jax.ShapeDtypeStruct(v.shape, v.dtype) for v in args), in_specs=[hbm] * n, out_specs=(hbm,) * n,
        scratch_shapes=[pltpu.VMEM(v.shape, v.dtype) for v in args] + [pltpu.SemaphoreType.DMA] * n,
        compiler_params=pltpu.CompilerParams(vmem_limit_bytes=16 * 2**20))(*args)


def body(tokens, lengths, norm1_gain, in_proj, conv_weight, out_proj, norm2_gain, w_gate, w_up, w_down, cotangent):
    rows = tokens.shape[0]
    place = lax.axis_index("shard")
    slot = lax.axis_index("rep")
    slot_ids = jnp.arange(lengths.shape[0], dtype=jnp.int32)
    length = jnp.sum(jnp.where(slot_ids == slot, lengths, 0))
    valid = jnp.clip(length - place * rows, 0, rows)
    keep = (jnp.arange(rows, dtype=jnp.int32) < valid).astype(jnp.float32)[:, None]
    a = forward_all(tokens, cotangent, keep, in_proj, out_proj, smalls(norm1_gain, norm2_gain, conv_weight), w_gate, w_up, w_down)
    b = backward_all(a, tokens, keep)
    sm = b.ds[0] + b.ds[1]
    mixed, dtok, din, dout, dg, du, dd = finish_all(b.mixed, b.dtok, b.din, b.dout, b.dg, b.du, b.dd)
    return mixed, dtok, sm[:, 0], din, sm[:, 2:5].T, dout, sm[:, 1], dg, du, dd

def solution(mesh):
    tok = P(("rep", "shard"), None)
    par = (P("shard"), P("shard", None), P(None, "shard"), P("shard", None), P("shard"), P("shard", None), P("shard", None), P("shard", None))
    return jax.shard_map(body, mesh=mesh, in_specs=(tok, P()) + par + (tok,), out_specs=(tok, tok) + par, check_vma=False)
```

```python
ORDER_A = (
    (0, 1), (0, 0), (0, 2), (0, 3), (1, 0), (1, 1), (2, 0), (4, 0, 0), (2, 1), (4, 1, 0), (3, 0), (4, 0, -1), (4, 1, -1), (4, 0, 1), (5, 0, 0),
    (4, 1, 1), (3, 1), (5, 1, 0), (4, 0, 2), (5, 1, -1), (1, 2), (1, 3), (5, 0, -1), (5, 1, 1), (5, 0, 1), (5, 0, 2), (4, 1, 2), (2, 2), (4, 2, 0),
    (4, 3, 0), (2, 3), (5, 1, 2), (3, 2), (5, 3, 0), (4, 2, -1), (4, 3, -1), (0, 5), (0, 4), (4, 2, 1), (0,), (5, 2, 0), (4, 3, 1), (3, 3), (1,),
    (5, 3, -1), (2,), (3,), (4, 2, 2), (5, 3, 1), (5, 2, -1), (1, 4), (1, 5), (4,), (5,), (6,), (4, 3, 2), (5, 2, 1), (4, 4, 0), (7,), (2, 5),
    (5, 2, 2), (2, 4), (5, 3, 2), (4, 5, 0), (5, 4, 0), (8,), (3, 5), (9,), (4, 5, -1), (10,), (4, 4, -1), (11,), (4, 5, 1), (12,), (3, 4), (13,),
    (5, 5, 0), (4, 4, 1), (14,), (5, 4, -1), (15,), (16,), (4, 5, 2), (4, 4, 2), (17,), (5, 5, -1), (18,), (5, 5, 1), (5, 4, 1), (5, 5, 2), (5, 4, 2),)
ORDER_B = (
    (0, 5, -1), (0, 5, 2), (0, 6, -1), (0, 6, 2), (0, 5, 0), (0, 5, 1), (0, 6, 0), (0, 6, 1), (0,), (1,), (1, 6, -1), (1, 5, -1), (2,), (1, 6, 2),
    (1, 6, 0), (1, 5, 2), (1, 5, 0), (3,), (1, 6, 1), (1, 5, 1), (4,), (5,), (6,), (7,), (8,), (9,), (10,), (11,), (2, 6, 2), (2, 5, 2), (12,), (13,),
    (14,), (15,), (16,), (17,), (18,), (19,), (2, 6, 0), (2, 5, 0), (0, 3, 2), (20,), (21,), (22,), (23,), (24,), (25,), (0, 4, 2), (26,), (27,),
    (28,), (2, 6, -1), (2, 6, 1), (2, 5, -1), (2, 5, 1), (29,), (0, 4, -1), (0, 3, -1), (1, 4, 2), (1, 3, 2), (30,), (31,), (3, 6), (3, 5), (0, 4, 1),
    (32,), (1, 3, -1), (1, 4, -1), (0, 3, 1), (33,), (0, 4, 0), (34,), (35,), (2, 3, 2), (36,), (2, 4, 2), (37,), (38,), (1, 4, 1), (4, 6), (0, 3, 0),
    (4, 5), (1, 3, 1), (39,), (2, 4, -1), (0, 1, 2), (0, 2, -1), (0, 2, 2), (0, 2, 0), (0, 2, 1), (40,), (0, 0, 2), (1, 4, 0), (2, 3, -1), (1, 3, 0),
    (0, 1, -1), (41,), (2, 3, 1), (0, 0, -1), (2, 4, 1), (1, 0, 2), (0, 1, 1), (1, 1, 2), (1, 2, -1), (1, 2, 2), (1, 2, 0), (1, 2, 1), (0, 0, 1),
    (2, 4, 0), (0, 1, 0), (2, 3, 0), (1, 1, -1), (3, 4), (0, 0, 0), (1, 1, 1), (3, 3), (2, 1, 2), (1, 0, -1), (2, 2, 2), (2, 2, 0), (2, 0, 2),
    (1, 1, 0), (1, 0, 1), (1, 0, 0), (2, 1, -1), (2, 1, 1), (2, 0, -1), (2, 2, -1), (2, 2, 1), (2, 0, 1), (2, 1, 0), (4, 4), (2, 0, 0), (3, 1),
    (3, 2), (3, 0), (4, 3), (4, 1), (4, 2), (4, 0),)

import functools
import jax, jax.numpy as jnp
from jax import lax
from jax.experimental import pallas as pl
from jax.experimental.pallas import tpu as pltpu
from jax.sharding import PartitionSpec as P
MESH = pl.DeviceIdType.MESH
EPS = 1e-05
bf, f32 = jnp.bfloat16, jnp.float32
C1 = 2176; HALF = 1152; CAT = 6784; UNIT = 32; DUNIT = 144; FH = 2304
COPIES = 272
JS = (2, -1, 1, 0)
PAIR, CROSS, X, Y = 1, 2, 0, 1
ONE, TWO, THREE = 1, 2, 3
XY, YX = (X, Y), (Y, X)
class Box:
    def __init__(self, *a, **kw):
        for d in a: self.__dict__.update(d)
        self.__dict__.update(kw)

FLOWS = dict(
    f1a=Box(kind=1, base=0, step=384, gw=640, fw=384, to=PAIR, order=XY),
    f1b=Box(kind=1, base=1024, step=384, gw=768, fw=384, to=CROSS, order=YX),
    f2a=Box(kind=2, base=0, step=768, gw=1536, fw=768, to=PAIR, order=YX),
    f2b=Box(kind=2, base=2304, step=768, gw=1536, fw=768, to=CROSS, order=XY),
    f3a=Box(kind=3, base=0, step=0, gw=256, fw=0, to=None, order=XY),
    f3b=Box(kind=3, base=256, step=0, gw=256, fw=0, to=None, order=YX))

def spot():
    rep = lax.axis_index("rep"); s = lax.axis_index("shard")
    return (s // 4) % 4, s // 16, ((s // 2) % 2) * 2 + rep, s % 2

def device(x, y, z, c):
    return (z % 2, ((y * 4 + x) * 2 + z // 2) * 2 + c)

def moved(x, y, z, c, axis, step):
    if axis == X: return device((x + step + 4) % 4, y, z, c)
    return device(x, (y + step + 4) % 4, z, c)

def along(x, y, z, c, step):
    k = ((y * 4 + x) * 2 + z // 2 + step + 32) % 32
    return device((k // 2) % 4, k // 8, (k % 2) * 2 + z % 2, c)

def greet(devices):
    bar = pltpu.get_barrier_semaphore()
    for d in devices:
        pl.semaphore_signal(bar, inc=1, device_id=d, device_id_type=MESH)
    return len(devices)

def met(count): pl.semaphore_wait(pltpu.get_barrier_semaphore(), count)

class Copy:
    def __init__(self, cp): self.cp, self.here, self.gone = cp, False, False
    def wait_recv(self): self.cp.wait_recv(); self.here = True
    def wait_send(self): self.cp.wait_send(); self.gone = True

class Near:
    def __init__(self, cp): self.cp, self.here = cp, False
    def wait(self): self.cp.wait(); self.here = True

class Wire:
    def __init__(self, ss, rs, ls): self.ss, self.rs, self.ls, self.sent, self.near = ss, rs, ls, [], []
    def send(self, src, dst, dev):
        i = len(self.sent)
        cp = pltpu.make_async_remote_copy(src_ref=src, dst_ref=dst, send_sem=self.ss.at[i], recv_sem=self.rs.at[i], device_id=dev, device_id_type=MESH)
        cp.start(); self.sent.append(Copy(cp)); return self.sent[-1]
    def local(self, src, dst):
        cp = pltpu.make_async_copy(src, dst, self.ls.at[len(self.near)])
        cp.start(); self.near.append(Near(cp)); return self.near[-1]
    def drain(self):
        for cp in self.near:
            if not cp.here: cp.wait()
        for cp in self.sent:
            if not cp.here: cp.wait_recv()
            if not cp.gone: cp.wait_send()

def at_rows(v, n, m=16): return pl.ds(pl.multiple_of(v, m), n)

class All:
    def __init__(self, *q): self.q = q
    def wait_recv(self):
        for q in self.q: q.wait_recv()

class Gather:
    def __init__(self, w, go, pair, cross, other, x, y, z, w1, w2, wd, wdr):
        self.w, self.go, self.x, self.y, self.other, self.wdr, self.hi = w, go, x, y, other, wdr, z // 2
        self.f = Box()
        for n, t in FLOWS.items():
            sel = {PAIR: z % 2, CROSS: z // 2, None: 0}[t.to]
            d = t.kind == 3
            vars(self.f)[n] = Box(vars(t), buf=(w1, w2, wd)[t.kind - 1], unit=DUNIT if d else UNIT, mine=(t.base + t.step * sel, t.gw),
                alone=(t.base + t.gw * sel, t.fw), dev={PAIR: pair, CROSS: cross, None: None}[t.to], z=[], p={}, m={}, p2={}, m2={})
    def block(self, f, da, db, unit=None, cols=None, buf=None):
        a, b = f.order
        pos = {X: self.x, Y: self.y}
        pos[a] = (pos[a] + da + 4) % 4
        pos[b] = (pos[b] + db + 4) % 4
        u = f.unit
        row = (pos[Y] * 4 + pos[X]) * (2 * u)
        n = 2 * u
        if unit is not None: row, n = row + unit * u, u
        col, width = cols or f.mine
        return (f.buf if buf is None else buf).at[at_rows(row, n), pl.ds(col if isinstance(col, int) else pl.multiple_of(col, 128), width)]
    def push(self, f, da, db, dev, unit=None):
        v = self.block(f, da, db, unit)
        return self.w.send(v, v, dev)
    def fwd(self, f, da, db):
        if f.dev is not None and (da or db):
            v = self.block(f, da, db, None, f.alone)
            f.z.append(self.w.send(v, v, f.dev))
        if f.kind == 3: f.z.append(self.w.send(self.block(f, da, db), self.block(f, da, db, None, None, self.wdr), self.other))
    def open2(self, f, j):
        b = f.order[1]
        f.p[j] = self.push(f, j, 0, self.go[(b, 1)])
        f.m[j] = self.push(f, j, 0, self.go[(b, -1)])
    def r1(self, f, own):
        a, b = f.order
        u = self.hi if own else 1 - self.hi
        new = [self.push(f, 0, 0, self.go[(d, st)], u) for d in (a, b) for st in (1, -1)]
        if own: f.half = new
        else:
            f.p[None], f.m[None], f.p[0], f.m[0] = (All(*q) for q in zip(f.half, new))
            self.fwd(f, 0, 0)
    def r2(self, f):
        a = f.order[0]
        f.p[None].wait_recv(); f.p2[None] = self.push(f, -1, 0, self.go[(a, 1)], 0)
        f.m[None].wait_recv(); f.m2[None] = self.push(f, 1, 0, self.go[(a, -1)], 1)
        self.open2(f, -1); self.open2(f, 1)
        self.fwd(f, -1, 0); self.fwd(f, 1, 0)
    def r3(self, f):
        f.p2[None].wait_recv(); f.m2[None].wait_recv()
        self.open2(f, 2); self.fwd(f, 2, 0)
    def r4(self, f, j):
        b = f.order[1]
        f.p[j].wait_recv(); f.p2[j] = self.push(f, j, -1, self.go[(b, 1)], 0)
        f.m[j].wait_recv(); f.m2[j] = self.push(f, j, 1, self.go[(b, -1)], 1)
        self.fwd(f, j, -1); self.fwd(f, j, 1)
    def r5(self, f, j):
        f.p2[j].wait_recv(); f.m2[j].wait_recv()
        self.fwd(f, j, 2)
    def all_here(self, f):
        for q in f.z: q.wait_recv()

def dot(a, b): return jnp.dot(a, b, preferred_element_type=f32)
def tn(a, b): return lax.dot_general(a, b, (((0,), (0,)), ((), ())), preferred_element_type=f32)
def nt(a, b): return lax.dot_general(a, b, (((1,), (1,)), ((), ())), preferred_element_type=f32)

A_GOT = dict(w1=((1024, C1), bf), w2=((1024, 2 * FH), bf), wd=((4608, 512), bf), wor=((512, 512), bf), wdr=((4608, 512), bf), ddown=((4608, 512), bf))
A_MADE = dict(h=((512, 1024), bf), bcx=((512, 1536), bf), ext=((528, 512), f32), conv=((512, 512), bf), y=((512, 512), bf),
    resid=((256, 1024), f32), h2=((512, 1024), bf), gate=((512, FH), bf), up=((512, FH), bf), act=((512, FH), bf),
    dffo=((512, 1024), bf), small=((8, 1024), f32), keep=((256, 1), f32))
A_SCR = dict(T=((512, 1024), bf), cotv=((256, 1024), bf), win=((1024, 1536), bf), wo=((512, 1024), bf), wsm=((1024, 128), bf),
    w2=((1024, 2 * FH), bf), gf=((512, FH), f32), cpart=((512, 512), f32), mixs=((256, 1024), f32), mixr=((256, 1024), f32),
    dnf=((DUNIT, 512), f32), dns=((72, 512), f32), dnb=((DUNIT, 512), bf), ddn=((2, FH, 512), bf),
    inp=((16, 3072), bf), outp=((16, 1024), bf), sml=((16, 128), bf), srow=((16, 128), bf), wgs=((16, 4608), bf), wus=((16, 4608), bf), wds=((72, 1024), bf))

def named(groups, refs):
    refs, out = list(refs), []
    for g in groups:
        out.append(Box(dict(zip(g, refs)))); refs = refs[len(g):]
    return out, refs

def forward_kernel(*refs):
    A_IN = dict(lengths=0, tokens=0, cot=0, inp=0, outp=0, sml=0, wgs=0, wus=0, wds=0)
    (I, O, M, V, S), (ss, rs, ls) = named([A_IN, A_GOT, A_MADE, A_MADE, A_SCR], refs)
    w1, w2, wd, wor, wdr = O.w1, S.w2, O.wd, O.wor, O.wdr
    x, y, z, c = spot()
    hi = z // 2
    s = ((y * 4 + x) * 2 + hi) * 2 + c
    k = s // 2
    pair = device(x, y, z + 1 - 2 * (z % 2), c)
    cross = device(x, y, 3 - z, c)
    other = device(x, y, z, 1 - c)
    nxt, prv = along(x, y, z, c, 1), along(x, y, z, c, -1)
    go = {(a, st): moved(x, y, z, c, a, st) for a in XY for st in (1, -1)}
    count = greet(list(go.values()) + [pair, cross, other, nxt, prv])
    w = Wire(ss, rs, ls)
    own, oth = at_rows(256 * c, 256, 256), at_rows(256 * (1 - c), 256, 256)
    col = lambda p, n: pl.ds(pl.multiple_of(p, 128), n)
    lds = w.local(I.wds, S.wds)
    lrow = w.local(I.sml, S.srow)
    lin = [w.local(a, b) for a, b in ((I.inp, S.inp), (I.outp, S.outp), (I.wgs, S.wgs), (I.wus, S.wus))]
    lcot = [w.local(I.cot, S.cotv)]
    ltok = w.local(I.tokens, S.T.at[own])
    lrow.wait()
    eye = (lax.broadcasted_iota(jnp.int32, (16, 128), 0) == lax.broadcasted_iota(jnp.int32, (16, 128), 1)).astype(f32).astype(bf)
    S.sml[...] = tn(S.srow[...], eye)[0:16].astype(bf)
    met(count)
    rows = at_rows(16 * s, 16)
    pieces = [(I.inp, S.inp, 1024 * i, 512, w1, 512 * i) for i in range(3)] + [(I.outp, S.outp, 0, 512, w1, 1536), (I.wgs, S.wgs, 0, FH, w2, 0), (I.wus, S.wus, 0, FH, w2, FH)]
    got = [w.send(S.sml, w1.at[rows, pl.ds(2048, 128)], other)]
    for src, _, a, n, to, d in pieces: got.append(w.send(src.at[:, col(a + n * (1 - c), n)], to.at[rows, pl.ds(d, n)], other))
    for q in lin: q.wait()
    mine = [w.local(S.sml, w1.at[rows, pl.ds(2048, 128)])]
    for _, src, a, n, to, d in pieces: mine.append(w.local(src.at[:, col(a + n * c, n)], to.at[rows, pl.ds(d, n)]))
    lds.wait()
    S.dns[...] = S.wds[:, col(512 * (1 - c), 512)].astype(f32)
    gdn = w.send(S.dns, S.dnf.at[at_rows(72 * c, 72, 8)], other)
    S.dnf[at_rows(72 * c, 72, 8), :] = S.wds[:, col(512 * c, 512)].astype(f32)
    gtok = w.send(I.tokens, S.T.at[own], other)
    g = Gather(w, go, pair, cross, other, x, y, z, w1, w2, wd, wdr)
    F = g.f
    for q in mine: q.wait()
    for q in got: q.wait_recv()
    urow, drow = at_rows(UNIT * k, UNIT, UNIT), at_rows(DUNIT * k, DUNIT)
    z1 = w.send(w1.at[urow], w1.at[urow], cross)
    z2, z2b = (w.send(w2.at[urow, pl.ds(n, FH)], w2.at[urow, pl.ds(n, FH)], cross) for n in (0, FH))
    gdn.wait_recv()
    S.dnb[...] = S.dnf[...].astype(bf)
    lwd = w.local(S.dnb, wd.at[drow, :])
    for q in lcot: q.wait()
    valid = I.lengths[lax.axis_index("rep")] - 256 * s
    V.keep[...] = (lax.broadcasted_iota(jnp.int32, (256, 1), 0) < valid).astype(f32)
    V.dffo[own, :] = (V.keep[...] * S.cotv[...].astype(f32)).astype(bf)
    gdf = w.send(V.dffo.at[own], V.dffo.at[own], other)
    ltok.wait(); gtok.wait_recv(); lwd.wait()
    t = Box()
    def save(**kw):
        for n in kw: w.local(vars(V)[n], vars(M)[n])
    def one():
        for f in (F.f1a, F.f1b): g.all_here(f)
        l1 = w.local(w1.at[:, pl.ds(2048, 128)], S.wsm)
        t.win = w.local(w1.at[:, pl.ds(0, 1536)], S.win)
        t.wor = w.send(w1.at[at_rows(512 * (1 - c), 512, 512), pl.ds(1536, 512)], wor, other)
        t.wo = w.local(w1.at[at_rows(512 * c, 512, 512), pl.ds(1536, 512)], S.wo.at[:, col(512 * c, 512)])
        l1.wait()
        V.small[...] = nt(eye, S.wsm[...])[0:8]
    def norm1():
        def rows(i, _):
            q = at_rows(i * 64, 64, 64)
            v = S.T[q, :].astype(f32)
            sc = lax.rsqrt(jnp.mean(v * v, axis=1, keepdims=True) + EPS)
            V.h[q, :] = (v * sc * V.small[0:1, :]).astype(bf)
            return 0
        lax.fori_loop(0, 8, rows, 0)
        t.win.wait()
    ext = V.ext
    def b_x():
        for n in (0, 256):
            b_ = dot(V.h[...], S.win[:, n:n + 256])
            x_ = dot(V.h[...], S.win[:, 1024 + n:1280 + n])
            V.bcx[:, n:n + 256] = b_.astype(bf)
            V.bcx[:, 1024 + n:1280 + n] = x_.astype(bf)
            ext[16:528, n:n + 256] = (b_ * x_).astype(bf).astype(f32)
        t.halo = w.send(ext.at[pl.ds(520, 8)], ext.at[pl.ds(8, 8)], nxt)
        t.wor.wait_recv()
        t.wo2 = w.local(wor, S.wo.at[:, col(512 * (1 - c), 512)])
    def c_():
        for n in (0, 256):
            v = dot(V.h[...], S.win[:, 512 + n:768 + n])
            S.cpart[:, n:n + 256] = v
            V.bcx[:, 512 + n:768 + n] = v.astype(bf)
        save(h=1, bcx=1, small=1)
    def conv():
        t.halo.wait_recv()
        ext[8:16, :] = ext[8:16, :] * (k > 0).astype(f32)
        t0, t1, t2 = (V.small[2 + i:3 + i, col(512 * c, 512)] for i in range(3))
        for q in range(0, 512, 128):
            cv = t0 * ext[14 + q:142 + q, :] + t1 * ext[15 + q:143 + q, :] + t2 * ext[16 + q:144 + q, :]
            V.conv[q:q + 128, :] = cv.astype(bf)
            V.y[q:q + 128, :] = (S.cpart[q:q + 128, :] * cv).astype(bf)
        t.wo.wait(); t.wo2.wait()
    def mix():
        S.mixs[...] = dot(V.y[oth, :], S.wo[...])
        t.mix = w.send(S.mixs, S.mixr, other)
    def mix2():
        V.resid[...] = dot(V.y[own, :], S.wo[...])
        save(ext=1, conv=1, y=1)
    def norm2():
        t.mix.wait_recv()
        def rows(i, _):
            q, qo = at_rows(i * 64, 64, 64), at_rows(256 * c + i * 64, 64, 64)
            v = S.T[qo, :].astype(f32) + (V.resid[q, :] + S.mixr[q, :])
            V.resid[q, :] = v
            sc = lax.rsqrt(jnp.mean(v * v, axis=1, keepdims=True) + EPS)
            V.h2[qo, :] = (v * sc * V.small[1:2, :]).astype(bf)
            return 0
        lax.fori_loop(0, 4, rows, 0)
        t.h2 = w.send(V.h2.at[own], V.h2.at[own], other)
        save(resid=1)
    def two():
        g.all_here(F.f2a)
        w.local(w2.at[:, pl.ds(0, FH)], O.w2.at[:, pl.ds(0, FH)])
        t.h2.wait_recv(); gdf.wait_recv()
        save(h2=1, dffo=1, keep=1)
    def gate(i):
        n = 768 * i
        v = dot(V.h2[...], w2[:, n:n + 768])
        S.gf[:, n:n + 768] = v * jax.nn.sigmoid(v)
        V.gate[:, n:n + 768] = v.astype(bf)
    def up_here():
        g.all_here(F.f2b)
        w.local(w2.at[:, pl.ds(FH, FH)], O.w2.at[:, pl.ds(FH, FH)])
        save(gate=1)
    def up(i):
        n = 768 * i
        g_, u_ = S.gf[:, n:n + 768], dot(V.h2[...], w2[:, FH + n:FH + n + 768])
        V.up[:, n:n + 768] = u_.astype(bf)
        V.act[:, n:n + 768] = (g_ * u_).astype(bf)
        if i == 2: save(up=1, act=1)
    def down(i):
        def rows(m, _):
            q = at_rows(768 * i + m * 256, 256, 256)
            v = tn(V.act[:, q], V.dffo[...]).astype(bf)
            S.ddn[0, q, :] = v[:, :512]
            S.ddn[1, q, :] = v[:, 512:]
            return 0
        lax.fori_loop(0, 3, rows, 0)
        to = at_rows(FH * c + 768 * i, 768, 256)
        w.send(S.ddn.at[1 - c, pl.ds(768 * i, 768)], O.ddown.at[to, :], other)
        w.local(S.ddn.at[c, pl.ds(768 * i, 768)], O.ddown.at[to, :])
    each = functools.partial
    chunks = [one, norm1, b_x, c_, conv, mix, mix2, norm2, two] + [each(gate, i) for i in range(3)] + [up_here] + [each(up, i) for i in range(3)] + [each(down, i) for i in range(3)]
    flows = list(vars(F).values())
    moves = (g.r1, g.r1, g.r2, g.r3, g.r4, g.r5)
    need = {0: z1, 1: z1, 2: z2, 3: z2b}
    for what, *where in ORDER_A:
        if not where: chunks[what](); continue
        f = flows[where[0]]
        if what == 0 and where[0] > 3 and 4 not in need: need[4] = need[5] = w.send(S.dnb, wd.at[drow, :], cross)
        if what == 1 and not need[where[0]].here: need[where[0]].wait_recv()
        if what < 2: g.r1(f, what == 0)
        else: moves[what](f, *where[1:])
    w.drain()

def call(kernel, outs, scratch, ident, limit, extra, first, *args):
    hbm = pl.BlockSpec(memory_space=pl.ANY)
    return pl.pallas_call(
        kernel, out_shape=tuple(jax.ShapeDtypeStruct(*v) for v in outs), in_specs=[first] + [hbm] * (len(args) - 1), out_specs=(hbm,) * len(outs),
        scratch_shapes=[pltpu.VMEM(*v) for v in scratch] + [pltpu.SemaphoreType.DMA((n,)) for n in (COPIES, COPIES, 96)] + extra,
        compiler_params=pltpu.CompilerParams(collective_id=ident, has_side_effects=True, vmem_limit_bytes=limit * 2**20))(*args)

def forward_all(*args):
    outs = call(forward_kernel, [*A_GOT.values(), *A_MADE.values()], [*A_MADE.values(), *A_SCR.values()], 1, 60, [], pl.BlockSpec(memory_space=pltpu.SMEM), *args)
    return dict(zip([*A_GOT, *A_MADE], outs))

def smalls(norm1_gain, norm2_gain, conv_weight):
    return jnp.pad(jnp.concatenate([norm1_gain[None], norm2_gain[None], conv_weight]), ((0, 11), (0, 112)))


RFLOWS = dict(
    f1a=Box(kind=1, base=0, step=128, gw=128, fw=128, to=PAIR, order=XY),
    f1b=Box(kind=1, base=256, step=128, gw=128, fw=128, to=CROSS, order=YX),
    f1s=Box(kind=0, base=0, step=0, gw=128, fw=0, to=None, order=YX),
    f2a=Box(kind=2, base=0, step=640, gw=1664, fw=640, to=PAIR, order=YX),
    f2b=Box(kind=2, base=2304, step=384, gw=1920, fw=384, to=CROSS, order=XY),
    f3a=Box(kind=3, base=0, step=0, gw=256, fw=0, to=None, order=XY),
    f3b=Box(kind=3, base=256, step=0, gw=256, fw=0, to=None, order=YX))
UNITS, WIDTH = (32, 128, 32, 144), (128, 512, 2 * FH, 512)
B_OUT = dict(mixed=((256, 1024), bf), dtok=((256, 1024), f32), din=((16, 3072), f32), dout=((16, 1024), f32),
    dg=((16, 4608), f32), du=((16, 4608), f32), dd=((72, 1024), f32), ds=((2, 16, 128), f32))
GRADS = [((4, 4, 2, u, n), bf) for u, n in zip(UNITS, WIDTH)]
def flow_scratch(t):
    u = UNITS[t.kind]
    return [((6, u, t.gw), bf), ((3, u, t.gw), bf), ((u, t.gw + t.fw), f32)]
B_SCR = dict(W=((2, FH, 512), bf), gate=((512, FH), bf), up=((512, FH), bf), dffo=((512, 1024), bf), h2=((512, 1024), bf),
    bcx=((512, 1536), bf), ext=((528, 512), f32), resid=((256, 1024), f32), small=((8, 1024), f32),
    tok=((256, 1024), bf), dhs=((256, 1024), f32), dhr=((256, 1024), f32), dho=((256, 1024), f32), dcv=((520, 512), f32),
    gsum=((8, 1024), f32), keep=((256, 1), f32))

def add_into(dst, srcs, rows, step=16):
    def body(i, _):
        r = pl.ds(pl.multiple_of(i * step, step), step)
        if len(srcs) == 1: dst[r, :] = dst[r, :] + srcs[0][r, :]
        else:
            v = dst[r, :].astype(f32)
            for q in srcs: v = v + q[r, :].astype(f32)
            dst[r, :] = v.astype(bf)
        return 0
    lax.fori_loop(0, rows // step, body, 0)

class Scatter:
    def __init__(self, w, go, pair, cross, far, x, y, z, c, other, grads, lands, bufs):
        self.w, self.go, self.x, self.y, self.z, self.c, self.other = w, go, x, y, z, c, other
        self.hi, self.zl = z // 2, z % 2
        self.f = Box()
        for i, (n, t) in enumerate(RFLOWS.items()):
            sel = {PAIR: (self.zl + self.hi) % 2, CROSS: self.hi, None: 0}[t.to]
            k = t.kind
            f = Box(vars(t), G=grads[k], L=lands[k], u=UNITS[k], sel=sel, col=t.base + t.step * sel, out=[],
                ecol=t.base + t.gw * sel, pcol=t.base + t.gw * (1 - sel), dev={PAIR: pair, CROSS: cross, None: None}[t.to],
                A={}, s={}, t={}, s2={}, t2={})
            f.M, f.E, f.F = bufs[3 * i:3 * i + 3]
            vars(self.f)[n] = f
        self.pair, self.cross, self.far = pair, cross, far
    def cols(self, c, n): return pl.ds(c if isinstance(c, int) else pl.multiple_of(c, 128), n)
    def at(self, f, da, db):
        a, b = f.order
        pos = {X: self.x, Y: self.y}
        pos[a] = (pos[a] + da + 4) % 4
        pos[b] = (pos[b] + db + 4) % 4
        return pos[Y], pos[X]
    def part(self, ref, f, p, u=None):
        if u is None: return ref.at[p[0], p[1], :, :, self.cols(f.col, f.gw)]
        return ref.at[p[0], p[1], u, :, self.cols(f.col, f.gw)]
    def zline(self, ref, f, j, col):
        l = self.at(f, j, 0)
        cs = self.cols(col, f.fw)
        return ref.at[l[0], :, :, :, cs] if f.order[0] == Y else ref.at[:, l[1], :, :, cs]
    def zsend(self, f, j):
        f.A[j] = self.w.send(self.zline(f.G, f, j, f.pcol), self.zline(f.L, f, j, f.ecol), f.dev)
    def first(self, f, j):
        b = f.order[1]
        if f.to:
            f.A[j].wait_recv()
            g, l = self.zline(f.G, f, j, f.ecol), self.zline(f.L, f, j, f.pcol)
            for i in range(4):
                for u in (0, 1): add_into(g.at[i, u], [l.at[i, u]], f.u)
        p = self.at(f, j, 2)
        f.s[j] = self.w.send(self.part(f.G, f, p, 0), self.part(f.L, f, p, 0), self.go[(b, 1)])
        f.t[j] = self.w.send(self.part(f.G, f, p, 1), self.part(f.L, f, p, 1), self.go[(b, -1)])
    def second(self, f, j):
        b, u = f.order[1], f.u
        f.s[j].wait_recv(); p = self.at(f, j, 1)
        add_into(self.part(f.G, f, p, 0), [self.part(f.L, f, p, 0)], u)
        f.s2[j] = self.w.send(self.part(f.G, f, p), self.part(f.L, f, p), self.go[(b, 1)])
        f.t[j].wait_recv(); p = self.at(f, j, -1)
        add_into(self.part(f.G, f, p, 1), [self.part(f.L, f, p, 1)], u)
        f.t2[j] = self.w.send(self.part(f.G, f, p), self.part(f.L, f, self.at(f, j, 1)), self.go[(b, -1)])
    def third(self, f, j):
        a, u, M = f.order[0], f.u, f.M
        f.s2[j].wait_recv(); f.t2[j].wait_recv()
        p = self.at(f, j, 0); o = self.at(f, j, 2)
        for v in (0, 1): add_into(self.part(f.G, f, p, v), [self.part(f.L, f, p, v), self.part(f.L, f, o, v)], u)
        if j == 2:
            f.c = self.w.send(self.part(f.G, f, p, 0), M.at[0], self.go[(a, 1)])
            f.d = self.w.send(self.part(f.G, f, p, 1), M.at[1], self.go[(a, -1)])
        elif j == 1:
            f.c.wait_recv(); add_into(self.part(f.G, f, p, 0), [M.at[0]], u)
            f.c2 = self.w.send(self.part(f.G, f, p), M.at[pl.ds(2, 2)], self.go[(a, 1)])
        elif j == -1:
            f.d.wait_recv(); add_into(self.part(f.G, f, p, 1), [M.at[1]], u)
            f.d2 = self.w.send(self.part(f.G, f, p), M.at[pl.ds(4, 2)], self.go[(a, -1)])
    def last1(self, f):
        u, M, me = f.u, f.M, (self.y, self.x)
        f.c2.wait_recv(); f.d2.wait_recv()
        for v in (0, 1): add_into(self.part(f.G, f, me, v), [M.at[2 + v], M.at[4 + v]], u)
        away = self.part(f.G, f, me, 1 - self.hi)
        f.e = [self.w.send(self.part(f.G, f, me, self.hi), f.E.at[0], self.pair), self.w.send(away, f.E.at[1], self.cross), self.w.send(away, f.E.at[2], self.far)]
    def last2(self, f, targets):
        E, F, gw, fw, sel = f.E, f.F, f.gw, f.fw, f.sel
        for q in f.e: q.wait_recv()
        G = f.G.at[self.y, self.x, self.hi]
        same, two = (1, (0, 2)) if f.to == PAIR else (0, (1, 2))
        def mine(o, n): return G[:, self.cols(o + f.col, n)].astype(f32) + E[same, :, self.cols(o, n)].astype(f32)
        def theirs(o, n): return E[two[0], :, self.cols(o, n)].astype(f32) + E[two[1], :, self.cols(o, n)].astype(f32)
        ov = gw - fw
        if fw:
            F[:, self.cols(gw * sel, fw)] = mine(ov * sel, fw)
            F[:, self.cols(gw * (1 - sel), fw)] = theirs(ov * (1 - sel), fw)
        if ov: F[:, pl.ds(fw, ov)] = mine(fw * (1 - sel), ov) + theirs(fw * sel, ov)
        rows = f.u if f.kind == 3 else 32
        half = rows // 2
        m = 8
        for prow, pcol, pw, out, ocol in targets:
            src = lambda q: F.at[pl.ds(pl.multiple_of(prow + half * q, m), half), pl.ds(pcol, pw)]
            dst = out if ocol is None else out.at[:, self.cols(ocol, pw)]
            f.out.append(self.w.send(src(1 - self.c), dst, self.other))
            f.out.append(self.w.local(src(self.c), dst))
    def wait_out(self, f):
        for i, q in enumerate(f.out):
            if i % 2: q.wait()
            else: q.wait_recv()

def backward_kernel(*refs):
    (I, O, r), refs = named([dict(A_GOT, **A_MADE, tokens=0), B_OUT, B_SCR], refs)
    grads, lands, bufs, (ss, rs, ls, free) = refs[:4], refs[4:8], refs[8:-4], refs[-4:]
    x, y, z, c = spot()
    hi = z // 2
    k = (y * 4 + x) * 2 + hi
    pair = device(x, y, z + 1 - 2 * (z % 2), c)
    cross = device(x, y, 3 - z, c)
    far = device(x, y, (z + 2) % 4, c)
    other = device(x, y, z, 1 - c)
    nxt, prv = along(x, y, z, c, 1), along(x, y, z, c, -1)
    go = {(a, st): moved(x, y, z, c, a, st) for a in XY for st in (1, -1)}
    count = greet(list(go.values()) + [pair, cross, far, other, nxt, prv])
    w = Wire(ss, rs, ls)
    own, oth = at_rows(256 * c, 256, 256), at_rows(256 * (1 - c), 256, 256)
    col = lambda p, n: pl.ds(pl.multiple_of(p, 128), n)
    W = r.W
    slot = lambda i: W.at[i // 2, pl.ds(1024 * (i % 2), 1024)]
    def w_down():
        return [w.local(I.wd.at[at_rows(FH * c, FH, FH), :], W.at[c]), w.local(I.wdr.at[at_rows(FH * c, FH, FH), :], W.at[1 - c])]
    lgd = w.local(I.ddown, grads[3])
    lwd = w_down()
    ld = Box({n: w.local(vars(I)[n], vars(r)[n]) for n in dict(dffo=0, gate=0, up=0, h2=0, small=0, resid=0, ext=0, bcx=0, keep=0)})
    ld.tok = w.local(I.tokens, r.tok)
    met(count)
    sc = Scatter(w, go, pair, cross, far, x, y, z, c, other, grads, lands, bufs)
    F = sc.f
    lgd.wait()
    r.gsum[...] = jnp.zeros((8, 1024), f32)
    gain = lambda i: r.small[i:i + 1, :]
    t = Box(got={})
    def d_act(n):
        if n == 0:
            for q in lwd + [ld.dffo, ld.gate, ld.up]: q.wait()
        d = nt(r.dffo[:, :512], W[0, n:n + 768, :]) + nt(r.dffo[:, 512:], W[1, n:n + 768, :])
        g, u = r.gate[:, n:n + 768].astype(f32), r.up[:, n:n + 768].astype(f32)
        sg = jax.nn.sigmoid(g)
        r.gate[:, n:n + 768] = (d * u * sg * (1.0 + g * (1.0 - sg))).astype(bf)
        r.up[:, n:n + 768] = (d * (g * sg)).astype(bf)
    panels = [[(r.gate, 512 * p, 512, 512 * p)] for p in range(4)] + [[(r.up, FH + 512 * p, 512, 512 * p)] for p in range(4)]
    panels += [[(r.gate, 2048, 256, 2048), (r.up, FH + 2048, 256, 2048)]]
    def fetch(i):
        out, o = [], 0
        for _, cc, n, _ in panels[i % 9]:
            out.append(w.local(I.w2.at[:, pl.ds(cc, n)], slot(i % 4).at[:, pl.ds(o, n)])); o += n
        return out
    def slab(src, yy, base):
        d = tn(r.h2[:, col(256 * yy, 256)], src[...]).astype(bf)
        for xx in range(4):
            for u in (0, 1): grads[2][yy, xx, u, :, base:base + FH] = d[64 * xx + 32 * u:64 * xx + 32 * u + 32]
    def d_gate(i):
        if i == 0:
            t.got.update({p: fetch(p) for p in range(4)})
            ld.h2.wait()
        slab(r.gate, (y + JS[i] + 4) % 4, 0)
        sc.zsend(F.f2a, JS[i])
    def d_up(i):
        slab(r.up, (y + JS[i] + 4) % 4, FH)
        if i == 3:
            for j in JS: sc.zsend(F.f2b, j)
    def panel(i):
        for q in t.got[i]: q.wait()
        rr, acc = ((oth, r.dhs), (own, r.dho))[i // 9]
        o, d = 0, 0
        for nm, _, n, off in panels[i % 9]:
            d = d + nt(nm[rr, off:off + n], slot(i % 4)[:, o:o + n])
            o += n
        acc[...] = d if i % 9 == 0 else acc[...] + d
        if i + 4 < 18: t.got[i + 4] = fetch(i + 4)
        if i == 8: t.dh = w.send(r.dhs, r.dhr, other)
        if i == 17:
            r.h, r.y, r.conv = (r.gate.at[:, pl.ds(a, m)] for a, m in ((0, 1024), (1024, 512), (1536, 512)))
            ld.h, ld.y, ld.conv = w.local(I.h, r.h), w.local(I.y, r.y), w.local(I.conv, r.conv)
            t.win = [w.local(I.w1.at[:, pl.ds(512 * p, 512)], slot(p + 1)) for p in range(3)]
            t.wo = [w.local(I.w1.at[at_rows(512 * c, 512, 512), pl.ds(1536, 512)], slot(0).at[at_rows(512 * c, 512, 512)]),
                w.local(I.wor, slot(0).at[at_rows(512 * (1 - c), 512, 512)])]
            ld.small.wait(); ld.resid.wait()
    def back2():
        t.dh.wait_recv()
        def rows(i, _):
            q = at_rows(i * 64, 64, 64); qo = at_rows(256 * c + i * 64, 64, 64)
            v = r.resid[q, :]
            s2 = lax.rsqrt(jnp.mean(v * v, axis=1, keepdims=True) + EPS)
            d = r.dho[q, :] + r.dhr[q, :]
            r.gsum[1:2, :] += jnp.sum(d * v * s2, axis=0, keepdims=True)
            wt = d * gain(1)
            inner = jnp.mean(wt * v, axis=1, keepdims=True)
            dr = r.dffo[qo, :].astype(f32) + (s2 * wt - v * (s2 * s2 * s2) * inner)
            r.resid[q, :] = dr
            r.h2[qo, :] = dr.astype(bf)
            return 0
        lax.fori_loop(0, 4, rows, 0)
        t.dm = w.send(r.h2.at[own], r.h2.at[own], other)
        for q in (ld.y, ld.ext, ld.conv, ld.bcx, ld.h, ld.tok, ld.keep): q.wait()
        for q in t.wo: q.wait()
    def d_y():
        t.dm.wait_recv()
        d = nt(r.h2[:, :512], slot(0)[0:512, :]) + nt(r.h2[:, 512:], slot(0)[512:1024, :])
        r.dcv[0:512, :] = d * r.bcx[:, 512:1024].astype(f32)
        r.bcx[:, 512:1024] = (d * r.conv[...].astype(f32)).astype(bf)
        t.halo = w.send(r.dcv.at[pl.ds(0, 8)], r.dcv.at[pl.ds(512, 8)], prv)
    def d_out():
        def rows(i, _):
            d = tn(r.y[:, at_rows(256 * i, 256, 256)], r.h2[...]).astype(bf)
            for xx in range(4):
                for u in (0, 1):
                    v = d[64 * xx + 32 * u:64 * xx + 32 * u + 32]
                    r.up[at_rows(256 * i + 64 * xx + 32 * u, 32, 32), 0:512] = jnp.where(c == 0, v[:, 512:], v[:, :512])
                    grads[1][2 * c + i, xx, u, 96:128, :] = jnp.where(c == 0, v[:, :512], v[:, 512:])
            return 0
        lax.fori_loop(0, 2, rows, 0)
        t.do = [w.send(r.up.at[pl.ds(256 * i + 64 * xx + 32 * u, 32), pl.ds(0, 512)], grads[1].at[2 * c + i, xx, u, pl.ds(96, 32), :], other)
            for i in (0, 1) for xx in range(4) for u in (0, 1)]
    def d_taps():
        for q in range(0, 512, 128):
            dv = r.dcv[q:q + 128, :]
            for i in range(3):
                r.gsum[2 + i:3 + i, col(512 * c, 512)] += jnp.sum(dv * r.ext[14 + i + q:142 + i + q, :], axis=0, keepdims=True)
    def d_bx():
        t.halo.wait_recv()
        tap = [r.small[2 + i:3 + i, col(512 * c, 512)] for i in range(3)]
        r.dcv[512:520, :] = r.dcv[512:520, :] * (k < 31).astype(f32)
        for q in range(0, 512, 128):
            dx = tap[2] * r.dcv[q:q + 128, :] + tap[1] * r.dcv[q + 1:q + 129, :] + tap[0] * r.dcv[q + 2:q + 130, :]
            bp, xp = r.bcx[q:q + 128, 0:512].astype(f32), r.bcx[q:q + 128, 1024:1536].astype(f32)
            r.bcx[q:q + 128, 0:512] = (dx * xp).astype(bf)
            r.bcx[q:q + 128, 1024:1536] = (dx * bp).astype(bf)
    def d_in(i):
        if i == 0:
            for q in t.do: q.wait_recv()
        yy = (y + JS[i] + 4) % 4
        d = tn(r.h[:, col(256 * yy, 256)], r.bcx[...]).astype(bf)
        for p in range(3):
            for xx in range(4):
                for u in (0, 1): grads[1][yy, xx, u, 32 * p:32 * p + 32, :] = d[64 * xx + 32 * u:64 * xx + 32 * u + 32, 512 * p:512 * p + 512]
        sc.zsend(F.f1b, JS[i])
        if i == 3:
            for j in JS: sc.zsend(F.f1a, j)
    def d_h():
        t.dh.wait_send()
        for q in t.win: q.wait()
        for rr, acc in ((oth, r.dhs), (own, r.dho)):
            acc[...] = sum(nt(r.bcx[rr, 512 * i:512 * i + 512], slot(i + 1)[...]) for i in range(3))
        t.dh = w.send(r.dhs, r.dhr, other)
        t.act = w_down() + [w.local(I.act, r.gate)]
    def back1():
        t.dh.wait_recv()
        def rows(i, _):
            q = at_rows(i * 64, 64, 64)
            v = r.tok[q, :].astype(f32)
            s1 = lax.rsqrt(jnp.mean(v * v, axis=1, keepdims=True) + EPS)
            d = r.dho[q, :] + r.dhr[q, :]
            r.gsum[0:1, :] += jnp.sum(d * v * s1, axis=0, keepdims=True)
            wt = d * gain(0)
            inner = jnp.mean(wt * v, axis=1, keepdims=True)
            r.dho[q, :] = r.resid[q, :] + (s1 * wt - v * (s1 * s1 * s1) * inner)
            return 0
        lax.fori_loop(0, 4, rows, 0)
        pl.semaphore_signal(free, inc=1, device_id=other, device_id_type=MESH)
        t.tok = w.local(r.dho, O.dtok)
        eye = (lax.broadcasted_iota(jnp.int32, (8, 128), 0) == lax.broadcasted_iota(jnp.int32, (8, 128), 1)).astype(f32).astype(bf)
        sm = tn(r.gsum[...].astype(bf), eye).astype(bf)
        for yy in range(4):
            for xx in range(4):
                for u in (0, 1):
                    o = 256 * yy + 64 * xx + 32 * u
                    grads[0][yy, xx, u] = sm[o:o + 32]
        t.dh.wait_send()
    def ffo():
        for q in t.act: q.wait()
        t.tok.wait()
        t.resid = w.local(I.resid, r.resid)
        for rr, acc in ((oth, r.dhs), (own, r.dho)):
            for i in (0, 1): acc[:, 512 * i:512 * i + 512] = dot(r.gate[rr, :], W[i])
        pl.semaphore_wait(free, 1)
        t.dh = w.send(r.dhs, r.dhr, other)
    def mixed():
        t.dh.wait_recv(); t.resid.wait()
        r.tok[...] = (r.keep[...] * (r.resid[...] + (r.dho[...] + r.dhr[...]))).astype(bf)
        w.local(r.tok, O.mixed)
    each = functools.partial
    chunks = [each(d_act, n) for n in (0, 768, 1536)] + [each(d_gate, i) for i in range(4)] + [each(d_up, i) for i in range(4)]
    chunks += [each(panel, i) for i in range(18)] + [back2, d_y, d_out, d_taps, d_bx] + [each(d_in, i) for i in range(4)] + [d_h, back1, ffo, mixed]
    half = 512 * c
    at_in = lambda o: [(32 * p, 0, 256, O.din, 1024 * p + half + o) for p in range(3)] + [(96, 0, 256, O.dout, half + o)]
    ends = [at_in(0), at_in(256), [(0, 0, 128, O.ds.at[c], None)], [(0, 0, FH, O.dg, FH * c)], [(0, 0, FH, O.du, FH * c)],
        [(0, 0, 256, O.dd, half)], [(0, 0, 256, O.dd, half + 256)]]
    flows = list(vars(F).values())
    moves = (sc.first, sc.second, sc.third, sc.last1)
    for what, *where in ORDER_B:
        if not where: chunks[what]()
        elif what < 3: moves[what](flows[where[0]], where[1])
        elif what < 4: moves[what](flows[where[0]])
        else: sc.last2(flows[where[0]], ends[where[0]])
    w.drain()

def backward_all(a, tokens):
    a = Box(a)
    a.ddown = a.ddown.reshape(4, 4, 2, 144, 512)
    scr = [*B_SCR.values()] + GRADS + GRADS + [v for t in RFLOWS.values() for v in flow_scratch(t)]
    outs = call(backward_kernel, [*B_OUT.values()], scr, 2, 63, [pltpu.SemaphoreType.REGULAR], pl.BlockSpec(memory_space=pl.ANY), *vars(a).values(), tokens)
    return Box(dict(zip(B_OUT, outs)))

def finish_kernel(n, *refs):
    src, part, dst, (dn1, dn2, dtap), held, sems, (square,) = refs[:n], refs[n], refs[n + 1:2 * n + 1], refs[2 * n + 1:2 * n + 4], refs[2 * n + 4:3 * n + 4], refs[3 * n + 4:4 * n + 4], refs[4 * n + 4:]
    ins = [pltpu.make_async_copy(a, v, s) for a, v, s in zip(src, held, sems)]
    for cp in ins: cp.start()
    square[...] = jnp.zeros((128, 128), f32)
    square[0:16, :] = part[0] + part[1]
    rows = jnp.transpose(square[...])
    dn1[...] = rows[0:1, 0:16]
    dn2[...] = rows[1:2, 0:16]
    dtap[...] = rows[2:5, 0:16]
    outs = [pltpu.make_async_copy(v, d, s) for v, d, s in zip(held, dst, sems)]
    for a, d in zip(ins, outs): a.wait(); d.start()
    for d in outs: d.wait()

def finish_all(part, *args):
    hbm, vm = pl.BlockSpec(memory_space=pl.ANY), pl.BlockSpec(memory_space=pltpu.VMEM)
    n = len(args)
    out = [jax.ShapeDtypeStruct(v.shape, v.dtype) for v in args] + [jax.ShapeDtypeStruct((m, 16), f32) for m in (1, 1, 3)]
    return pl.pallas_call(
        functools.partial(finish_kernel, n), out_shape=tuple(out), in_specs=[hbm] * n + [vm], out_specs=(hbm,) * n + (vm,) * 3,
        scratch_shapes=[pltpu.VMEM(v.shape, v.dtype) for v in args] + [pltpu.SemaphoreType.DMA] * n + [pltpu.VMEM((128, 128), f32)],
        compiler_params=pltpu.CompilerParams(vmem_limit_bytes=62 * 2**20))(*args, part)


def body(tokens, lengths, norm1_gain, in_proj, conv_weight, out_proj, norm2_gain, w_gate, w_up, w_down, cotangent):
    a = forward_all(lengths, tokens, cotangent, in_proj, out_proj, smalls(norm1_gain, norm2_gain, conv_weight), w_gate, w_up, w_down)
    b = backward_all(a, tokens)
    mixed, dtok, din, dout, dg, du, dd, dn1, dn2, dtap = finish_all(b.ds, b.mixed, b.dtok, b.din, b.dout, b.dg, b.du, b.dd)
    return mixed, dtok, dn1[0], din, dtap, dout, dn2[0], dg, du, dd

def solution(mesh):
    tok = P(("rep", "shard"), None)
    par = (P("shard"), P("shard", None), P(None, "shard"), P("shard", None), P("shard"), P("shard", None), P("shard", None), P("shard", None))
    return jax.shard_map(body, mesh=mesh, in_specs=(tok, P()) + par + (tok,), out_specs=(tok, tok) + par, check_vma=False)
```

```python
ORDER_A = (
    (0, 1), (0, 0), (0, 2), (0, 3), (1, 0), (1, 1), (2, 0), (4, 0, 0), (2, 1), (4, 1, 0), (3, 0), (4, 0, -1), (4, 1, -1), (4, 0, 1), (5, 0, 0),
    (4, 1, 1), (3, 1), (5, 1, 0), (4, 0, 2), (5, 1, -1), (1, 2), (1, 3), (5, 0, -1), (5, 1, 1), (5, 0, 1), (5, 0, 2), (4, 1, 2), (2, 2), (4, 2, 0),
    (4, 3, 0), (2, 3), (5, 1, 2), (3, 2), (5, 3, 0), (4, 2, -1), (4, 3, -1), (0, 5), (0, 4), (4, 2, 1), (0,), (5, 2, 0), (4, 3, 1), (3, 3), (1,),
    (5, 3, -1), (2,), (3,), (4, 2, 2), (5, 3, 1), (5, 2, -1), (1, 4), (1, 5), (4,), (5,), (6,), (4, 3, 2), (5, 2, 1), (4, 4, 0), (7,), (2, 5),
    (5, 2, 2), (2, 4), (5, 3, 2), (4, 5, 0), (5, 4, 0), (8,), (3, 5), (9,), (4, 5, -1), (10,), (4, 4, -1), (11,), (4, 5, 1), (12,), (3, 4), (13,),
    (5, 5, 0), (4, 4, 1), (14,), (5, 4, -1), (15,), (16,), (4, 5, 2), (4, 4, 2), (17,), (5, 5, -1), (18,), (5, 5, 1), (5, 4, 1), (5, 5, 2), (5, 4, 2),)
ORDER_B = (
    (0, 5, -1), (0, 5, 2), (0, 6, -1), (0, 6, 2), (0, 5, 0), (0, 5, 1), (0, 6, 0), (0, 6, 1), (0,), (1,), (1, 6, -1), (1, 5, -1), (2,), (1, 6, 2),
    (1, 6, 0), (1, 5, 2), (1, 5, 0), (3,), (1, 6, 1), (1, 5, 1), (4,), (5,), (6,), (7,), (8,), (9,), (10,), (11,), (2, 6, 2), (2, 5, 2), (12,), (13,),
    (14,), (15,), (16,), (17,), (18,), (19,), (2, 6, 0), (2, 5, 0), (0, 3, 2), (20,), (21,), (22,), (23,), (24,), (25,), (0, 4, 2), (26,), (27,),
    (28,), (2, 6, -1), (2, 6, 1), (2, 5, -1), (2, 5, 1), (29,), (0, 4, -1), (0, 3, -1), (1, 4, 2), (1, 3, 2), (30,), (31,), (3, 6), (3, 5), (0, 4, 1),
    (32,), (1, 3, -1), (1, 4, -1), (0, 3, 1), (33,), (0, 4, 0), (34,), (35,), (2, 3, 2), (36,), (2, 4, 2), (37,), (38,), (1, 4, 1), (4, 6), (0, 3, 0),
    (4, 5), (1, 3, 1), (39,), (2, 4, -1), (0, 1, 2), (0, 2, -1), (0, 2, 2), (0, 2, 0), (0, 2, 1), (40,), (0, 0, 2), (1, 4, 0), (2, 3, -1), (1, 3, 0),
    (0, 1, -1), (41,), (2, 3, 1), (0, 0, -1), (2, 4, 1), (1, 0, 2), (0, 1, 1), (1, 1, 2), (1, 2, -1), (1, 2, 2), (1, 2, 0), (1, 2, 1), (0, 0, 1),
    (2, 4, 0), (0, 1, 0), (2, 3, 0), (1, 1, -1), (3, 4), (0, 0, 0), (1, 1, 1), (3, 3), (2, 1, 2), (1, 0, -1), (2, 2, 2), (2, 2, 0), (2, 0, 2),
    (1, 1, 0), (1, 0, 1), (1, 0, 0), (2, 1, -1), (2, 1, 1), (2, 0, -1), (2, 2, -1), (2, 2, 1), (2, 0, 1), (2, 1, 0), (4, 4), (2, 0, 0), (3, 1),
    (3, 2), (3, 0), (4, 3), (4, 1), (4, 2), (4, 0),)

import functools
import jax, jax.numpy as jnp
from jax import lax
from jax.experimental import pallas as pl
from jax.experimental.pallas import tpu as pltpu
from jax.sharding import PartitionSpec as P
MESH = pl.DeviceIdType.MESH
EPS = 1e-05
bf, f32 = jnp.bfloat16, jnp.float32
C1 = 2176; HALF = 1152; CAT = 6784; UNIT = 32; DUNIT = 144; FH = 2304
COPIES = 272
JS = (2, -1, 1, 0)
PAIR, CROSS, X, Y = 1, 2, 0, 1
ONE, TWO, THREE = 1, 2, 3
XY, YX = (X, Y), (Y, X)
class Box:
    def __init__(self, *a, **kw):
        for d in a: self.__dict__.update(d)
        self.__dict__.update(kw)

FLOWS = dict(
    f1a=Box(kind=1, base=0, step=384, gw=640, fw=384, to=PAIR, order=XY),
    f1b=Box(kind=1, base=1024, step=384, gw=768, fw=384, to=CROSS, order=YX),
    f2a=Box(kind=2, base=0, step=768, gw=1536, fw=768, to=PAIR, order=YX),
    f2b=Box(kind=2, base=2304, step=768, gw=1536, fw=768, to=CROSS, order=XY),
    f3a=Box(kind=3, base=0, step=0, gw=256, fw=0, to=None, order=XY),
    f3b=Box(kind=3, base=256, step=0, gw=256, fw=0, to=None, order=YX))

def spot():
    rep = lax.axis_index("rep"); s = lax.axis_index("shard")
    return (s // 4) % 4, s // 16, ((s // 2) % 2) * 2 + rep, s % 2

def device(x, y, z, c):
    return (z % 2, ((y * 4 + x) * 2 + z // 2) * 2 + c)

def moved(x, y, z, c, axis, step):
    if axis == X: return device((x + step + 4) % 4, y, z, c)
    return device(x, (y + step + 4) % 4, z, c)

def along(x, y, z, c, step):
    k = ((y * 4 + x) * 2 + z // 2 + step + 32) % 32
    return device((k // 2) % 4, k // 8, (k % 2) * 2 + z % 2, c)

def greet(devices):
    bar = pltpu.get_barrier_semaphore()
    for d in devices:
        pl.semaphore_signal(bar, inc=1, device_id=d, device_id_type=MESH)
    return len(devices)

def met(count): pl.semaphore_wait(pltpu.get_barrier_semaphore(), count)

class Copy:
    def __init__(self, cp): self.cp, self.here, self.gone = cp, False, False
    def wait_recv(self): self.cp.wait_recv(); self.here = True
    def wait_send(self): self.cp.wait_send(); self.gone = True

class Near:
    def __init__(self, cp): self.cp, self.here = cp, False
    def wait(self): self.cp.wait(); self.here = True

class Wire:
    def __init__(self, ss, rs, ls): self.ss, self.rs, self.ls, self.sent, self.near = ss, rs, ls, [], []
    def send(self, src, dst, dev):
        i = len(self.sent)
        cp = pltpu.make_async_remote_copy(src_ref=src, dst_ref=dst, send_sem=self.ss.at[i], recv_sem=self.rs.at[i], device_id=dev, device_id_type=MESH)
        cp.start(); self.sent.append(Copy(cp)); return self.sent[-1]
    def local(self, src, dst):
        cp = pltpu.make_async_copy(src, dst, self.ls.at[len(self.near)])
        cp.start(); self.near.append(Near(cp)); return self.near[-1]
    def drain(self):
        for cp in self.near:
            if not cp.here: cp.wait()
        for cp in self.sent:
            if not cp.here: cp.wait_recv()
            if not cp.gone: cp.wait_send()

def at_rows(v, n, m=16): return pl.ds(pl.multiple_of(v, m), n)

class All:
    def __init__(self, *q): self.q = q
    def wait_recv(self):
        for q in self.q: q.wait_recv()

class Gather:
    def __init__(self, w, go, pair, cross, other, x, y, z, w1, w2, wd, wdr):
        self.w, self.go, self.x, self.y, self.other, self.wdr, self.hi = w, go, x, y, other, wdr, z // 2
        self.f = Box()
        for n, t in FLOWS.items():
            sel = {PAIR: z % 2, CROSS: z // 2, None: 0}[t.to]
            d = t.kind == 3
            vars(self.f)[n] = Box(vars(t), buf=(w1, w2, wd)[t.kind - 1], unit=DUNIT if d else UNIT, mine=(t.base + t.step * sel, t.gw),
                alone=(t.base + t.gw * sel, t.fw), dev={PAIR: pair, CROSS: cross, None: None}[t.to], z=[], p={}, m={}, p2={}, m2={})
    def block(self, f, da, db, unit=None, cols=None, buf=None):
        a, b = f.order
        pos = {X: self.x, Y: self.y}
        pos[a] = (pos[a] + da + 4) % 4
        pos[b] = (pos[b] + db + 4) % 4
        u = f.unit
        row = (pos[Y] * 4 + pos[X]) * (2 * u)
        n = 2 * u
        if unit is not None: row, n = row + unit * u, u
        col, width = cols or f.mine
        return (f.buf if buf is None else buf).at[at_rows(row, n), pl.ds(col if isinstance(col, int) else pl.multiple_of(col, 128), width)]
    def push(self, f, da, db, dev, unit=None):
        v = self.block(f, da, db, unit)
        return self.w.send(v, v, dev)
    def fwd(self, f, da, db):
        if f.dev is not None and (da or db):
            v = self.block(f, da, db, None, f.alone)
            f.z.append(self.w.send(v, v, f.dev))
        if f.kind == 3: f.z.append(self.w.send(self.block(f, da, db), self.block(f, da, db, None, None, self.wdr), self.other))
    def open2(self, f, j):
        b = f.order[1]
        f.p[j] = self.push(f, j, 0, self.go[(b, 1)])
        f.m[j] = self.push(f, j, 0, self.go[(b, -1)])
    def r1(self, f, own):
        a, b = f.order
        u = self.hi if own else 1 - self.hi
        new = [self.push(f, 0, 0, self.go[(d, st)], u) for d in (a, b) for st in (1, -1)]
        if own: f.half = new
        else:
            f.p[None], f.m[None], f.p[0], f.m[0] = (All(*q) for q in zip(f.half, new))
            self.fwd(f, 0, 0)
    def r2(self, f):
        a = f.order[0]
        f.p[None].wait_recv(); f.p2[None] = self.push(f, -1, 0, self.go[(a, 1)], 0)
        f.m[None].wait_recv(); f.m2[None] = self.push(f, 1, 0, self.go[(a, -1)], 1)
        self.open2(f, -1); self.open2(f, 1)
        self.fwd(f, -1, 0); self.fwd(f, 1, 0)
    def r3(self, f):
        f.p2[None].wait_recv(); f.m2[None].wait_recv()
        self.open2(f, 2); self.fwd(f, 2, 0)
    def r4(self, f, j):
        b = f.order[1]
        f.p[j].wait_recv(); f.p2[j] = self.push(f, j, -1, self.go[(b, 1)], 0)
        f.m[j].wait_recv(); f.m2[j] = self.push(f, j, 1, self.go[(b, -1)], 1)
        self.fwd(f, j, -1); self.fwd(f, j, 1)
    def r5(self, f, j):
        f.p2[j].wait_recv(); f.m2[j].wait_recv()
        self.fwd(f, j, 2)
    def all_here(self, f):
        for q in f.z: q.wait_recv()

def dot(a, b): return jnp.dot(a, b, preferred_element_type=f32)
def tn(a, b): return lax.dot_general(a, b, (((0,), (0,)), ((), ())), preferred_element_type=f32)
def nt(a, b): return lax.dot_general(a, b, (((1,), (1,)), ((), ())), preferred_element_type=f32)

A_GOT = dict(w1=((1024, C1), bf), w2=((1024, 2 * FH), bf), wd=((4608, 512), bf), wor=((512, 512), bf), wdr=((4608, 512), bf), ddown=((4608, 512), bf))
A_MADE = dict(h=((512, 1024), bf), bcx=((512, 1536), bf), ext=((528, 512), f32), conv=((512, 512), bf), y=((512, 512), bf),
    resid=((256, 1024), f32), h2=((512, 1024), bf), gate=((512, FH), bf), up=((512, FH), bf), act=((512, FH), bf),
    dffo=((512, 1024), bf), small=((8, 1024), f32), keep=((256, 1), f32))
A_SCR = dict(T=((512, 1024), bf), cotv=((256, 1024), bf), win=((1024, 1536), bf), wo=((512, 1024), bf), wsm=((1024, 128), bf),
    w2=((1024, 2 * FH), bf), gf=((512, FH), f32), cpart=((512, 512), f32), mixs=((256, 1024), f32), mixr=((256, 1024), f32),
    dnf=((DUNIT, 512), f32), dns=((72, 512), f32), dnb=((DUNIT, 512), bf), ddn=((2, FH, 512), bf),
    inp=((16, 3072), bf), outp=((16, 1024), bf), sml=((16, 128), bf), srow=((16, 128), bf), wgs=((16, 4608), bf), wus=((16, 4608), bf), wds=((72, 1024), bf))

def named(groups, refs):
    refs, out = list(refs), []
    for g in groups:
        out.append(Box(dict(zip(g, refs)))); refs = refs[len(g):]
    return out, refs

def forward_kernel(*refs):
    A_IN = dict(lengths=0, tokens=0, cot=0, inp=0, outp=0, sml=0, wgs=0, wus=0, wds=0)
    (I, O, M, V, S), (ss, rs, ls) = named([A_IN, A_GOT, A_MADE, A_MADE, A_SCR], refs)
    w1, w2, wd, wor, wdr = O.w1, S.w2, O.wd, O.wor, O.wdr
    x, y, z, c = spot()
    hi = z // 2
    s = ((y * 4 + x) * 2 + hi) * 2 + c
    k = s // 2
    pair = device(x, y, z + 1 - 2 * (z % 2), c)
    cross = device(x, y, 3 - z, c)
    other = device(x, y, z, 1 - c)
    nxt, prv = along(x, y, z, c, 1), along(x, y, z, c, -1)
    go = {(a, st): moved(x, y, z, c, a, st) for a in XY for st in (1, -1)}
    count = greet(list(go.values()) + [pair, cross, other, nxt, prv])
    w = Wire(ss, rs, ls)
    own, oth = at_rows(256 * c, 256, 256), at_rows(256 * (1 - c), 256, 256)
    col = lambda p, n: pl.ds(pl.multiple_of(p, 128), n)
    lds = w.local(I.wds, S.wds)
    lrow = w.local(I.sml, S.srow)
    lin = [w.local(a, b) for a, b in ((I.inp, S.inp), (I.outp, S.outp), (I.wgs, S.wgs), (I.wus, S.wus))]
    lcot = [w.local(I.cot, S.cotv)]
    ltok = w.local(I.tokens, S.T.at[own])
    lrow.wait()
    eye = (lax.broadcasted_iota(jnp.int32, (16, 128), 0) == lax.broadcasted_iota(jnp.int32, (16, 128), 1)).astype(f32).astype(bf)
    S.sml[...] = tn(S.srow[...], eye)[0:16].astype(bf)
    met(count)
    rows = at_rows(16 * s, 16)
    pieces = [(I.inp, S.inp, 1024 * i, 512, w1, 512 * i) for i in range(3)] + [(I.outp, S.outp, 0, 512, w1, 1536), (I.wgs, S.wgs, 0, FH, w2, 0), (I.wus, S.wus, 0, FH, w2, FH)]
    got = [w.send(S.sml, w1.at[rows, pl.ds(2048, 128)], other)]
    for src, _, a, n, to, d in pieces: got.append(w.send(src.at[:, col(a + n * (1 - c), n)], to.at[rows, pl.ds(d, n)], other))
    for q in lin: q.wait()
    mine = [w.local(S.sml, w1.at[rows, pl.ds(2048, 128)])]
    for _, src, a, n, to, d in pieces: mine.append(w.local(src.at[:, col(a + n * c, n)], to.at[rows, pl.ds(d, n)]))
    lds.wait()
    S.dns[...] = S.wds[:, col(512 * (1 - c), 512)].astype(f32)
    gdn = w.send(S.dns, S.dnf.at[at_rows(72 * c, 72, 8)], other)
    S.dnf[at_rows(72 * c, 72, 8), :] = S.wds[:, col(512 * c, 512)].astype(f32)
    gtok = w.send(I.tokens, S.T.at[own], other)
    g = Gather(w, go, pair, cross, other, x, y, z, w1, w2, wd, wdr)
    F = g.f
    for q in mine: q.wait()
    for q in got: q.wait_recv()
    urow, drow = at_rows(UNIT * k, UNIT, UNIT), at_rows(DUNIT * k, DUNIT)
    z1 = w.send(w1.at[urow], w1.at[urow], cross)
    z2, z2b = (w.send(w2.at[urow, pl.ds(n, FH)], w2.at[urow, pl.ds(n, FH)], cross) for n in (0, FH))
    gdn.wait_recv()
    S.dnb[...] = S.dnf[...].astype(bf)
    lwd = w.local(S.dnb, wd.at[drow, :])
    for q in lcot: q.wait()
    valid = I.lengths[lax.axis_index("rep")] - 256 * s
    V.keep[...] = (lax.broadcasted_iota(jnp.int32, (256, 1), 0) < valid).astype(f32)
    V.dffo[own, :] = (V.keep[...] * S.cotv[...].astype(f32)).astype(bf)
    gdf = w.send(V.dffo.at[own], V.dffo.at[own], other)
    ltok.wait(); gtok.wait_recv(); lwd.wait()
    t = Box()
    def save(**kw):
        for n in kw: w.local(vars(V)[n], vars(M)[n])
    def one():
        for f in (F.f1a, F.f1b): g.all_here(f)
        l1 = w.local(w1.at[:, pl.ds(2048, 128)], S.wsm)
        t.win = w.local(w1.at[:, pl.ds(0, 1536)], S.win)
        t.wor = w.send(w1.at[at_rows(512 * (1 - c), 512, 512), pl.ds(1536, 512)], wor, other)
        t.wo = w.local(w1.at[at_rows(512 * c, 512, 512), pl.ds(1536, 512)], S.wo.at[:, col(512 * c, 512)])
        l1.wait()
        V.small[...] = nt(eye, S.wsm[...])[0:8]
    def norm1():
        def rows(i, _):
            q = at_rows(i * 64, 64, 64)
            v = S.T[q, :].astype(f32)
            sc = lax.rsqrt(jnp.mean(v * v, axis=1, keepdims=True) + EPS)
            V.h[q, :] = (v * sc * V.small[0:1, :]).astype(bf)
            return 0
        lax.fori_loop(0, 8, rows, 0)
        t.win.wait()
    ext = V.ext
    def b_x():
        for n in (0, 256):
            b_ = dot(V.h[...], S.win[:, n:n + 256])
            x_ = dot(V.h[...], S.win[:, 1024 + n:1280 + n])
            V.bcx[:, n:n + 256] = b_.astype(bf)
            V.bcx[:, 1024 + n:1280 + n] = x_.astype(bf)
            ext[16:528, n:n + 256] = (b_ * x_).astype(bf).astype(f32)
        t.halo = w.send(ext.at[pl.ds(520, 8)], ext.at[pl.ds(8, 8)], nxt)
        t.wor.wait_recv()
        t.wo2 = w.local(wor, S.wo.at[:, col(512 * (1 - c), 512)])
    def c_():
        for n in (0, 256):
            v = dot(V.h[...], S.win[:, 512 + n:768 + n])
            S.cpart[:, n:n + 256] = v
            V.bcx[:, 512 + n:768 + n] = v.astype(bf)
        save(h=1, bcx=1, small=1)
    def conv():
        t.halo.wait_recv()
        ext[8:16, :] = ext[8:16, :] * (k > 0).astype(f32)
        t0, t1, t2 = (V.small[2 + i:3 + i, col(512 * c, 512)] for i in range(3))
        for q in range(0, 512, 128):
            cv = t0 * ext[14 + q:142 + q, :] + t1 * ext[15 + q:143 + q, :] + t2 * ext[16 + q:144 + q, :]
            V.conv[q:q + 128, :] = cv.astype(bf)
            V.y[q:q + 128, :] = (S.cpart[q:q + 128, :] * cv).astype(bf)
        t.wo.wait(); t.wo2.wait()
    def mix():
        S.mixs[...] = dot(V.y[oth, :], S.wo[...])
        t.mix = w.send(S.mixs, S.mixr, other)
    def mix2():
        V.resid[...] = dot(V.y[own, :], S.wo[...])
        save(ext=1, conv=1, y=1)
    def norm2():
        t.mix.wait_recv()
        def rows(i, _):
            q, qo = at_rows(i * 64, 64, 64), at_rows(256 * c + i * 64, 64, 64)
            v = S.T[qo, :].astype(f32) + (V.resid[q, :] + S.mixr[q, :])
            V.resid[q, :] = v
            sc = lax.rsqrt(jnp.mean(v * v, axis=1, keepdims=True) + EPS)
            V.h2[qo, :] = (v * sc * V.small[1:2, :]).astype(bf)
            return 0
        lax.fori_loop(0, 4, rows, 0)
        t.h2 = w.send(V.h2.at[own], V.h2.at[own], other)
        save(resid=1)
    def two():
        g.all_here(F.f2a)
        w.local(w2.at[:, pl.ds(0, FH)], O.w2.at[:, pl.ds(0, FH)])
        t.h2.wait_recv(); gdf.wait_recv()
        save(h2=1, dffo=1, keep=1)
    def gate(i):
        n = 768 * i
        v = dot(V.h2[...], w2[:, n:n + 768])
        S.gf[:, n:n + 768] = v * jax.nn.sigmoid(v)
        V.gate[:, n:n + 768] = v.astype(bf)
    def up_here():
        g.all_here(F.f2b)
        w.local(w2.at[:, pl.ds(FH, FH)], O.w2.at[:, pl.ds(FH, FH)])
        save(gate=1)
    def up(i):
        n = 768 * i
        g_, u_ = S.gf[:, n:n + 768], dot(V.h2[...], w2[:, FH + n:FH + n + 768])
        V.up[:, n:n + 768] = u_.astype(bf)
        V.act[:, n:n + 768] = (g_ * u_).astype(bf)
        if i == 2: save(up=1, act=1)
    def down(i):
        def rows(m, _):
            q = at_rows(768 * i + m * 256, 256, 256)
            v = tn(V.act[:, q], V.dffo[...]).astype(bf)
            S.ddn[0, q, :] = v[:, :512]
            S.ddn[1, q, :] = v[:, 512:]
            return 0
        lax.fori_loop(0, 3, rows, 0)
        to = at_rows(FH * c + 768 * i, 768, 256)
        w.send(S.ddn.at[1 - c, pl.ds(768 * i, 768)], O.ddown.at[to, :], other)
        w.local(S.ddn.at[c, pl.ds(768 * i, 768)], O.ddown.at[to, :])
    each = functools.partial
    chunks = [one, norm1, b_x, c_, conv, mix, mix2, norm2, two] + [each(gate, i) for i in range(3)] + [up_here] + [each(up, i) for i in range(3)] + [each(down, i) for i in range(3)]
    flows = list(vars(F).values())
    moves = (g.r1, g.r1, g.r2, g.r3, g.r4, g.r5)
    need = {0: z1, 1: z1, 2: z2, 3: z2b}
    for what, *where in ORDER_A:
        if not where: chunks[what](); continue
        f = flows[where[0]]
        if what == 0 and where[0] > 3 and 4 not in need: need[4] = need[5] = w.send(S.dnb, wd.at[drow, :], cross)
        if what == 1 and not need[where[0]].here: need[where[0]].wait_recv()
        if what < 2: g.r1(f, what == 0)
        else: moves[what](f, *where[1:])
    w.drain()

def call(kernel, outs, scratch, ident, limit, extra, first, *args):
    hbm = pl.BlockSpec(memory_space=pl.ANY)
    return pl.pallas_call(
        kernel, out_shape=tuple(jax.ShapeDtypeStruct(*v) for v in outs), in_specs=[first] + [hbm] * (len(args) - 1), out_specs=(hbm,) * len(outs),
        scratch_shapes=[pltpu.VMEM(*v) for v in scratch] + [pltpu.SemaphoreType.DMA((n,)) for n in (COPIES, COPIES, 96)] + extra,
        compiler_params=pltpu.CompilerParams(collective_id=ident, has_side_effects=True, vmem_limit_bytes=limit * 2**20))(*args)

def forward_all(*args):
    outs = call(forward_kernel, [*A_GOT.values(), *A_MADE.values()], [*A_MADE.values(), *A_SCR.values()], 1, 60, [], pl.BlockSpec(memory_space=pltpu.SMEM), *args)
    return dict(zip([*A_GOT, *A_MADE], outs))

def smalls(norm1_gain, norm2_gain, conv_weight):
    return jnp.pad(jnp.concatenate([norm1_gain[None], norm2_gain[None], conv_weight]), ((0, 11), (0, 112)))


RFLOWS = dict(
    f1a=Box(kind=1, base=0, step=128, gw=128, fw=128, to=PAIR, order=XY),
    f1b=Box(kind=1, base=256, step=128, gw=128, fw=128, to=CROSS, order=YX),
    f1s=Box(kind=0, base=0, step=0, gw=128, fw=0, to=None, order=YX),
    f2a=Box(kind=2, base=0, step=640, gw=1664, fw=640, to=PAIR, order=YX),
    f2b=Box(kind=2, base=2304, step=384, gw=1920, fw=384, to=CROSS, order=XY),
    f3a=Box(kind=3, base=0, step=0, gw=256, fw=0, to=None, order=XY),
    f3b=Box(kind=3, base=256, step=0, gw=256, fw=0, to=None, order=YX))
UNITS, WIDTH = (32, 128, 32, 144), (128, 512, 2 * FH, 512)
B_OUT = dict(mixed=((256, 1024), bf), dtok=((256, 1024), f32), din=((16, 3072), f32), dout=((16, 1024), f32),
    dg=((16, 4608), f32), du=((16, 4608), f32), dd=((72, 1024), f32), ds=((2, 16, 128), f32))
GRADS = [((4, 4, 2, u, n), bf) for u, n in zip(UNITS, WIDTH)]
def flow_scratch(t):
    u = UNITS[t.kind]
    return [((6, u, t.gw), bf), ((3, u, t.gw), bf), ((u, t.gw + t.fw), f32)]
B_SCR = dict(W=((2, FH, 512), bf), gate=((512, FH), bf), up=((512, FH), bf), dffo=((512, 1024), bf), h2=((512, 1024), bf),
    bcx=((512, 1536), bf), ext=((528, 512), f32), resid=((256, 1024), f32), small=((8, 1024), f32),
    tok=((256, 1024), bf), dhs=((256, 1024), f32), dhr=((256, 1024), f32), dho=((256, 1024), f32), dcv=((520, 512), f32),
    gsum=((8, 1024), f32), keep=((256, 1), f32))

def add_into(dst, srcs, rows, step=16):
    def body(i, _):
        r = pl.ds(pl.multiple_of(i * step, step), step)
        if len(srcs) == 1: dst[r, :] = dst[r, :] + srcs[0][r, :]
        else:
            v = dst[r, :].astype(f32)
            for q in srcs: v = v + q[r, :].astype(f32)
            dst[r, :] = v.astype(bf)
        return 0
    lax.fori_loop(0, rows // step, body, 0)

class Scatter:
    def __init__(self, w, go, pair, cross, far, x, y, z, c, other, grads, lands, bufs):
        self.w, self.go, self.x, self.y, self.z, self.c, self.other = w, go, x, y, z, c, other
        self.hi, self.zl = z // 2, z % 2
        self.f = Box()
        for i, (n, t) in enumerate(RFLOWS.items()):
            sel = {PAIR: (self.zl + self.hi) % 2, CROSS: self.hi, None: 0}[t.to]
            k = t.kind
            f = Box(vars(t), G=grads[k], L=lands[k], u=UNITS[k], sel=sel, col=t.base + t.step * sel, out=[],
                ecol=t.base + t.gw * sel, pcol=t.base + t.gw * (1 - sel), dev={PAIR: pair, CROSS: cross, None: None}[t.to],
                A={}, s={}, t={}, s2={}, t2={})
            f.M, f.E, f.F = bufs[3 * i:3 * i + 3]
            vars(self.f)[n] = f
        self.pair, self.cross, self.far = pair, cross, far
    def cols(self, c, n): return pl.ds(c if isinstance(c, int) else pl.multiple_of(c, 128), n)
    def at(self, f, da, db):
        a, b = f.order
        pos = {X: self.x, Y: self.y}
        pos[a] = (pos[a] + da + 4) % 4
        pos[b] = (pos[b] + db + 4) % 4
        return pos[Y], pos[X]
    def part(self, ref, f, p, u=None):
        if u is None: return ref.at[p[0], p[1], :, :, self.cols(f.col, f.gw)]
        return ref.at[p[0], p[1], u, :, self.cols(f.col, f.gw)]
    def zline(self, ref, f, j, col):
        l = self.at(f, j, 0)
        cs = self.cols(col, f.fw)
        return ref.at[l[0], :, :, :, cs] if f.order[0] == Y else ref.at[:, l[1], :, :, cs]
    def zsend(self, f, j):
        f.A[j] = self.w.send(self.zline(f.G, f, j, f.pcol), self.zline(f.L, f, j, f.ecol), f.dev)
    def first(self, f, j):
        b = f.order[1]
        if f.to:
            f.A[j].wait_recv()
            g, l = self.zline(f.G, f, j, f.ecol), self.zline(f.L, f, j, f.pcol)
            for i in range(4):
                for u in (0, 1): add_into(g.at[i, u], [l.at[i, u]], f.u)
        p = self.at(f, j, 2)
        f.s[j] = self.w.send(self.part(f.G, f, p, 0), self.part(f.L, f, p, 0), self.go[(b, 1)])
        f.t[j] = self.w.send(self.part(f.G, f, p, 1), self.part(f.L, f, p, 1), self.go[(b, -1)])
    def second(self, f, j):
        b, u = f.order[1], f.u
        f.s[j].wait_recv(); p = self.at(f, j, 1)
        add_into(self.part(f.G, f, p, 0), [self.part(f.L, f, p, 0)], u)
        f.s2[j] = self.w.send(self.part(f.G, f, p), self.part(f.L, f, p), self.go[(b, 1)])
        f.t[j].wait_recv(); p = self.at(f, j, -1)
        add_into(self.part(f.G, f, p, 1), [self.part(f.L, f, p, 1)], u)
        f.t2[j] = self.w.send(self.part(f.G, f, p), self.part(f.L, f, self.at(f, j, 1)), self.go[(b, -1)])
    def third(self, f, j):
        a, u, M = f.order[0], f.u, f.M
        f.s2[j].wait_recv(); f.t2[j].wait_recv()
        p = self.at(f, j, 0); o = self.at(f, j, 2)
        for v in (0, 1): add_into(self.part(f.G, f, p, v), [self.part(f.L, f, p, v), self.part(f.L, f, o, v)], u)
        if j == 2:
            f.c = self.w.send(self.part(f.G, f, p, 0), M.at[0], self.go[(a, 1)])
            f.d = self.w.send(self.part(f.G, f, p, 1), M.at[1], self.go[(a, -1)])
        elif j == 1:
            f.c.wait_recv(); add_into(self.part(f.G, f, p, 0), [M.at[0]], u)
            f.c2 = self.w.send(self.part(f.G, f, p), M.at[pl.ds(2, 2)], self.go[(a, 1)])
        elif j == -1:
            f.d.wait_recv(); add_into(self.part(f.G, f, p, 1), [M.at[1]], u)
            f.d2 = self.w.send(self.part(f.G, f, p), M.at[pl.ds(4, 2)], self.go[(a, -1)])
    def last1(self, f):
        u, M, me = f.u, f.M, (self.y, self.x)
        f.c2.wait_recv(); f.d2.wait_recv()
        for v in (0, 1): add_into(self.part(f.G, f, me, v), [M.at[2 + v], M.at[4 + v]], u)
        away = self.part(f.G, f, me, 1 - self.hi)
        f.e = [self.w.send(self.part(f.G, f, me, self.hi), f.E.at[0], self.pair), self.w.send(away, f.E.at[1], self.cross), self.w.send(away, f.E.at[2], self.far)]
    def last2(self, f, targets):
        E, F, gw, fw, sel = f.E, f.F, f.gw, f.fw, f.sel
        for q in f.e: q.wait_recv()
        G = f.G.at[self.y, self.x, self.hi]
        same, two = (1, (0, 2)) if f.to == PAIR else (0, (1, 2))
        def mine(o, n): return G[:, self.cols(o + f.col, n)].astype(f32) + E[same, :, self.cols(o, n)].astype(f32)
        def theirs(o, n): return E[two[0], :, self.cols(o, n)].astype(f32) + E[two[1], :, self.cols(o, n)].astype(f32)
        ov = gw - fw
        if fw:
            F[:, self.cols(gw * sel, fw)] = mine(ov * sel, fw)
            F[:, self.cols(gw * (1 - sel), fw)] = theirs(ov * (1 - sel), fw)
        if ov: F[:, pl.ds(fw, ov)] = mine(fw * (1 - sel), ov) + theirs(fw * sel, ov)
        rows = f.u if f.kind == 3 else 32
        half = rows // 2
        m = 8
        for prow, pcol, pw, out, ocol in targets:
            src = lambda q: F.at[pl.ds(pl.multiple_of(prow + half * q, m), half), pl.ds(pcol, pw)]
            dst = out if ocol is None else out.at[:, self.cols(ocol, pw)]
            f.out.append(self.w.send(src(1 - self.c), dst, self.other))
            f.out.append(self.w.local(src(self.c), dst))
    def wait_out(self, f):
        for i, q in enumerate(f.out):
            if i % 2: q.wait()
            else: q.wait_recv()

def backward_kernel(*refs):
    (I, O, r), refs = named([dict(A_GOT, **A_MADE, tokens=0), B_OUT, B_SCR], refs)
    grads, lands, bufs, (ss, rs, ls, free) = refs[:4], refs[4:8], refs[8:-4], refs[-4:]
    x, y, z, c = spot()
    hi = z // 2
    k = (y * 4 + x) * 2 + hi
    pair = device(x, y, z + 1 - 2 * (z % 2), c)
    cross = device(x, y, 3 - z, c)
    far = device(x, y, (z + 2) % 4, c)
    other = device(x, y, z, 1 - c)
    nxt, prv = along(x, y, z, c, 1), along(x, y, z, c, -1)
    go = {(a, st): moved(x, y, z, c, a, st) for a in XY for st in (1, -1)}
    count = greet(list(go.values()) + [pair, cross, far, other, nxt, prv])
    w = Wire(ss, rs, ls)
    own, oth = at_rows(256 * c, 256, 256), at_rows(256 * (1 - c), 256, 256)
    col = lambda p, n: pl.ds(pl.multiple_of(p, 128), n)
    W = r.W
    slot = lambda i: W.at[i // 2, pl.ds(1024 * (i % 2), 1024)]
    def w_down():
        return [w.local(I.wd.at[at_rows(FH * c, FH, FH), :], W.at[c]), w.local(I.wdr.at[at_rows(FH * c, FH, FH), :], W.at[1 - c])]
    lgd = w.local(I.ddown, grads[3])
    lwd = w_down()
    ld = Box({n: w.local(vars(I)[n], vars(r)[n]) for n in dict(dffo=0, gate=0, up=0, h2=0, small=0, resid=0, ext=0, bcx=0, keep=0)})
    ld.tok = w.local(I.tokens, r.tok)
    met(count)
    sc = Scatter(w, go, pair, cross, far, x, y, z, c, other, grads, lands, bufs)
    F = sc.f
    lgd.wait()
    r.gsum[...] = jnp.zeros((8, 1024), f32)
    gain = lambda i: r.small[i:i + 1, :]
    t = Box(got={})
    def d_act(n):
        if n == 0:
            for q in lwd + [ld.dffo, ld.gate, ld.up]: q.wait()
        d = nt(r.dffo[:, :512], W[0, n:n + 768, :]) + nt(r.dffo[:, 512:], W[1, n:n + 768, :])
        g, u = r.gate[:, n:n + 768].astype(f32), r.up[:, n:n + 768].astype(f32)
        sg = jax.nn.sigmoid(g)
        r.gate[:, n:n + 768] = (d * u * sg * (1.0 + g * (1.0 - sg))).astype(bf)
        r.up[:, n:n + 768] = (d * (g * sg)).astype(bf)
    panels = [[(r.gate, 512 * p, 512, 512 * p)] for p in range(4)] + [[(r.up, FH + 512 * p, 512, 512 * p)] for p in range(4)]
    panels += [[(r.gate, 2048, 256, 2048), (r.up, FH + 2048, 256, 2048)]]
    def fetch(i):
        out, o = [], 0
        for _, cc, n, _ in panels[i % 9]:
            out.append(w.local(I.w2.at[:, pl.ds(cc, n)], slot(i % 4).at[:, pl.ds(o, n)])); o += n
        return out
    def slab(src, yy, base):
        def part(m, _):
            d = tn(r.h2[:, col(256 * yy, 256)], src[:, col(768 * m, 768)]).astype(bf)
            for xx in range(4):
                for u in (0, 1): grads[2][yy, xx, u, :, col(base + 768 * m, 768)] = d[64 * xx + 32 * u:64 * xx + 32 * u + 32]
            return 0
        lax.fori_loop(0, 3, part, 0)
    def d_gate(i):
        if i == 0:
            t.got.update({p: fetch(p) for p in range(4)})
            ld.h2.wait()
        slab(r.gate, (y + JS[i] + 4) % 4, 0)
        sc.zsend(F.f2a, JS[i])
    def d_up(i):
        slab(r.up, (y + JS[i] + 4) % 4, FH)
        if i == 3:
            for j in JS: sc.zsend(F.f2b, j)
    def panel(i):
        for q in t.got[i]: q.wait()
        rr, acc = ((oth, r.dhs), (own, r.dho))[i // 9]
        def part(m, _):
            o, d, q = 0, 0, col(512 * m, 512)
            for nm, _, n, off in panels[i % 9]:
                d = d + nt(nm[rr, off:off + n], slot(i % 4)[q, o:o + n])
                o += n
            acc[:, q] = d if i % 9 == 0 else acc[:, q] + d
            return 0
        lax.fori_loop(0, 2, part, 0)
        if i + 4 < 18: t.got[i + 4] = fetch(i + 4)
        if i == 8: t.dh = w.send(r.dhs, r.dhr, other)
        if i == 17:
            r.h, r.y, r.conv = (r.gate.at[:, pl.ds(a, m)] for a, m in ((0, 1024), (1024, 512), (1536, 512)))
            ld.h, ld.y, ld.conv = w.local(I.h, r.h), w.local(I.y, r.y), w.local(I.conv, r.conv)
            t.win = [w.local(I.w1.at[:, pl.ds(512 * p, 512)], slot(p + 1)) for p in range(3)]
            t.wo = [w.local(I.w1.at[at_rows(512 * c, 512, 512), pl.ds(1536, 512)], slot(0).at[at_rows(512 * c, 512, 512)]),
                w.local(I.wor, slot(0).at[at_rows(512 * (1 - c), 512, 512)])]
            ld.small.wait(); ld.resid.wait()
    def back2():
        t.dh.wait_recv()
        def rows(i, _):
            q = at_rows(i * 64, 64, 64); qo = at_rows(256 * c + i * 64, 64, 64)
            v = r.resid[q, :]
            s2 = lax.rsqrt(jnp.mean(v * v, axis=1, keepdims=True) + EPS)
            d = r.dho[q, :] + r.dhr[q, :]
            r.gsum[1:2, :] += jnp.sum(d * v * s2, axis=0, keepdims=True)
            wt = d * gain(1)
            inner = jnp.mean(wt * v, axis=1, keepdims=True)
            dr = r.dffo[qo, :].astype(f32) + (s2 * wt - v * (s2 * s2 * s2) * inner)
            r.resid[q, :] = dr
            r.h2[qo, :] = dr.astype(bf)
            return 0
        lax.fori_loop(0, 4, rows, 0)
        t.dm = w.send(r.h2.at[own], r.h2.at[own], other)
        for q in (ld.y, ld.ext, ld.conv, ld.bcx, ld.h, ld.tok, ld.keep): q.wait()
        for q in t.wo: q.wait()
    def d_y():
        t.dm.wait_recv()
        d = nt(r.h2[:, :512], slot(0)[0:512, :]) + nt(r.h2[:, 512:], slot(0)[512:1024, :])
        r.dcv[0:512, :] = d * r.bcx[:, 512:1024].astype(f32)
        r.bcx[:, 512:1024] = (d * r.conv[...].astype(f32)).astype(bf)
        t.halo = w.send(r.dcv.at[pl.ds(0, 8)], r.dcv.at[pl.ds(512, 8)], prv)
    def d_out():
        def rows(i, _):
            d = tn(r.y[:, at_rows(256 * i, 256, 256)], r.h2[...]).astype(bf)
            for xx in range(4):
                for u in (0, 1):
                    v = d[64 * xx + 32 * u:64 * xx + 32 * u + 32]
                    r.up[at_rows(256 * i + 64 * xx + 32 * u, 32, 32), 0:512] = jnp.where(c == 0, v[:, 512:], v[:, :512])
                    grads[1][2 * c + i, xx, u, 96:128, :] = jnp.where(c == 0, v[:, :512], v[:, 512:])
            return 0
        lax.fori_loop(0, 2, rows, 0)
        t.do = [w.send(r.up.at[pl.ds(256 * i + 64 * xx + 32 * u, 32), pl.ds(0, 512)], grads[1].at[2 * c + i, xx, u, pl.ds(96, 32), :], other)
            for i in (0, 1) for xx in range(4) for u in (0, 1)]
    def d_taps():
        for q in range(0, 512, 128):
            dv = r.dcv[q:q + 128, :]
            for i in range(3):
                r.gsum[2 + i:3 + i, col(512 * c, 512)] += jnp.sum(dv * r.ext[14 + i + q:142 + i + q, :], axis=0, keepdims=True)
    def d_bx():
        t.halo.wait_recv()
        tap = [r.small[2 + i:3 + i, col(512 * c, 512)] for i in range(3)]
        r.dcv[512:520, :] = r.dcv[512:520, :] * (k < 31).astype(f32)
        for q in range(0, 512, 128):
            dx = tap[2] * r.dcv[q:q + 128, :] + tap[1] * r.dcv[q + 1:q + 129, :] + tap[0] * r.dcv[q + 2:q + 130, :]
            bp, xp = r.bcx[q:q + 128, 0:512].astype(f32), r.bcx[q:q + 128, 1024:1536].astype(f32)
            r.bcx[q:q + 128, 0:512] = (dx * xp).astype(bf)
            r.bcx[q:q + 128, 1024:1536] = (dx * bp).astype(bf)
    def d_in(i):
        if i == 0:
            for q in t.do: q.wait_recv()
        yy = (y + JS[i] + 4) % 4
        def part(p, _):
            d = tn(r.h[:, col(256 * yy, 256)], r.bcx[:, col(512 * p, 512)]).astype(bf)
            for xx in range(4):
                for u in (0, 1): grads[1][yy, xx, u, at_rows(32 * p, 32, 32), :] = d[64 * xx + 32 * u:64 * xx + 32 * u + 32]
            return 0
        lax.fori_loop(0, 3, part, 0)
        sc.zsend(F.f1b, JS[i])
        if i == 3:
            for j in JS: sc.zsend(F.f1a, j)
    def d_h():
        t.dh.wait_send()
        for q in t.win: q.wait()
        for rr, acc in ((oth, r.dhs), (own, r.dho)):
            acc[...] = sum(nt(r.bcx[rr, 512 * i:512 * i + 512], slot(i + 1)[...]) for i in range(3))
        t.dh = w.send(r.dhs, r.dhr, other)
        t.act = w_down() + [w.local(I.act, r.gate)]
    def back1():
        t.dh.wait_recv()
        def rows(i, _):
            q = at_rows(i * 64, 64, 64)
            v = r.tok[q, :].astype(f32)
            s1 = lax.rsqrt(jnp.mean(v * v, axis=1, keepdims=True) + EPS)
            d = r.dho[q, :] + r.dhr[q, :]
            r.gsum[0:1, :] += jnp.sum(d * v * s1, axis=0, keepdims=True)
            wt = d * gain(0)
            inner = jnp.mean(wt * v, axis=1, keepdims=True)
            r.dho[q, :] = r.resid[q, :] + (s1 * wt - v * (s1 * s1 * s1) * inner)
            return 0
        lax.fori_loop(0, 4, rows, 0)
        pl.semaphore_signal(free, inc=1, device_id=other, device_id_type=MESH)
        t.tok = w.local(r.dho, O.dtok)
        eye = (lax.broadcasted_iota(jnp.int32, (8, 128), 0) == lax.broadcasted_iota(jnp.int32, (8, 128), 1)).astype(f32).astype(bf)
        sm = tn(r.gsum[...].astype(bf), eye).astype(bf)
        for yy in range(4):
            for xx in range(4):
                for u in (0, 1):
                    o = 256 * yy + 64 * xx + 32 * u
                    grads[0][yy, xx, u] = sm[o:o + 32]
        t.dh.wait_send()
    def ffo():
        for q in t.act: q.wait()
        t.tok.wait()
        t.resid = w.local(I.resid, r.resid)
        for rr, acc in ((oth, r.dhs), (own, r.dho)):
            def part(i, _):
                acc[:, col(512 * i, 512)] = dot(r.gate[rr, :], W[i])
                return 0
            lax.fori_loop(0, 2, part, 0)
        pl.semaphore_wait(free, 1)
        t.dh = w.send(r.dhs, r.dhr, other)
    def mixed():
        t.dh.wait_recv(); t.resid.wait()
        r.tok[...] = (r.keep[...] * (r.resid[...] + (r.dho[...] + r.dhr[...]))).astype(bf)
        w.local(r.tok, O.mixed)
    each = functools.partial
    chunks = [each(d_act, n) for n in (0, 768, 1536)] + [each(d_gate, i) for i in range(4)] + [each(d_up, i) for i in range(4)]
    chunks += [each(panel, i) for i in range(18)] + [back2, d_y, d_out, d_taps, d_bx] + [each(d_in, i) for i in range(4)] + [d_h, back1, ffo, mixed]
    half = 512 * c
    at_in = lambda o: [(32 * p, 0, 256, O.din, 1024 * p + half + o) for p in range(3)] + [(96, 0, 256, O.dout, half + o)]
    ends = [at_in(0), at_in(256), [(0, 0, 128, O.ds.at[c], None)], [(0, 0, FH, O.dg, FH * c)], [(0, 0, FH, O.du, FH * c)],
        [(0, 0, 256, O.dd, half)], [(0, 0, 256, O.dd, half + 256)]]
    flows = list(vars(F).values())
    moves = (sc.first, sc.second, sc.third, sc.last1)
    for what, *where in ORDER_B:
        if not where: chunks[what]()
        elif what < 3: moves[what](flows[where[0]], where[1])
        elif what < 4: moves[what](flows[where[0]])
        else: sc.last2(flows[where[0]], ends[where[0]])
    w.drain()

def backward_all(a, tokens):
    a = Box(a)
    a.ddown = a.ddown.reshape(4, 4, 2, 144, 512)
    scr = [*B_SCR.values()] + GRADS + GRADS + [v for t in RFLOWS.values() for v in flow_scratch(t)]
    outs = call(backward_kernel, [*B_OUT.values()], scr, 2, 63, [pltpu.SemaphoreType.REGULAR], pl.BlockSpec(memory_space=pl.ANY), *vars(a).values(), tokens)
    return Box(dict(zip(B_OUT, outs)))

def finish_kernel(n, *refs):
    src, part, dst, (dn1, dn2, dtap), held, sems, (square,) = refs[:n], refs[n], refs[n + 1:2 * n + 1], refs[2 * n + 1:2 * n + 4], refs[2 * n + 4:3 * n + 4], refs[3 * n + 4:4 * n + 4], refs[4 * n + 4:]
    ins = [pltpu.make_async_copy(a, v, s) for a, v, s in zip(src, held, sems)]
    for cp in ins: cp.start()
    square[...] = jnp.zeros((128, 128), f32)
    square[0:16, :] = part[0] + part[1]
    rows = jnp.transpose(square[...])
    dn1[...] = rows[0:1, 0:16]
    dn2[...] = rows[1:2, 0:16]
    dtap[...] = rows[2:5, 0:16]
    outs = [pltpu.make_async_copy(v, d, s) for v, d, s in zip(held, dst, sems)]
    for a, d in zip(ins, outs): a.wait(); d.start()
    for d in outs: d.wait()

def finish_all(part, *args):
    hbm, vm = pl.BlockSpec(memory_space=pl.ANY), pl.BlockSpec(memory_space=pltpu.VMEM)
    n = len(args)
    out = [jax.ShapeDtypeStruct(v.shape, v.dtype) for v in args] + [jax.ShapeDtypeStruct((m, 16), f32) for m in (1, 1, 3)]
    return pl.pallas_call(
        functools.partial(finish_kernel, n), out_shape=tuple(out), in_specs=[hbm] * n + [vm], out_specs=(hbm,) * n + (vm,) * 3,
        scratch_shapes=[pltpu.VMEM(v.shape, v.dtype) for v in args] + [pltpu.SemaphoreType.DMA] * n + [pltpu.VMEM((128, 128), f32)],
        compiler_params=pltpu.CompilerParams(vmem_limit_bytes=62 * 2**20))(*args, part)


def body(tokens, lengths, norm1_gain, in_proj, conv_weight, out_proj, norm2_gain, w_gate, w_up, w_down, cotangent):
    a = forward_all(lengths, tokens, cotangent, in_proj, out_proj, smalls(norm1_gain, norm2_gain, conv_weight), w_gate, w_up, w_down)
    b = backward_all(a, tokens)
    mixed, dtok, din, dout, dg, du, dd, dn1, dn2, dtap = finish_all(b.ds, b.mixed, b.dtok, b.din, b.dout, b.dg, b.du, b.dd)
    return mixed, dtok, dn1[0], din, dtap, dout, dn2[0], dg, du, dd

def solution(mesh):
    tok = P(("rep", "shard"), None)
    par = (P("shard"), P("shard", None), P(None, "shard"), P("shard", None), P("shard"), P("shard", None), P("shard", None), P("shard", None))
    return jax.shard_map(body, mesh=mesh, in_specs=(tok, P()) + par + (tok,), out_specs=(tok, tok) + par, check_vma=False)
```
